32 devices in a mesh: win: 16 (over z, y, x), tp: 2 (over core).
Axes of the slice: x: 2, y: 2, z: 4, core: 2. Of those that a mesh axis runs over, the one named last changes fastest.
Arguments:
- pixels: bfloat16 [128, 20, 20, 512], P(('win', 'tp')), may hold values from -6 to 6
- merge_gain: float32 [2048], P('tp'), may hold values from 0.1 to 1.9
- merge_shift: float32 [2048], P('tp'), may hold values from -3 to 3
- merge_weight: bfloat16 [2048, 1024], P('tp'), may hold values from -0.125 to 0.125
- norm1_gain: float32 [1024], P('tp'), may hold values from 0.1 to 1.9
- norm1_shift: float32 [1024], P('tp'), may hold values from -3 to 3
- qkv_weight: bfloat16 [1024, 3, 1024], P(None, None, 'tp'), may hold values from -0.1875 to 0.1875
- qkv_bias: float32 [2, 1024], P(None, 'tp'), may hold values from -3 to 3
- rel_table: float32 [361, 32], P(None, 'tp'), may hold values from -6 to 6
- proj_weight: bfloat16 [1024, 1024], P('tp'), may hold values from -0.5 to 0.5
- proj_bias: float32 [1024], P('tp'), may hold values from -3 to 3
- norm2_gain: float32 [1024], P('tp'), may hold values from 0.1 to 1.9
- norm2_shift: float32 [1024], P('tp'), may hold values from -3 to 3
- fc1_weight: bfloat16 [1024, 4096], P(None, 'tp'), may hold values from -0.1875 to 0.1875
- fc1_bias: float32 [4096], P('tp'), may hold values from -3 to 3
- fc2_weight: bfloat16 [4096, 1024], P('tp'), may hold values from -0.125 to 0.125
- fc2_bias: float32 [1024], P('tp'), may hold values from -3 to 3
- rel_index: int32 [100, 100], replicated, may hold values from 0 to 360
- keep: int32 [12800], P('win'), may hold values 0 or 1
- cotangent: bfloat16 [12800, 1024], P('win', 'tp'), may hold values from -6 to 6
Outputs:
- out: bfloat16 [12800, 1024], P('win', 'tp')
- pixels_grad: float32 [128, 20, 20, 512], P(('win', 'tp'))
- merge_gain_grad: float32 [2048], P('tp')
- merge_shift_grad: float32 [2048], P('tp')
- merge_weight_grad: float32 [2048, 1024], P('tp', 'win')
- norm1_gain_grad: float32 [1024], P('tp')
- norm1_shift_grad: float32 [1024], P('tp')
- qkv_weight_grad: float32 [1024, 3, 1024], P('win', None, 'tp')
- qkv_bias_grad: float32 [2, 1024], P(None, 'tp')
- rel_table_grad: float32 [361, 32], P(None, 'tp')
- proj_weight_grad: float32 [1024, 1024], P('tp', 'win')
- proj_bias_grad: float32 [1024], P('tp')
- norm2_gain_grad: float32 [1024], P('tp')
- norm2_shift_grad: float32 [1024], P('tp')
- fc1_weight_grad: float32 [1024, 4096], P('win', 'tp')
- fc1_bias_grad: float32 [4096], P('tp')
- fc2_weight_grad: float32 [4096, 1024], P('tp', 'win')
- fc2_bias_grad: float32 [1024], P('tp')
The draws below stay inside these ranges and needn't reach their ends.
All inputs are finite; a program needn't handle non-finite values. No bound on the sum of `keep` on one device may be relied on, other than what follows from the above.
Results may differ from the reference program's by a relative error of at most 0.015.
Values may be sent and summed in bfloat16 or wider, within the bound.
A program may use at most 192 MiB of HBM per device.

```python
import jax
import jax.numpy as jnp
from jax import lax

D = 1024
FF = 4096
HEADS = 32
HEAD_DIM = 32
C_IN = 512
SIDE = 10
W_DEV = 8
WINDOWS = 128
TOKENS = 12800
REL = 361


def set_ends(drawn, stream_key, least, largest):
    shape = drawn.shape
    spot = [jax.random.randint(jax.random.fold_in(stream_key, axis), (), 0, shape[axis]) for axis in range(len(shape))]
    drawn = drawn.at[tuple(spot)].set(least)
    longest = shape.index(max(shape))
    spot[longest] = (spot[longest] + 1) % shape[longest]
    return drawn.at[tuple(spot)].set(largest)


def level_of(rng, shape, cuts, low, largest):
    def one(dim, parts):
        draws = jax.random.uniform(jax.random.fold_in(jax.random.fold_in(rng, 6), dim), (parts,), jnp.float32, low / len(cuts), largest / len(cuts))
        return jnp.repeat(jnp.exp(draws), shape[dim] // parts).reshape((-1,) + (1,) * (len(shape) - dim - 1))

    level = one(*cuts[0])
    for cut in cuts[1:]:
        level = level * one(*cut)
    return level


def gaussian(stream_key, extent, scale, most, cuts=(), held_as=jnp.bfloat16):
    values = scale * jax.random.normal(stream_key, extent, jnp.float32)
    if cuts:
        values = values * level_of(stream_key, extent, cuts, -0.22, 0.18)
    return jnp.clip(values, -most, most).astype(held_as)


def setup_inputs(seed: int = 0) -> dict:
    streams_of = jax.random.split(jax.random.key(seed), 21)
    return {
        "pixels": gaussian(streams_of[0], (WINDOWS, 2 * SIDE, 2 * SIDE, C_IN), 1.0, 6.0, ((0, 32),)),
        "merge_gain": jnp.clip(1.0 + 0.18 * jax.random.normal(streams_of[1], (4 * C_IN,), jnp.float32), 0.1, 1.9),
        "merge_shift": gaussian(streams_of[2], (4 * C_IN,), 0.5, 3.0, ((0, 2),), jnp.float32),
        "merge_weight": gaussian(streams_of[3], (4 * C_IN, D), (4 * C_IN) ** -0.5, 0.125, ((0, 2),)),
        "norm1_gain": jnp.clip(1.0 + 0.18 * jax.random.normal(streams_of[4], (D,), jnp.float32), 0.1, 1.9),
        "norm1_shift": gaussian(streams_of[5], (D,), 0.5, 3.0, ((0, 2),), jnp.float32),
        "qkv_weight": gaussian(streams_of[6], (D, 3, D), D ** -0.5, 0.1875, ((2, 2),)),
        "qkv_bias": gaussian(streams_of[7], (2, D), 0.5, 3.0, ((1, 2),), jnp.float32),
        "rel_table": gaussian(streams_of[8], (REL, HEADS), 1.0, 6.0, ((1, 2),), jnp.float32),
        "proj_weight": gaussian(streams_of[9], (D, D), (D // 8) ** -0.5, 0.5, ((0, 2),)),
        "proj_bias": gaussian(streams_of[10], (D,), 0.5, 3.0, ((0, 2),), jnp.float32),
        "norm2_gain": jnp.clip(1.0 + 0.18 * jax.random.normal(streams_of[11], (D,), jnp.float32), 0.1, 1.9),
        "norm2_shift": gaussian(streams_of[12], (D,), 0.5, 3.0, ((0, 2),), jnp.float32),
        "fc1_weight": gaussian(streams_of[13], (D, FF), D ** -0.5, 0.1875, ((1, 2),)),
        "fc1_bias": gaussian(streams_of[14], (FF,), 0.5, 3.0, ((0, 2),), jnp.float32),
        "fc2_weight": gaussian(streams_of[15], (FF, D), (FF // 2) ** -0.5, 0.125, ((0, 2),)),
        "fc2_bias": gaussian(streams_of[16], (D,), 0.5, 3.0, ((0, 2),), jnp.float32),
        "rel_index": set_ends(jax.random.randint(streams_of[17], (SIDE * SIDE, SIDE * SIDE), 0, REL), jax.random.fold_in(streams_of[17], 1), 0, REL - 1).astype(jnp.int32),
        "keep": set_ends((jax.random.randint(streams_of[18], (TOKENS,), 0, 4) < 3).astype(jnp.int32), jax.random.fold_in(streams_of[18], 1), 0, 1),
        "cotangent": gaussian(streams_of[19], (TOKENS, D), 1.0, 6.0, ((0, 16), (1, 2))),
    }


EPS = 1e-05
HIGH = lax.Precision.HIGHEST

@jax.custom_vjp
def low(v):
    return lax.optimization_barrier(v.astype(jnp.bfloat16)).astype(jnp.float32)

@jax.custom_vjp
def low_back(v):
    return v

def low_keep(v):
    return (low(v), None)

def low_pass(kept, grad):
    return (grad,)

def back_keep(v):
    return (v, None)

def back_low(kept, grad):
    return (low(grad),)
low.defvjp(low_keep, low_pass)
low_back.defvjp(back_keep, back_low)

def matmul(left, right):
    return jnp.dot(left, right, precision=HIGH)

def norm_rows(values, gain, shift):
    mean = lax.optimization_barrier(jnp.mean(values, axis=-1, keepdims=True))
    second = lax.optimization_barrier(jnp.mean(values * values, axis=-1, keepdims=True))
    scale = lax.rsqrt(second - mean * mean + EPS)
    return (values - mean) * scale * gain + shift

def layer(pixels, merge_gain, merge_shift, merge_weight, norm1_gain, norm1_shift, qkv_weight, qkv_bias, rel_table, proj_weight, proj_bias, norm2_gain, norm2_shift, fc1_weight, fc1_bias, fc2_weight, fc2_bias, rel_index, keep_rows):
    count = pixels.shape[0]
    area = SIDE * SIDE
    merged = pixels.reshape(count, SIDE, 2, SIDE, 2, C_IN).transpose(0, 1, 3, 4, 2, 5).reshape(count * area, 4 * C_IN)
    merge_low = low(norm_rows(merged, merge_gain, merge_shift))
    stream0 = low_back(matmul(merge_low, merge_weight))
    first = low(norm_rows(stream0, norm1_gain, norm1_shift))
    zero_bias = jnp.zeros_like(qkv_bias[0])
    qkv = matmul(first, qkv_weight.reshape(D, 3 * D)).reshape(count * area, 3, D)
    qkv = qkv + jnp.stack([qkv_bias[0], zero_bias, qkv_bias[1]])[None]
    qkv = low(low_back(qkv))
    shaped = qkv.reshape(count, area, 3, HEADS, HEAD_DIM)
    bias = rel_table[rel_index].transpose(2, 0, 1)
    scores = jnp.einsum('wqhd,wkhd->whqk', shaped[:, :, 0], shaped[:, :, 1], precision=HIGH) * HEAD_DIM ** (-0.5) + bias[None]
    probs = jax.nn.softmax(low_back(scores), axis=-1)
    attended = jnp.einsum('whqk,wkhd->wqhd', low(probs), shaped[:, :, 2], precision=HIGH).reshape(count * area, D)
    attended = low(low_back(attended))
    attention = low_back(matmul(attended, proj_weight) + proj_bias)
    stream1 = stream0 + attention
    second = low(norm_rows(stream1, norm2_gain, norm2_shift))
    hidden = low_back(matmul(second, fc1_weight) + fc1_bias)
    activated = low(jax.nn.gelu(hidden, approximate=False))
    feed = low_back(matmul(activated, fc2_weight) + fc2_bias)
    return keep_rows[:, None] * (stream1 + feed)

def reference(pixels, merge_gain, merge_shift, merge_weight, norm1_gain, norm1_shift, qkv_weight, qkv_bias, rel_table, proj_weight, proj_bias, norm2_gain, norm2_shift, fc1_weight, fc1_bias, fc2_weight, fc2_bias, rel_index, keep, cotangent):
    weights = (merge_gain, merge_shift, merge_weight, norm1_gain, norm1_shift, qkv_weight, qkv_bias, rel_table, proj_weight, proj_bias, norm2_gain, norm2_shift, fc1_weight, fc1_bias, fc2_weight, fc2_bias)
    floats = tuple((weight.astype(jnp.float32) for weight in weights))
    groups = pixels.shape[0] // W_DEV
    rows = W_DEV * SIDE * SIDE
    pixel_groups = pixels.reshape(groups, W_DEV, 2 * SIDE, 2 * SIDE, C_IN)
    keep_groups = keep.astype(jnp.float32).reshape(groups, rows)
    cot_groups = cotangent.reshape(groups, rows, D)

    def step(totals, inputs):
        pix, keep_rows, cot = inputs

        def run(pix_float, *params):
            return layer(pix_float, *params, rel_index, keep_rows)
        result, pull = jax.vjp(run, pix.astype(jnp.float32), *floats)
        grads = pull(cot.astype(jnp.float32))
        totals = tuple((total + grad for total, grad in zip(totals, grads[1:])))
        return (totals, (result.astype(jnp.bfloat16), grads[0]))
    zeros = tuple((jnp.zeros(weight.shape, jnp.float32) for weight in floats))
    totals, (outs, pixel_grads) = lax.scan(step, zeros, (pixel_groups, keep_groups, cot_groups))
    out = outs.reshape(groups * rows, D)
    pixels_grad = pixel_grads.reshape(pixels.shape)
    return (out, pixels_grad, totals[0], totals[1], totals[2], totals[3], totals[4], totals[5], totals[6], totals[7], totals[8], totals[9], totals[10], totals[11], totals[12], totals[13], totals[14], totals[15])
```

```python
import jax
import jax.numpy as jnp
from jax import lax
from jax.experimental import pallas as pl
from jax.experimental.pallas import tpu as pltpu
from jax.sharding import PartitionSpec as P

EPS = 1e-05
F32 = jnp.float32
BF16 = jnp.bfloat16
VMEM = pl.BlockSpec(memory_space=pltpu.VMEM)
SMEM = pl.BlockSpec(memory_space=pltpu.SMEM)
PAD = 112
LIMIT = 56 * 1024 * 1024


def call(body, out, ins, scratch=(), flops=0, nbytes=0, **more):
    return pl.pallas_call(
        body,
        out_shape=out,
        scratch_shapes=list(scratch),
        compiler_params=pltpu.CompilerParams(vmem_limit_bytes=LIMIT),
        cost_estimate=pl.CostEstimate(
            flops=int(flops), bytes_accessed=int(nbytes), transcendentals=0
        ),
        **more,
    )(*ins)


def whole(body, out, ins, scratch=(), flops=0, nbytes=0, smem_first=False):
    specs = [VMEM] * len(ins)
    if smem_first:
        specs[0] = SMEM
    outs = jax.tree.map(lambda _: VMEM, out)
    return call(body, out, ins, scratch, flops, nbytes, in_specs=specs, out_specs=outs)


def shape(dims, dtype=F32):
    return jax.ShapeDtypeStruct(tuple(dims), dtype)


def dot(a, b):
    return jnp.dot(a, b, preferred_element_type=F32)


def dot_nt(a, b):
    return lax.dot_general(a, b, (((1,), (1,)), ((), ())), preferred_element_type=F32)


def stats(x, width):
    mean = jnp.sum(x, 1, keepdims=True) * (1.0 / width)
    second = jnp.sum(x * x, 1, keepdims=True) * (1.0 / width)
    return mean, lax.rsqrt(second - mean * mean + EPS)


def tiles(total, size):
    return total // size


def row_loop(rows, size, fn):
    @pl.loop(0, rows // size)
    def _(step):
        fn(pl.ds(pl.multiple_of(step * size, size), size))


def merge_body(
    t_ref, x_ref, w_own, w_oth, mg, ms, g1, s1, stream0, mn_own, mn_oth, first
):
    t = t_ref[0]
    rows, half = mn_own.shape
    width = 2 * half

    def norm(r):
        xa = x_ref[t, r, :].astype(F32)
        xb = x_ref[1 - t, r, :].astype(F32)
        total = jnp.sum(xa, 1, keepdims=True) + jnp.sum(xb, 1, keepdims=True)
        square = jnp.sum(xa * xa, 1, keepdims=True) + jnp.sum(xb * xb, 1, keepdims=True)
        mean = total * (1.0 / width)
        scale = lax.rsqrt(square * (1.0 / width) - mean * mean + EPS)
        mn_own[r, :] = ((xa - mean) * scale * mg[t] + ms[t]).astype(BF16)
        mn_oth[r, :] = ((xb - mean) * scale * mg[1 - t] + ms[1 - t]).astype(BF16)

    row_loop(rows, 32, norm)
    model = stream0.shape[1]

    @pl.loop(0, model // 256)
    def _(c):
        cols = pl.ds(pl.multiple_of(c * 256, 256), 256)
        stream0[:, cols] = dot(mn_own[...], w_own[:, cols]) + dot(mn_oth[...], w_oth[:, cols])

    def norm1(r):
        x = stream0[r, :]
        mean, scale = stats(x, model)
        first[r, :] = ((x - mean) * scale * g1[...] + s1[...]).astype(BF16)

    row_loop(rows, 32, norm1)


def qkv_body(first, w_own, w_oth, bias, out):
    half = w_own.shape[2]
    for s in range(3):
        for side, w in enumerate((w_own, w_oth)):

            @pl.loop(0, half // 256)
            def _(c):
                src = pl.ds(pl.multiple_of(c * 256, 256), 256)
                dst = pl.ds(pl.multiple_of(side * half + c * 256, 256), 256)
                out[s, :, dst] = (dot(first[...], w[s, :, src]) + bias[s, :, dst]).astype(BF16)


def onehot_of(index_row, entries):
    ids = lax.broadcasted_iota(jnp.int32, (entries, index_row.shape[1]), 0)
    return jnp.where(ids == index_row, 1.0, 0.0).astype(BF16)


def bias_body(index, table, out):
    heads = out.shape[0] // PAD
    entries = table.shape[1]
    area = index.shape[0]

    @pl.loop(0, area)
    def _(j):
        hot = onehot_of(index[pl.ds(j, 1), :], entries)
        both = dot(table[...], hot)
        out[pl.ds(pl.multiple_of(j * heads, heads), heads), :] = both[:heads] + both[heads:]

    out[pl.ds(area * heads, (PAD - area) * heads), :] = jnp.full(
        ((PAD - area) * heads, out.shape[1]), -1e30, F32
    )


def rel_body(index, sums, out):
    heads = sums.shape[0] // PAD
    entries = out.shape[1]
    area = index.shape[0]
    out[...] = jnp.zeros_like(out)

    @pl.loop(0, area)
    def _(j):
        hot = onehot_of(index[pl.ds(j, 1), :], entries)
        s = sums[pl.ds(pl.multiple_of(j * heads, heads), heads), :]
        top = s.astype(BF16)
        low = (s - top.astype(F32)).astype(BF16)
        both = dot_nt(jnp.concatenate([top, low], 0), hot)
        out[...] += both[:heads] + both[heads:]


def head_masks(rows, width, dim):
    lane = lax.broadcasted_iota(jnp.int32, (rows, width), 1) // dim
    return [lane == h for h in range(width // dim)]


def stacked(block, masks):
    return jnp.concatenate([jnp.where(m, block, 0.0).astype(BF16) for m in masks], 0)


def attention_body(dim, heads, q, k, v, bias, out, lse):
    g = pl.program_id(0)
    width = q.shape[1]
    per = width // dim
    windows = q.shape[0] // PAD
    scale = dim ** (-0.5)
    masks = head_masks(PAD, width, dim)
    for w in range(windows):
        rows = pl.ds(w * PAD, PAD)
        kst = stacked(k[rows, :], masks)
        s_all = dot_nt(kst, q[rows, :])
        vt = v[rows, :].T
        outs = []
        for h in range(per):
            b = bias[pl.ds(g * per + h, PAD, stride=heads), :][:, :PAD]
            s = s_all[h * PAD : (h + 1) * PAD] * scale + b
            top = jnp.max(s, 0, keepdims=True)
            e = jnp.exp(s - top)
            total = jnp.sum(e, 0, keepdims=True)
            p = (e * (1.0 / total)).astype(BF16)
            lse[0, pl.ds(w * per + h, 1), :] = top + jnp.log(total)
            outs.append(dot(vt[h * dim : (h + 1) * dim], p))
        out[rows, :] = jnp.concatenate(outs, 0).T.astype(BF16)


def attention_back_body(dim, heads, q, k, v, do, bias, lse, dq, dk, dv, sums, vec):
    g = pl.program_id(0)
    width = q.shape[1]
    per = width // dim
    windows = q.shape[0] // PAD
    scale = dim ** (-0.5)
    masks = head_masks(PAD, width, dim)
    q_sum = jnp.zeros((1, width), F32)
    v_sum = jnp.zeros((1, width), F32)
    for w in range(windows):
        rows = pl.ds(w * PAD, PAD)
        kb, vb, qb, gb = k[rows, :], v[rows, :], q[rows, :], do[rows, :]
        s_all = dot_nt(stacked(kb, masks), qb)
        dp_all = dot_nt(stacked(vb, masks), gb)
        kt = kb.T
        p_parts, g_parts, dqs = [], [], []
        for h in range(per):
            at = pl.ds(g * per + h, PAD, stride=heads)
            b = bias[at, :][:, :PAD]
            p = jnp.exp(
                s_all[h * PAD : (h + 1) * PAD] * scale + b - lse[0, pl.ds(w * per + h, 1), :]
            )
            dp = dp_all[h * PAD : (h + 1) * PAD]
            inner = jnp.sum(dp * p, 0, keepdims=True)
            gs = (p * (dp - inner)).astype(BF16)
            gf = gs.astype(F32)
            if w == 0:
                sums[at, pl.ds(0, PAD)] = gf
            else:
                sums[at, pl.ds(0, PAD)] += gf
            p_parts.append(p.astype(BF16))
            g_parts.append(gs)
            dqs.append(dot(kt[h * dim : (h + 1) * dim], gs))
        dv_all = dot(jnp.concatenate(p_parts, 0), gb)
        dk_all = dot(jnp.concatenate(g_parts, 0), qb)
        dv_w = dv_all[:PAD]
        dk_w = dk_all[:PAD]
        for h in range(1, per):
            dv_w = jnp.where(masks[h], dv_all[h * PAD : (h + 1) * PAD], dv_w)
            dk_w = jnp.where(masks[h], dk_all[h * PAD : (h + 1) * PAD], dk_w)
        dq_w = (jnp.concatenate(dqs, 0).T * scale).astype(BF16)
        dv_w = dv_w.astype(BF16)
        dq[rows, :] = dq_w
        dk[rows, :] = (dk_w * scale).astype(BF16)
        dv[rows, :] = dv_w
        q_sum += jnp.sum(dq_w.astype(F32), 0, keepdims=True)
        v_sum += jnp.sum(dv_w.astype(F32), 0, keepdims=True)
    vec[...] = jnp.concatenate([q_sum, v_sum], 0)


def proj_body(att, w_own, w_oth, pb, stream0, g2, s2, stream1, second):
    rows, model = stream0.shape
    half = w_own.shape[0]

    @pl.loop(0, model // 256)
    def _(c):
        cols = pl.ds(pl.multiple_of(c * 256, 256), 256)
        value = dot(att[:, :half], w_own[:, cols]) + dot(att[:, half:], w_oth[:, cols])
        stream1[:, cols] = stream0[:, cols] + (value + pb[:, cols])

    def norm(r):
        x = stream1[r, :]
        mean, scale = stats(x, model)
        second[r, :] = ((x - mean) * scale * g2[...] + s2[...]).astype(BF16)

    row_loop(rows, 32, norm)


def mlp_body(
    t_ref, sec_own, sec_sib, cot_own, cot_oth, keep, s1, w1, b1, w2,
    wg1, wg2, gb1, gb2, feed, g2_sib, g2_own, d_out,
    gf, gft, sect, facc, gacc,
):
    t = t_ref[0]
    c = pl.program_id(0)
    rows, model = sec_own.shape
    half = model // 2

    @pl.when(c == 0)
    def _():
        own_cols = pl.ds(pl.multiple_of(t * half, half), half)
        oth_cols = pl.ds(pl.multiple_of((1 - t) * half, half), half)
        total = jnp.zeros((1, half), F32)
        for side, who in ((0, t), (1, 1 - t)):
            mine = cot_own[who].astype(F32) * keep[who]
            gf[side, :, own_cols] = mine.astype(BF16)
            gf[side, :, oth_cols] = (cot_oth[who].astype(F32) * keep[who]).astype(BF16)
            total += jnp.sum(mine, 0, keepdims=True)
        gb2[...] = total
        d_out[...] = gf[0]
        for side, sec in ((0, sec_own), (1, sec_sib)):

            @pl.loop(0, model // 128)
            def _(b):
                at = pl.ds(pl.multiple_of(b * 128, 128), 128)
                gft[side, at, :] = gf[side, :, at].T
                sect[side, at, :] = sec[:, at].T

        facc[...] = jnp.zeros_like(facc)
        gacc[...] = jnp.zeros_like(gacc)

    size = w1.shape[1]
    acts, ghs = [], []
    bias_sum = jnp.zeros((1, size), F32)
    for side, sec in ((0, sec_own), (1, sec_sib)):
        hidden = dot(sec[...], w1[...]) + b1[...]
        d_act = dot_nt(gf[side], w2[...])
        cdf = 0.5 * (1.0 + lax.erf(hidden * 0.7071067811865476))
        pdf = jnp.exp(hidden * hidden * -0.5) * 0.3989422804014327
        act = (hidden * cdf).astype(BF16)
        gh = (d_act * (cdf + hidden * pdf)).astype(BF16)
        bias_sum += jnp.sum(gh.astype(F32), 0, keepdims=True)
        facc[side] += dot(act, w2[...])
        gacc[side] += dot_nt(gh, w1[...])
        acts.append(act)
        ghs.append(gh)
    gb1[...] = bias_sum
    wg1[...] = (dot(sect[0], ghs[0]) + dot(sect[1], ghs[1])).astype(BF16)
    wg2[...] = (dot(gft[0], acts[0]) + dot(gft[1], acts[1])).astype(BF16)

    @pl.when(c == pl.num_programs(0) - 1)
    def _():
        own_cols = pl.ds(pl.multiple_of(t * half, half), half)
        oth_cols = pl.ds(pl.multiple_of((1 - t) * half, half), half)
        feed[0, t] = facc[0, :, own_cols] + s1[:, own_cols]
        feed[0, 1 - t] = facc[1, :, own_cols]
        feed[1, t] = facc[0, :, oth_cols] + s1[:, oth_cols]
        feed[1, 1 - t] = facc[1, :, oth_cols]
        g2_own[...] = gacc[0]
        g2_sib[...] = gacc[1].astype(BF16)


def norm_back(e, x, gain, width):
    mean, scale = stats(x, width)
    xhat = (x - mean) * scale
    scaled = e * gain
    first = jnp.sum(scaled, 1, keepdims=True) * (1.0 / width)
    cross = jnp.sum(scaled * xhat, 1, keepdims=True) * (1.0 / width)
    return scale * (scaled - first - xhat * cross), e * xhat


def norm2_back_body(
    g_own, g_recv, stream1, d_out, g2, w_own, w_oth, d_s1, g_att, g_attended, vec
):
    rows, model = g_own.shape
    half = w_own.shape[0]
    vec[...] = jnp.zeros_like(vec)

    def norm(r):
        e = g_own[r, :] + g_recv[r, :].astype(F32)
        dv, ex = norm_back(e, stream1[r, :], g2[...], model)
        d = d_out[r, :].astype(F32) + dv
        d_s1[r, :] = d
        low = d.astype(BF16)
        g_att[r, :] = low
        vec[0:1, :] += jnp.sum(ex, 0, keepdims=True)
        vec[1:2, :] += jnp.sum(e, 0, keepdims=True)
        vec[2:3, :] += jnp.sum(low.astype(F32), 0, keepdims=True)

    row_loop(rows, 32, norm)
    for side, w in enumerate((w_own, w_oth)):

        @pl.loop(0, half // 256)
        def _(c):
            src = pl.ds(pl.multiple_of(c * 256, 256), 256)
            dst = pl.ds(pl.multiple_of(side * half + c * 256, 256), 256)
            g_attended[:, dst] = dot_nt(g_att[...], w[src, :]).astype(BF16)


def norm1_back_body(dq, dk, dv, w_own, w_oth, stream0, d_s1, g1, d_s0, g_s0, vec, acc):
    rows, model = stream0.shape
    half = w_own.shape[2]
    vec[...] = jnp.zeros_like(vec)

    @pl.loop(0, model // 256)
    def _(c):
        at = pl.ds(pl.multiple_of(c * 256, 256), 256)
        value = jnp.zeros((rows, 256), F32)
        for s, d in enumerate((dq, dk, dv)):
            value += dot_nt(d[:, :half], w_own[s, at, :])
            value += dot_nt(d[:, half:], w_oth[s, at, :])
        acc[:, at] = value

    def norm(r):
        e = acc[r, :]
        d, ex = norm_back(e, stream0[r, :], g1[...], model)
        d = d_s1[r, :] + d
        d_s0[r, :] = d.astype(BF16)
        g_s0[r, :] = d.astype(BF16)
        vec[0:1, :] += jnp.sum(ex, 0, keepdims=True)
        vec[1:2, :] += jnp.sum(e, 0, keepdims=True)

    row_loop(rows, 32, norm)


def merge_back_body(t_ref, g_s0, w_own, w_oth, x_ref, mg, d_merged, vec, acc):
    t = t_ref[0]
    rows = g_s0.shape[0]
    half = w_own.shape[0]
    width = 2 * half
    vec[...] = jnp.zeros_like(vec)
    for side, w in enumerate((w_own, w_oth)):

        @pl.loop(0, half // 256)
        def _(c):
            at = pl.ds(pl.multiple_of(c * 256, 256), 256)
            acc[side, :, at] = dot_nt(g_s0[...], w[at, :])

    def norm(r):
        xs = [x_ref[t, r, :].astype(F32), x_ref[1 - t, r, :].astype(F32)]
        es = [acc[0, r, :], acc[1, r, :]]
        gains = [mg[t], mg[1 - t]]
        total = sum(jnp.sum(x, 1, keepdims=True) for x in xs)
        square = sum(jnp.sum(x * x, 1, keepdims=True) for x in xs)
        mean = total * (1.0 / width)
        scale = lax.rsqrt(square * (1.0 / width) - mean * mean + EPS)
        hats = [(x - mean) * scale for x in xs]
        scaled = [e * g for e, g in zip(es, gains)]
        first = sum(jnp.sum(s, 1, keepdims=True) for s in scaled) * (1.0 / width)
        cross = sum(jnp.sum(s * h, 1, keepdims=True) for s, h in zip(scaled, hats)) * (1.0 / width)
        for side, who in ((0, t), (1, 1 - t)):
            d_merged[who, r, :] = scale * (scaled[side] - first - hats[side] * cross)
            vec[2 * side : 2 * side + 1, :] += jnp.sum(es[side] * hats[side], 0, keepdims=True)
            vec[2 * side + 1 : 2 * side + 2, :] += jnp.sum(es[side], 0, keepdims=True)

    row_loop(rows, 16, norm)


def weight_grad_body(l_own, l_sib, r_own, r_sib, out, lt):
    for side, l in enumerate((l_own, l_sib)):

        @pl.loop(0, l.shape[1] // 128)
        def _(b):
            at = pl.ds(pl.multiple_of(b * 128, 128), 128)
            lt[side, at, :] = l[:, at].T

    @pl.loop(0, out.shape[1] // 256)
    def _(c):
        at = pl.ds(pl.multiple_of(c * 256, 256), 256)
        out[:, at] = (dot(lt[0], r_own[:, at]) + dot(lt[1], r_sib[:, at])).astype(BF16)


def weight_grad(l_own, l_sib, r_own, r_sib):
    rows, model = l_own.shape
    n = r_own.shape[1]
    return whole(
        weight_grad_body,
        shape((model, n), BF16),
        (l_own, l_sib, r_own, r_sib),
        [pltpu.VMEM((2, model, rows), BF16)],
        flops=4 * rows * model * n,
        nbytes=2 * (2 * rows * (model + n) + model * n),
    )


def swap(value):
    return lax.ppermute(value, "tp", [(0, 1), (1, 0)])


def take(value, index):
    return lax.dynamic_index_in_dim(value, index, 0, keepdims=False)


class Grid:
    def __init__(self, count):
        side = 1
        while 4 * (side + 1) * (side + 1) <= count:
            side += 1
        self.sizes = {"z": count // (side * side), "y": side, "x": side}
        self.strides = {"z": side * side, "y": side, "x": 1}
        self.count = count

    def place(self, axis):
        me = lax.axis_index("win")
        return (me // self.strides[axis]) % self.sizes[axis]

    def shift(self, value, axis, delta, senders):
        stride, size = self.strides[axis], self.sizes[axis]
        pairs = []
        for w in range(self.count):
            c = (w // stride) % size
            if c in senders:
                pairs.append((w, w + delta * stride))
        return lax.ppermute(value, "win", pairs)

    def chain(self, value, axis):
        size = self.sizes[axis]
        c = self.place(axis)
        right = left = None
        for s in range(1, size):
            go_right = take(value, jnp.clip(size - s + c, 0, size - 1))
            go_left = take(value, jnp.clip(c - 1 - (size - 1 - s), 0, size - 1))
            if s > 1:
                go_right = (go_right.astype(F32) + right.astype(F32)).astype(BF16)
                go_left = (go_left.astype(F32) + left.astype(F32)).astype(BF16)
            right = self.shift(go_right, axis, 1, range(0, min(s, size - 1)))
            left = self.shift(go_left, axis, -1, range(max(size - s, 1), size))
        return take(value, c).astype(F32) + right.astype(F32) + left.astype(F32)

    def scatter(self, value, order):
        sizes = self.sizes
        v = value.reshape(sizes["z"], sizes["y"], sizes["x"], -1, value.shape[1])
        left = ["z", "y", "x"]
        for step, axis in enumerate(order):
            v = self.chain(jnp.moveaxis(v, left.index(axis), 0), axis)
            left.remove(axis)
            if step < 2:
                v = v.astype(BF16)
        return v

    def total(self, value):
        for axis in ("x", "y", "z"):
            size, stride = self.sizes[axis], self.strides[axis]
            hop = 1
            while hop < size:
                pairs = []
                for w in range(self.count):
                    c = (w // stride) % size
                    pairs.append((w, w + ((c ^ hop) - c) * stride))
                value = value + lax.ppermute(value, "win", pairs)
                hop *= 2
        return value


def solution(mesh):
    count = mesh.shape["win"]

    def shards(
        pixels, merge_gain, merge_shift, merge_weight, norm1_gain, norm1_shift, qkv_weight,
        qkv_bias, rel_table, proj_weight, proj_bias, norm2_gain, norm2_shift, fc1_weight,
        fc1_bias, fc2_weight, fc2_bias, rel_index, keep, cotangent,
    ):
        grid = Grid(count)
        t = lax.axis_index("tp")
        t_arr = t.reshape(1).astype(jnp.int32)
        wins, height, _, channels = pixels.shape
        side = height // 2
        area = side * side
        rows = wins * PAD
        model = merge_weight.shape[1]
        half = model // 2
        heads_here = rel_table.shape[1]
        heads = 2 * heads_here
        dim = half // heads_here
        entries = rel_table.shape[0]
        slots = -(-entries // 128) * 128
        hidden = fc1_weight.shape[1]

        def pair(own, oth):
            return jnp.where(
                t == 0, jnp.concatenate([own, oth], -1), jnp.concatenate([oth, own], -1)
            )

        flat = [
            merge_gain, merge_shift, norm1_gain, norm1_shift, qkv_bias, rel_table.T,
            proj_bias, norm2_gain, norm2_shift,
        ]
        packed = jnp.concatenate([f.reshape(-1) for f in flat])
        got = swap(packed)
        others, at = [], 0
        for f in flat:
            others.append(got[at : at + f.size].reshape(f.shape))
            at += f.size
        wm_oth = swap(merge_weight)
        wqkv = qkv_weight.transpose(1, 0, 2)
        wqkv_oth = swap(wqkv)
        wp_oth = swap(proj_weight)
        mg = pair(merge_gain, others[0]).reshape(2, 1, model)
        ms = pair(merge_shift, others[1]).reshape(2, 1, model)
        g1 = pair(norm1_gain, others[2]).reshape(1, model)
        s1 = pair(norm1_shift, others[3]).reshape(1, model)
        qb = jnp.concatenate([qkv_bias, others[4]], -1)
        qb = jnp.stack([qb[0], jnp.zeros_like(qb[0]), qb[1]]).reshape(3, 1, model)
        pb = pair(proj_bias, others[6]).reshape(1, model)
        g2 = pair(norm2_gain, others[7]).reshape(1, model)
        s2 = pair(norm2_shift, others[8]).reshape(1, model)
        table = jnp.concatenate([rel_table.T, others[5].reshape(rel_table.T.shape)], 0)
        table = jnp.pad(table, ((0, 0), (0, slots - entries)))
        top = table.astype(BF16)
        table2 = jnp.concatenate([top, (table - top.astype(F32)).astype(BF16)], 0)

        x = (
            pixels.reshape(wins, side, 2, side, 2, channels)
            .transpose(4, 0, 1, 3, 2, 5)
            .reshape(2, wins, area, model)
        )
        x = jnp.pad(x, ((0, 0), (0, 0), (0, PAD - area), (0, 0))).reshape(2, rows, model)
        stream0, mn_own, mn_oth, first = whole(
            merge_body,
            (shape((rows, model)), shape((rows, model), BF16), shape((rows, model), BF16),
             shape((rows, model), BF16)),
            (t_arr, x, merge_weight, wm_oth, mg, ms, g1, s1),
            flops=4 * rows * model * model, nbytes=1e7, smem_first=True,
        )
        first_sib = swap(first)
        mn_sib = swap(mn_oth)
        qkv = whole(
            qkv_body, shape((3, rows, model), BF16), (first, wqkv, wqkv_oth, qb),
            flops=6 * rows * model * model, nbytes=1e7,
        )
        index_t = jnp.pad(rel_index.T, ((0, 0), (0, PAD - area)))
        bias = whole(
            bias_body, shape((PAD * heads, PAD)), (index_t, table2),
            flops=4 * heads * slots * area * 128, nbytes=2e6,
        )
        groups = model // 128
        per = 128 // dim
        lanes = pl.BlockSpec((rows, 128), lambda g: (0, g))

        def slot(s):
            return pl.BlockSpec((None, rows, 128), lambda g: (s, 0, g))

        lse_spec = pl.BlockSpec((1, wins * per, PAD), lambda g: (g, 0, 0))

        def attention(*refs):
            attention_body(dim, heads, *refs)

        attended, lse = call(
            attention,
            (shape((rows, model), BF16), shape((groups, wins * per, PAD))),
            (qkv, qkv, qkv, bias),
            flops=4 * rows * model * 448, nbytes=6e6,
            grid=(groups,),
            in_specs=[slot(0), slot(1), slot(2), VMEM],
            out_specs=(lanes, lse_spec),
        )
        att_sib = swap(attended[:, half:])
        stream1, second = whole(
            proj_body, (shape((rows, model)), shape((rows, model), BF16)),
            (attended, proj_weight, wp_oth, pb, stream0, g2, s2),
            flops=2 * rows * model * model, nbytes=8e6,
        )
        second_sib = swap(second)
        cot = jnp.pad(
            cotangent.reshape(2 * wins, area, half), ((0, 0), (0, PAD - area), (0, 0))
        ).reshape(2, rows, half)
        cot_oth = swap(cot)
        keep_rows = jnp.pad(
            keep.astype(F32).reshape(2 * wins, area), ((0, 0), (0, PAD - area))
        ).reshape(2, rows, 1)
        chunk = 512
        col_spec = pl.BlockSpec((model, chunk), lambda c: (0, c))
        row_spec = pl.BlockSpec((1, chunk), lambda c: (0, c))
        wg1, wg2, gb1, gb2, feed, g2_send, g2_own, d_out = call(
            mlp_body,
            (
                shape((model, hidden), BF16), shape((model, hidden), BF16), shape((1, hidden)),
                shape((1, half)), shape((2, 2, rows, half)), shape((rows, model), BF16),
                shape((rows, model)), shape((rows, model), BF16),
            ),
            (t_arr, second, second_sib, cot, cot_oth, keep_rows, stream1, fc1_weight,
             fc1_bias.reshape(1, hidden), fc2_weight),
            [
                pltpu.VMEM((2, rows, model), BF16), pltpu.VMEM((2, model, rows), BF16),
                pltpu.VMEM((2, model, rows), BF16), pltpu.VMEM((2, rows, model), F32),
                pltpu.VMEM((2, rows, model), F32),
            ],
            flops=24 * rows * model * hidden, nbytes=3e7,
            grid=(hidden // chunk,),
            in_specs=[SMEM, VMEM, VMEM, VMEM, VMEM, VMEM, VMEM, col_spec, row_spec,
                      pl.BlockSpec((chunk, model), lambda c: (c, 0))],
            out_specs=(col_spec, col_spec, row_spec, VMEM, VMEM, VMEM, VMEM, VMEM),
        )
        g2_recv = swap(g2_send)
        feed_recv = swap(feed[1].astype(BF16))
        out = keep_rows * (feed[0] + feed_recv.astype(F32) + fc2_bias)
        out = out.reshape(2 * wins, PAD, half)[:, :area].reshape(2 * wins * area, half).astype(BF16)
        fc1_grad = grid.scatter(wg1, ("x", "y", "z"))
        fc2_grad = grid.scatter(wg2, ("y", "x", "z")).T

        d_s1, g_att, g_attended, vec2 = whole(
            norm2_back_body,
            (shape((rows, model)), shape((rows, model), BF16), shape((rows, model), BF16),
             shape((3, model))),
            (g2_own, g2_recv, stream1, d_out, g2, proj_weight, wp_oth),
            flops=2 * rows * model * model, nbytes=1e7,
        )
        g_att_sib = swap(g_att)

        def attention_back(*refs):
            attention_back_body(dim, heads, *refs)

        dq, dk, dv, sums, qkv_sums = call(
            attention_back,
            (
                shape((rows, model), BF16), shape((rows, model), BF16), shape((rows, model), BF16),
                shape((PAD * heads, PAD)), shape((2, model)),
            ),
            (qkv, qkv, qkv, g_attended, bias, lse),
            flops=10 * rows * model * 448, nbytes=1e7,
            grid=(groups,),
            in_specs=[slot(0), slot(1), slot(2), lanes, VMEM, lse_spec],
            out_specs=(lanes, lanes, lanes, VMEM, pl.BlockSpec((2, 128), lambda g: (0, g))),
        )
        proj_part = weight_grad(g_att, g_att_sib, attended[:, :half], att_sib)
        d_qkv = jnp.concatenate([dq[:, :half], dk[:, :half], dv[:, :half]], 1)
        d_qkv_sib = swap(jnp.concatenate([dq[:, half:], dk[:, half:], dv[:, half:]], 1))
        qkv_part = weight_grad(first, first_sib, d_qkv, d_qkv_sib)
        d_s0, g_s0, vec1 = whole(
            norm1_back_body,
            (shape((rows, model), BF16), shape((rows, model), BF16), shape((2, model))),
            (dq, dk, dv, wqkv, wqkv_oth, stream0, d_s1, g1),
            [pltpu.VMEM((rows, model), F32)],
            flops=6 * rows * model * model, nbytes=1e7,
        )
        g_s0_sib = swap(g_s0)
        rel_sums = whole(
            rel_body, shape((heads, slots)), (index_t, sums),
            flops=4 * heads * slots * area * 128, nbytes=2e6,
        )
        merge_part = weight_grad(g_s0, g_s0_sib, mn_own, mn_sib)
        d_merged, vec0 = whole(
            merge_back_body,
            (shape((2, rows, model)), shape((4, model))),
            (t_arr, g_s0, merge_weight, wm_oth, x, mg),
            [pltpu.VMEM((2, rows, model), F32)],
            flops=4 * rows * model * model, nbytes=1e7, smem_first=True,
        )
        pixels_grad = (
            d_merged.reshape(2, wins, PAD, 2, channels)[:, :, :area]
            .reshape(2, wins, side, side, 2, channels)
            .transpose(1, 2, 4, 3, 0, 5)
            .reshape(pixels.shape)
        )
        a_part = jnp.concatenate([proj_part, qkv_part[:, :half]], 1)
        b_part = qkv_part[:, half:]
        a_sum = grid.scatter(a_part, ("x", "y", "z"))
        b_sum = grid.scatter(b_part, ("y", "x", "z"))
        ma_sum = grid.scatter(merge_part[:, :half], ("x", "y", "z"))
        mb_sum = grid.scatter(merge_part[:, half:], ("y", "x", "z"))
        proj_grad = a_sum[:, :half].T
        qkv_grad = jnp.stack([a_sum[:, half:], b_sum[:, :half], b_sum[:, half:]], 1)
        merge_grad = jnp.concatenate([ma_sum, mb_sum], 1).T

        def sides(v):
            both = jnp.stack([v[..., :half], v[..., half:]])
            return take(both, t), take(both, 1 - t)

        n2, n1 = sides(vec2), sides(vec1)
        rel = rel_sums[:, :entries]
        keepers = [
            vec0[0:2], n1[0], qkv_sums[:, :half], rel[:heads_here], n2[0]
        ]
        leavers = [
            vec0[2:4], n1[1], qkv_sums[:, half:], rel[heads_here:], n2[1]
        ]
        back = swap(jnp.concatenate([v.reshape(-1) for v in leavers]))
        mine = jnp.concatenate([v.reshape(-1) for v in keepers]) + back
        vectors = grid.total(jnp.concatenate([mine, gb1.reshape(-1), gb2.reshape(-1)]))
        parts, at = [], 0
        for v in keepers + [gb1, gb2]:
            parts.append(vectors[at : at + v.size].reshape(v.shape))
            at += v.size
        v0, v1, vq, vr, v2, vb1, vb2 = parts
        return (
            out, pixels_grad, v0[0], v0[1], merge_grad, v1[0], v1[1], qkv_grad, vq, vr.T,
            proj_grad, v2[2], v2[0], v2[1], fc1_grad, vb1[0], fc2_grad, vb2[0],
        )

    in_specs = (
        P(("win", "tp"), None, None, None), P("tp"), P("tp"), P("tp", None), P("tp"), P("tp"),
        P(None, None, "tp"), P(None, "tp"), P(None, "tp"), P("tp", None), P("tp"), P("tp"),
        P("tp"), P(None, "tp"), P("tp"), P("tp", None), P("tp"), P(), P("win"), P("win", "tp"),
    )
    out_specs = (
        P("win", "tp"), P(("win", "tp"), None, None, None), P("tp"), P("tp"), P("tp", "win"),
        P("tp"), P("tp"), P("win", None, "tp"), P(None, "tp"), P(None, "tp"), P("tp", "win"),
        P("tp"), P("tp"), P("tp"), P("win", "tp"), P("tp"), P("tp", "win"), P("tp"),
    )
    return jax.shard_map(shards, mesh=mesh, in_specs=in_specs, out_specs=out_specs, check_vma=False)
```

```python
import jax
import jax.numpy as jnp
from jax import lax
from jax.experimental import pallas as pl
from jax.experimental.pallas import tpu as pltpu
from jax.sharding import PartitionSpec as P

EPS = 1e-05
F32 = jnp.float32
BF16 = jnp.bfloat16
VMEM = pl.BlockSpec(memory_space=pltpu.VMEM)
SMEM = pl.BlockSpec(memory_space=pltpu.SMEM)
PAD = 112
LIMIT = 60 * 1024 * 1024
MESH = pl.DeviceIdType.MESH


def call(body, out, ins, scratch=(), flops=0, nbytes=0, **more):
    return pl.pallas_call(
        body,
        out_shape=out,
        scratch_shapes=list(scratch),
        compiler_params=pltpu.CompilerParams(vmem_limit_bytes=LIMIT),
        cost_estimate=pl.CostEstimate(
            flops=int(flops), bytes_accessed=int(nbytes), transcendentals=0
        ),
        **more,
    )(*ins)


def whole(body, out, ins, scratch=(), flops=0, nbytes=0, smem_first=False):
    specs = [VMEM] * len(ins)
    if smem_first:
        specs[0] = SMEM
    outs = jax.tree.map(lambda _: VMEM, out)
    return call(body, out, ins, scratch, flops, nbytes, in_specs=specs, out_specs=outs)


def shape(dims, dtype=F32):
    return jax.ShapeDtypeStruct(tuple(dims), dtype)


def dot(a, b):
    return jnp.dot(a, b, preferred_element_type=F32)


def dot_nt(a, b):
    return lax.dot_general(a, b, (((1,), (1,)), ((), ())), preferred_element_type=F32)


def stats(x, width):
    mean = jnp.sum(x, 1, keepdims=True) * (1.0 / width)
    second = jnp.sum(x * x, 1, keepdims=True) * (1.0 / width)
    return mean, lax.rsqrt(second - mean * mean + EPS)


def tiles(total, size):
    return total // size


def row_loop(rows, size, fn):
    @pl.loop(0, rows // size)
    def _(step):
        fn(pl.ds(pl.multiple_of(step * size, size), size))


def merge_body(
    t_ref, x_ref, w_own, w_oth, mg, ms, g1, s1, stream0, mn_own, mn_oth, first
):
    t = t_ref[0]
    rows, half = mn_own.shape
    width = 2 * half

    def norm(r):
        xa = x_ref[t, r, :].astype(F32)
        xb = x_ref[1 - t, r, :].astype(F32)
        total = jnp.sum(xa, 1, keepdims=True) + jnp.sum(xb, 1, keepdims=True)
        square = jnp.sum(xa * xa, 1, keepdims=True) + jnp.sum(xb * xb, 1, keepdims=True)
        mean = total * (1.0 / width)
        scale = lax.rsqrt(square * (1.0 / width) - mean * mean + EPS)
        mn_own[r, :] = ((xa - mean) * scale * mg[t] + ms[t]).astype(BF16)
        mn_oth[r, :] = ((xb - mean) * scale * mg[1 - t] + ms[1 - t]).astype(BF16)

    row_loop(rows, 32, norm)
    model = stream0.shape[1]

    @pl.loop(0, model // 256)
    def _(c):
        cols = pl.ds(pl.multiple_of(c * 256, 256), 256)
        stream0[:, cols] = dot(mn_own[...], w_own[:, cols]) + dot(mn_oth[...], w_oth[:, cols])

    def norm1(r):
        x = stream0[r, :]
        mean, scale = stats(x, model)
        first[r, :] = ((x - mean) * scale * g1[...] + s1[...]).astype(BF16)

    row_loop(rows, 32, norm1)


def qkv_body(first, w_own, w_oth, bias, out):
    half = w_own.shape[2]
    for s in range(3):
        for side, w in enumerate((w_own, w_oth)):

            @pl.loop(0, half // 256)
            def _(c):
                src = pl.ds(pl.multiple_of(c * 256, 256), 256)
                dst = pl.ds(pl.multiple_of(side * half + c * 256, 256), 256)
                out[s, :, dst] = (dot(first[...], w[s, :, src]) + bias[s, :, dst]).astype(BF16)


def onehot_of(index_row, entries):
    ids = lax.broadcasted_iota(jnp.int32, (entries, index_row.shape[1]), 0)
    return jnp.where(ids == index_row, 1.0, 0.0).astype(BF16)


def bias_body(index, table, out):
    heads = out.shape[0] // PAD
    entries = table.shape[1]
    area = index.shape[0]

    @pl.loop(0, area)
    def _(j):
        hot = onehot_of(index[pl.ds(j, 1), :], entries)
        both = dot(table[...], hot)
        out[pl.ds(pl.multiple_of(j * heads, heads), heads), :] = both[:heads] + both[heads:]

    out[pl.ds(area * heads, (PAD - area) * heads), :] = jnp.full(
        ((PAD - area) * heads, out.shape[1]), -1e30, F32
    )


def rel_body(index, sums, out):
    heads = sums.shape[0] // PAD
    entries = out.shape[1]
    area = index.shape[0]
    out[...] = jnp.zeros_like(out)

    @pl.loop(0, area)
    def _(j):
        hot = onehot_of(index[pl.ds(j, 1), :], entries)
        s = sums[pl.ds(pl.multiple_of(j * heads, heads), heads), :]
        top = s.astype(BF16)
        low = (s - top.astype(F32)).astype(BF16)
        both = dot_nt(jnp.concatenate([top, low], 0), hot)
        out[...] += both[:heads] + both[heads:]


def head_masks(rows, width, dim):
    lane = lax.broadcasted_iota(jnp.int32, (rows, width), 1) // dim
    return [lane == h for h in range(width // dim)]


def stacked(block, masks):
    return jnp.concatenate([jnp.where(m, block, 0.0).astype(BF16) for m in masks], 0)


def attention_body(dim, heads, q, k, v, bias, out, lse):
    g = pl.program_id(0)
    width = q.shape[1]
    per = width // dim
    windows = q.shape[0] // PAD
    scale = dim ** (-0.5)
    masks = head_masks(PAD, width, dim)
    for w in range(windows):
        rows = pl.ds(w * PAD, PAD)
        kst = stacked(k[rows, :], masks)
        s_all = dot_nt(kst, q[rows, :])
        vt = v[rows, :].T
        outs = []
        for h in range(per):
            b = bias[pl.ds(g * per + h, PAD, stride=heads), :][:, :PAD]
            s = s_all[h * PAD : (h + 1) * PAD] * scale + b
            top = jnp.max(s, 0, keepdims=True)
            e = jnp.exp(s - top)
            total = jnp.sum(e, 0, keepdims=True)
            p = (e * (1.0 / total)).astype(BF16)
            lse[0, pl.ds(w * per + h, 1), :] = top + jnp.log(total)
            outs.append(dot(vt[h * dim : (h + 1) * dim], p))
        out[rows, :] = jnp.concatenate(outs, 0).T.astype(BF16)


def attention_back_body(dim, heads, q, k, v, do, bias, lse, dq, dk, dv, sums, vec):
    g = pl.program_id(0)
    width = q.shape[1]
    per = width // dim
    windows = q.shape[0] // PAD
    scale = dim ** (-0.5)
    masks = head_masks(PAD, width, dim)
    q_sum = jnp.zeros((1, width), F32)
    v_sum = jnp.zeros((1, width), F32)
    for w in range(windows):
        rows = pl.ds(w * PAD, PAD)
        kb, vb, qb, gb = k[rows, :], v[rows, :], q[rows, :], do[rows, :]
        s_all = dot_nt(stacked(kb, masks), qb)
        dp_all = dot_nt(stacked(vb, masks), gb)
        kt = kb.T
        p_parts, g_parts, dqs = [], [], []
        for h in range(per):
            at = pl.ds(g * per + h, PAD, stride=heads)
            b = bias[at, :][:, :PAD]
            p = jnp.exp(
                s_all[h * PAD : (h + 1) * PAD] * scale + b - lse[0, pl.ds(w * per + h, 1), :]
            )
            dp = dp_all[h * PAD : (h + 1) * PAD]
            inner = jnp.sum(dp * p, 0, keepdims=True)
            gs = (p * (dp - inner)).astype(BF16)
            gf = gs.astype(F32)
            if w == 0:
                sums[at, pl.ds(0, PAD)] = gf
            else:
                sums[at, pl.ds(0, PAD)] += gf
            p_parts.append(p.astype(BF16))
            g_parts.append(gs)
            dqs.append(dot(kt[h * dim : (h + 1) * dim], gs))
        dv_all = dot(jnp.concatenate(p_parts, 0), gb)
        dk_all = dot(jnp.concatenate(g_parts, 0), qb)
        dv_w = dv_all[:PAD]
        dk_w = dk_all[:PAD]
        for h in range(1, per):
            dv_w = jnp.where(masks[h], dv_all[h * PAD : (h + 1) * PAD], dv_w)
            dk_w = jnp.where(masks[h], dk_all[h * PAD : (h + 1) * PAD], dk_w)
        dq_w = (jnp.concatenate(dqs, 0).T * scale).astype(BF16)
        dv_w = dv_w.astype(BF16)
        dq[rows, :] = dq_w
        dk[rows, :] = (dk_w * scale).astype(BF16)
        dv[rows, :] = dv_w
        q_sum += jnp.sum(dq_w.astype(F32), 0, keepdims=True)
        v_sum += jnp.sum(dv_w.astype(F32), 0, keepdims=True)
    vec[...] = jnp.concatenate([q_sum, v_sum], 0)


def proj_body(att, w_own, w_oth, pb, stream0, g2, s2, stream1, second):
    rows, model = stream0.shape
    half = w_own.shape[0]

    @pl.loop(0, model // 256)
    def _(c):
        cols = pl.ds(pl.multiple_of(c * 256, 256), 256)
        value = dot(att[:, :half], w_own[:, cols]) + dot(att[:, half:], w_oth[:, cols])
        stream1[:, cols] = stream0[:, cols] + (value + pb[:, cols])

    def norm(r):
        x = stream1[r, :]
        mean, scale = stats(x, model)
        second[r, :] = ((x - mean) * scale * g2[...] + s2[...]).astype(BF16)

    row_loop(rows, 32, norm)


def mlp_body(
    t_ref, sec_own, sec_sib, cot_own, cot_oth, keep, s1, w1, b1, w2,
    wg1, wg2, gb1, gb2, feed, g2_sib, g2_own, d_out,
    gf, gft, sect, facc, gacc,
):
    t = t_ref[0]
    c = pl.program_id(0)
    rows, model = sec_own.shape
    half = model // 2

    @pl.when(c == 0)
    def _():
        own_cols = pl.ds(pl.multiple_of(t * half, half), half)
        oth_cols = pl.ds(pl.multiple_of((1 - t) * half, half), half)
        total = jnp.zeros((1, half), F32)
        for side, who in ((0, t), (1, 1 - t)):
            mine = cot_own[who].astype(F32) * keep[who]
            gf[side, :, own_cols] = mine.astype(BF16)
            gf[side, :, oth_cols] = (cot_oth[who].astype(F32) * keep[who]).astype(BF16)
            total += jnp.sum(mine, 0, keepdims=True)
        gb2[...] = total
        d_out[...] = gf[0]
        for side, sec in ((0, sec_own), (1, sec_sib)):

            @pl.loop(0, model // 128)
            def _(b):
                at = pl.ds(pl.multiple_of(b * 128, 128), 128)
                gft[side, at, :] = gf[side, :, at].T
                sect[side, at, :] = sec[:, at].T

        facc[...] = jnp.zeros_like(facc)
        gacc[...] = jnp.zeros_like(gacc)

    size = w1.shape[1]
    acts, ghs = [], []
    bias_sum = jnp.zeros((1, size), F32)
    for side, sec in ((0, sec_own), (1, sec_sib)):
        hidden = dot(sec[...], w1[...]) + b1[...]
        d_act = dot_nt(gf[side], w2[...])
        cdf = 0.5 * (1.0 + lax.erf(hidden * 0.7071067811865476))
        pdf = jnp.exp(hidden * hidden * -0.5) * 0.3989422804014327
        act = (hidden * cdf).astype(BF16)
        gh = (d_act * (cdf + hidden * pdf)).astype(BF16)
        bias_sum += jnp.sum(gh.astype(F32), 0, keepdims=True)
        facc[side] += dot(act, w2[...])
        gacc[side] += dot_nt(gh, w1[...])
        acts.append(act)
        ghs.append(gh)
    gb1[...] = bias_sum
    wg1[...] = (dot(sect[0], ghs[0]) + dot(sect[1], ghs[1])).astype(BF16)
    wg2[...] = (dot(gft[0], acts[0]) + dot(gft[1], acts[1])).astype(BF16)

    @pl.when(c == pl.num_programs(0) - 1)
    def _():
        own_cols = pl.ds(pl.multiple_of(t * half, half), half)
        oth_cols = pl.ds(pl.multiple_of((1 - t) * half, half), half)
        feed[0, t] = facc[0, :, own_cols] + s1[:, own_cols]
        feed[0, 1 - t] = facc[1, :, own_cols]
        feed[1, t] = facc[0, :, oth_cols] + s1[:, oth_cols]
        feed[1, 1 - t] = facc[1, :, oth_cols]
        g2_own[...] = gacc[0]
        g2_sib[...] = gacc[1].astype(BF16)


def norm_back(e, x, gain, width):
    mean, scale = stats(x, width)
    xhat = (x - mean) * scale
    scaled = e * gain
    first = jnp.sum(scaled, 1, keepdims=True) * (1.0 / width)
    cross = jnp.sum(scaled * xhat, 1, keepdims=True) * (1.0 / width)
    return scale * (scaled - first - xhat * cross), e * xhat


def norm2_back_body(
    g_own, g_recv, stream1, d_out, g2, w_own, w_oth, d_s1, g_att, g_attended, vec
):
    rows, model = g_own.shape
    half = w_own.shape[0]
    vec[...] = jnp.zeros_like(vec)

    def norm(r):
        e = g_own[r, :] + g_recv[r, :].astype(F32)
        dv, ex = norm_back(e, stream1[r, :], g2[...], model)
        d = d_out[r, :].astype(F32) + dv
        d_s1[r, :] = d
        low = d.astype(BF16)
        g_att[r, :] = low
        vec[0:1, :] += jnp.sum(ex, 0, keepdims=True)
        vec[1:2, :] += jnp.sum(e, 0, keepdims=True)
        vec[2:3, :] += jnp.sum(low.astype(F32), 0, keepdims=True)

    row_loop(rows, 32, norm)
    for side, w in enumerate((w_own, w_oth)):

        @pl.loop(0, half // 256)
        def _(c):
            src = pl.ds(pl.multiple_of(c * 256, 256), 256)
            dst = pl.ds(pl.multiple_of(side * half + c * 256, 256), 256)
            g_attended[:, dst] = dot_nt(g_att[...], w[src, :]).astype(BF16)


def norm1_back_body(dq, dk, dv, w_own, w_oth, stream0, d_s1, g1, d_s0, g_s0, vec, acc):
    rows, model = stream0.shape
    half = w_own.shape[2]
    vec[...] = jnp.zeros_like(vec)

    @pl.loop(0, model // 256)
    def _(c):
        at = pl.ds(pl.multiple_of(c * 256, 256), 256)
        value = jnp.zeros((rows, 256), F32)
        for s, d in enumerate((dq, dk, dv)):
            value += dot_nt(d[:, :half], w_own[s, at, :])
            value += dot_nt(d[:, half:], w_oth[s, at, :])
        acc[:, at] = value

    def norm(r):
        e = acc[r, :]
        d, ex = norm_back(e, stream0[r, :], g1[...], model)
        d = d_s1[r, :] + d
        d_s0[r, :] = d.astype(BF16)
        g_s0[r, :] = d.astype(BF16)
        vec[0:1, :] += jnp.sum(ex, 0, keepdims=True)
        vec[1:2, :] += jnp.sum(e, 0, keepdims=True)

    row_loop(rows, 32, norm)


def merge_back_body(t_ref, g_s0, w_own, w_oth, x_ref, mg, d_merged, vec, acc):
    t = t_ref[0]
    rows = g_s0.shape[0]
    half = w_own.shape[0]
    width = 2 * half
    vec[...] = jnp.zeros_like(vec)
    for side, w in enumerate((w_own, w_oth)):

        @pl.loop(0, half // 256)
        def _(c):
            at = pl.ds(pl.multiple_of(c * 256, 256), 256)
            acc[side, :, at] = dot_nt(g_s0[...], w[at, :])

    def norm(r):
        xs = [x_ref[t, r, :].astype(F32), x_ref[1 - t, r, :].astype(F32)]
        es = [acc[0, r, :], acc[1, r, :]]
        gains = [mg[t], mg[1 - t]]
        total = sum(jnp.sum(x, 1, keepdims=True) for x in xs)
        square = sum(jnp.sum(x * x, 1, keepdims=True) for x in xs)
        mean = total * (1.0 / width)
        scale = lax.rsqrt(square * (1.0 / width) - mean * mean + EPS)
        hats = [(x - mean) * scale for x in xs]
        scaled = [e * g for e, g in zip(es, gains)]
        first = sum(jnp.sum(s, 1, keepdims=True) for s in scaled) * (1.0 / width)
        cross = sum(jnp.sum(s * h, 1, keepdims=True) for s, h in zip(scaled, hats)) * (1.0 / width)
        for side, who in ((0, t), (1, 1 - t)):
            d_merged[who, r, :] = scale * (scaled[side] - first - hats[side] * cross)
            vec[2 * side : 2 * side + 1, :] += jnp.sum(es[side] * hats[side], 0, keepdims=True)
            vec[2 * side + 1 : 2 * side + 2, :] += jnp.sum(es[side], 0, keepdims=True)

    row_loop(rows, 16, norm)


def weight_grad_body(l_own, l_sib, r_own, r_sib, out, lt):
    for side, l in enumerate((l_own, l_sib)):

        @pl.loop(0, l.shape[1] // 128)
        def _(b):
            at = pl.ds(pl.multiple_of(b * 128, 128), 128)
            lt[side, at, :] = l[:, at].T

    @pl.loop(0, out.shape[1] // 256)
    def _(c):
        at = pl.ds(pl.multiple_of(c * 256, 256), 256)
        out[:, at] = (dot(lt[0], r_own[:, at]) + dot(lt[1], r_sib[:, at])).astype(BF16)


def weight_grad(l_own, l_sib, r_own, r_sib):
    rows, model = l_own.shape
    n = r_own.shape[1]
    return whole(
        weight_grad_body,
        shape((model, n), BF16),
        (l_own, l_sib, r_own, r_sib),
        [pltpu.VMEM((2, model, rows), BF16)],
        flops=4 * rows * model * n,
        nbytes=2 * (2 * rows * (model + n) + model * n),
    )


def swap(value):
    return lax.ppermute(value, "tp", [(0, 1), (1, 0)])


def take(value, index):
    return lax.dynamic_index_in_dim(value, index, 0, keepdims=False)


def win_sizes(count):
    side = 1
    while 4 * (side + 1) * (side + 1) <= count:
        side += 1
    return count // (side * side), side, side


def my_place(sizes):
    me = lax.axis_index("win")
    _, ny, nx = sizes
    return lax.div(me, ny * nx), lax.rem(lax.div(me, nx), ny), lax.rem(me, nx)


def wins_along(sizes, place, axis):
    z, y, x = place
    strides = (sizes[1] * sizes[2], sizes[2], 1)
    base = z * strides[0] + y * strides[1] + x
    found = []
    for d in range(1, sizes[axis]):
        c = lax.rem(place[axis] + d, sizes[axis])
        found.append((d, c, base + (c - place[axis]) * strides[axis]))
    return found


def enter(sizes, place):
    barrier = pltpu.get_barrier_semaphore()
    tp = lax.axis_index("tp")
    peers = [(lax.axis_index("win"), 1 - tp)]
    for axis in range(3):
        peers += [(w, tp) for _, _, w in wins_along(sizes, place, axis)]
    for peer in peers:
        pl.semaphore_signal(barrier, inc=1, device_id=peer, device_id_type=MESH)
    pl.semaphore_wait(barrier, len(peers))


class Scatter:
    def __init__(self, sizes, place, order, src, bufs, sends, recvs, unit):
        self.sizes, self.place, self.order = sizes, place, order
        self.src, self.bufs, self.sends, self.recvs, self.unit = src, bufs, sends, recvs, unit

    def pick(self, step, c):
        if step == 0:
            return self.src.at[:, :, c] if self.order[0] == 2 else self.src.at[:, c]
        before = self.bufs[step - 1].at[0]
        if step == 1:
            return before.at[:, c]
        return before.at[c]

    def copies(self, step):
        axis = self.order[step]
        tp = lax.axis_index("tp")
        made = []
        for d, c, w in wins_along(self.sizes, self.place, axis):
            made.append(
                pltpu.make_async_remote_copy(
                    src_ref=self.pick(step, c),
                    dst_ref=self.bufs[step].at[d - 1],
                    send_sem=self.sends.at[self.unit, step, d - 1],
                    recv_sem=self.recvs.at[self.unit, step, d - 1],
                    device_id=(w, tp),
                    device_id_type=MESH,
                )
            )
        return made

    def start(self, step):
        for copy in self.copies(step):
            copy.start()

    def wait_sent(self, step):
        for copy in self.copies(step):
            copy.wait_send()

    def finish(self, step, out=None):
        copies = self.copies(step)
        for copy in copies:
            copy.wait_recv()
        mine = self.pick(step, self.place[self.order[step]])
        buf = self.bufs[step]
        lead = mine.shape[:-2]
        rows, n = mine.shape[-2:]
        width = min(n, 512)
        if step == 2:
            for b in range(n // width):
                at = pl.ds(b * width, width)
                total = mine[:, at].astype(F32)
                for d in range(len(copies)):
                    total += buf[d, :, at].astype(F32)
                out[:, at] = total
            return
        count = 1
        for size in lead:
            count *= size

        @pl.loop(0, count)
        def _(i):
            where = (i,) if len(lead) == 1 else (lax.div(i, lead[1]), lax.rem(i, lead[1]))
            for b in range(n // width):
                at = pl.ds(b * width, width)
                total = mine[(*where, slice(None), at)].astype(F32)
                for d in range(len(copies)):
                    total += buf[(d, *where, slice(None), at)].astype(F32)
                buf[(0, *where, slice(None), at)] = total.astype(BF16)


def scatter_buffers(sizes, order, rows, n):
    left = [0, 1, 2]
    shapes = []
    for axis in order:
        left.remove(axis)
        shapes.append(
            pltpu.VMEM((sizes[axis] - 1, *[sizes[a] for a in left], rows, n), BF16)
        )
    return shapes


X_FIRST, Y_FIRST = (2, 1, 0), (1, 2, 0)


def all_sum(sizes, place, src, bufs, sends, recvs):
    tp = lax.axis_index("tp")
    for step, axis in enumerate((2, 1, 0)):
        copies = []
        for d, c, w in wins_along(sizes, place, axis):
            copies.append(
                pltpu.make_async_remote_copy(
                    src_ref=src.at[step],
                    dst_ref=bufs.at[step, d - 1],
                    send_sem=sends.at[step, d - 1],
                    recv_sem=recvs.at[step, d - 1],
                    device_id=(w, tp),
                    device_id_type=MESH,
                )
            )
        for copy in copies:
            copy.start()
        total = src[step]
        for d, copy in enumerate(copies):
            copy.wait()
            total += bufs[step, d]
        src[step + 1] = total


def sums_body(sizes, orders, n_units, *refs):
    srcs, vec = refs[:n_units], refs[n_units]
    outs, vec_out = refs[n_units + 1 : 2 * n_units + 1], refs[2 * n_units + 1]
    scratch = refs[2 * n_units + 2 :]
    bufs = [scratch[3 * u : 3 * u + 3] for u in range(n_units)]
    sends, recvs, vsrc, vbuf, vsends, vrecvs = scratch[3 * n_units :]
    place = my_place(sizes)
    enter(sizes, place)
    units = [
        Scatter(sizes, place, orders[u], srcs[u], bufs[u], sends, recvs, u)
        for u in range(n_units)
    ]
    for unit in units:
        unit.start(0)
    for unit in units:
        unit.finish(0)
        unit.start(1)
    vsrc[0] = vec[...]
    all_sum(sizes, place, vsrc, vbuf, vsends, vrecvs)
    vec_out[...] = vsrc[3]
    for unit in units:
        unit.finish(1)
        unit.start(2)
    for unit, out in zip(units, outs):
        unit.finish(2, out)
    for unit in units:
        for step in range(3):
            unit.wait_sent(step)


def sums_over_win(count, units, vec):
    sizes = win_sizes(count)
    rows = units[0][0].shape[0] // count
    most = max(sizes) - 1
    scratch = []
    for value, order in units:
        scratch += scatter_buffers(sizes, order, rows, value.shape[1])
    dma = pltpu.SemaphoreType.DMA
    scratch += [
        dma((len(units), 3, most)), dma((len(units), 3, most)),
        pltpu.VMEM((4, *vec.shape), F32), pltpu.VMEM((3, most, *vec.shape), F32),
        dma((3, most)), dma((3, most)),
    ]

    def body(*refs):
        sums_body(sizes, [order for _, order in units], len(units), *refs)

    ins = [value.reshape(*sizes, rows, value.shape[1]) for value, _ in units] + [vec]
    outs = [shape((rows, value.shape[1])) for value, _ in units] + [shape(vec.shape)]
    return pl.pallas_call(
        body,
        out_shape=outs,
        in_specs=[VMEM] * len(ins),
        out_specs=[VMEM] * len(outs),
        scratch_shapes=scratch,
        compiler_params=pltpu.CompilerParams(
            vmem_limit_bytes=LIMIT, collective_id=1, has_side_effects=True
        ),
    )(*ins)


def solution(mesh):
    count = mesh.shape["win"]

    def shards(
        pixels, merge_gain, merge_shift, merge_weight, norm1_gain, norm1_shift, qkv_weight,
        qkv_bias, rel_table, proj_weight, proj_bias, norm2_gain, norm2_shift, fc1_weight,
        fc1_bias, fc2_weight, fc2_bias, rel_index, keep, cotangent,
    ):
        t = lax.axis_index("tp")
        t_arr = t.reshape(1).astype(jnp.int32)
        wins, height, _, channels = pixels.shape
        side = height // 2
        area = side * side
        rows = wins * PAD
        model = merge_weight.shape[1]
        half = model // 2
        heads_here = rel_table.shape[1]
        heads = 2 * heads_here
        dim = half // heads_here
        entries = rel_table.shape[0]
        slots = -(-entries // 128) * 128
        hidden = fc1_weight.shape[1]

        def pair(own, oth):
            return jnp.where(
                t == 0, jnp.concatenate([own, oth], -1), jnp.concatenate([oth, own], -1)
            )

        flat = [
            merge_gain, merge_shift, norm1_gain, norm1_shift, qkv_bias, rel_table.T,
            proj_bias, norm2_gain, norm2_shift,
        ]
        packed = jnp.concatenate([f.reshape(-1) for f in flat])
        got = swap(packed)
        others, at = [], 0
        for f in flat:
            others.append(got[at : at + f.size].reshape(f.shape))
            at += f.size
        wm_oth = swap(merge_weight)
        wqkv = qkv_weight.transpose(1, 0, 2)
        wqkv_oth = swap(wqkv)
        wp_oth = swap(proj_weight)
        mg = pair(merge_gain, others[0]).reshape(2, 1, model)
        ms = pair(merge_shift, others[1]).reshape(2, 1, model)
        g1 = pair(norm1_gain, others[2]).reshape(1, model)
        s1 = pair(norm1_shift, others[3]).reshape(1, model)
        qb = jnp.concatenate([qkv_bias, others[4]], -1)
        qb = jnp.stack([qb[0], jnp.zeros_like(qb[0]), qb[1]]).reshape(3, 1, model)
        pb = pair(proj_bias, others[6]).reshape(1, model)
        g2 = pair(norm2_gain, others[7]).reshape(1, model)
        s2 = pair(norm2_shift, others[8]).reshape(1, model)
        table = jnp.concatenate([rel_table.T, others[5].reshape(rel_table.T.shape)], 0)
        table = jnp.pad(table, ((0, 0), (0, slots - entries)))
        top = table.astype(BF16)
        table2 = jnp.concatenate([top, (table - top.astype(F32)).astype(BF16)], 0)

        x = (
            pixels.reshape(wins, side, 2, side, 2, channels)
            .transpose(4, 0, 1, 3, 2, 5)
            .reshape(2, wins, area, model)
        )
        x = jnp.pad(x, ((0, 0), (0, 0), (0, PAD - area), (0, 0))).reshape(2, rows, model)
        stream0, mn_own, mn_oth, first = whole(
            merge_body,
            (shape((rows, model)), shape((rows, model), BF16), shape((rows, model), BF16),
             shape((rows, model), BF16)),
            (t_arr, x, merge_weight, wm_oth, mg, ms, g1, s1),
            flops=4 * rows * model * model, nbytes=1e7, smem_first=True,
        )
        first_sib = swap(first)
        mn_sib = swap(mn_oth)
        qkv = whole(
            qkv_body, shape((3, rows, model), BF16), (first, wqkv, wqkv_oth, qb),
            flops=6 * rows * model * model, nbytes=1e7,
        )
        index_t = jnp.pad(rel_index.T, ((0, 0), (0, PAD - area)))
        bias = whole(
            bias_body, shape((PAD * heads, PAD)), (index_t, table2),
            flops=4 * heads * slots * area * 128, nbytes=2e6,
        )
        groups = model // 128
        per = 128 // dim
        lanes = pl.BlockSpec((rows, 128), lambda g: (0, g))

        def slot(s):
            return pl.BlockSpec((None, rows, 128), lambda g: (s, 0, g))

        lse_spec = pl.BlockSpec((1, wins * per, PAD), lambda g: (g, 0, 0))

        def attention(*refs):
            attention_body(dim, heads, *refs)

        attended, lse = call(
            attention,
            (shape((rows, model), BF16), shape((groups, wins * per, PAD))),
            (qkv, qkv, qkv, bias),
            flops=4 * rows * model * 448, nbytes=6e6,
            grid=(groups,),
            in_specs=[slot(0), slot(1), slot(2), VMEM],
            out_specs=(lanes, lse_spec),
        )
        att_sib = swap(attended[:, half:])
        stream1, second = whole(
            proj_body, (shape((rows, model)), shape((rows, model), BF16)),
            (attended, proj_weight, wp_oth, pb, stream0, g2, s2),
            flops=2 * rows * model * model, nbytes=8e6,
        )
        second_sib = swap(second)
        cot = jnp.pad(
            cotangent.reshape(2 * wins, area, half), ((0, 0), (0, PAD - area), (0, 0))
        ).reshape(2, rows, half)
        cot_oth = swap(cot)
        keep_rows = jnp.pad(
            keep.astype(F32).reshape(2 * wins, area), ((0, 0), (0, PAD - area))
        ).reshape(2, rows, 1)
        chunk = 512
        col_spec = pl.BlockSpec((model, chunk), lambda c: (0, c))
        row_spec = pl.BlockSpec((1, chunk), lambda c: (0, c))
        wg1, wg2, gb1, gb2, feed, g2_send, g2_own, d_out = call(
            mlp_body,
            (
                shape((model, hidden), BF16), shape((model, hidden), BF16), shape((1, hidden)),
                shape((1, half)), shape((2, 2, rows, half)), shape((rows, model), BF16),
                shape((rows, model)), shape((rows, model), BF16),
            ),
            (t_arr, second, second_sib, cot, cot_oth, keep_rows, stream1, fc1_weight,
             fc1_bias.reshape(1, hidden), fc2_weight),
            [
                pltpu.VMEM((2, rows, model), BF16), pltpu.VMEM((2, model, rows), BF16),
                pltpu.VMEM((2, model, rows), BF16), pltpu.VMEM((2, rows, model), F32),
                pltpu.VMEM((2, rows, model), F32),
            ],
            flops=24 * rows * model * hidden, nbytes=3e7,
            grid=(hidden // chunk,),
            in_specs=[SMEM, VMEM, VMEM, VMEM, VMEM, VMEM, VMEM, col_spec, row_spec,
                      pl.BlockSpec((chunk, model), lambda c: (c, 0))],
            out_specs=(col_spec, col_spec, row_spec, VMEM, VMEM, VMEM, VMEM, VMEM),
        )
        g2_recv = swap(g2_send)
        feed_recv = swap(feed[1].astype(BF16))
        out = keep_rows * (feed[0] + feed_recv.astype(F32) + fc2_bias)
        out = out.reshape(2 * wins, PAD, half)[:, :area].reshape(2 * wins * area, half).astype(BF16)

        d_s1, g_att, g_attended, vec2 = whole(
            norm2_back_body,
            (shape((rows, model)), shape((rows, model), BF16), shape((rows, model), BF16),
             shape((3, model))),
            (g2_own, g2_recv, stream1, d_out, g2, proj_weight, wp_oth),
            flops=2 * rows * model * model, nbytes=1e7,
        )
        g_att_sib = swap(g_att)

        def attention_back(*refs):
            attention_back_body(dim, heads, *refs)

        dq, dk, dv, sums, qkv_sums = call(
            attention_back,
            (
                shape((rows, model), BF16), shape((rows, model), BF16), shape((rows, model), BF16),
                shape((PAD * heads, PAD)), shape((2, model)),
            ),
            (qkv, qkv, qkv, g_attended, bias, lse),
            flops=10 * rows * model * 448, nbytes=1e7,
            grid=(groups,),
            in_specs=[slot(0), slot(1), slot(2), lanes, VMEM, lse_spec],
            out_specs=(lanes, lanes, lanes, VMEM, pl.BlockSpec((2, 128), lambda g: (0, g))),
        )
        proj_part = weight_grad(g_att, g_att_sib, attended[:, :half], att_sib)
        d_qkv = jnp.concatenate([dq[:, :half], dk[:, :half], dv[:, :half]], 1)
        d_qkv_sib = swap(jnp.concatenate([dq[:, half:], dk[:, half:], dv[:, half:]], 1))
        qkv_part = weight_grad(first, first_sib, d_qkv, d_qkv_sib)
        d_s0, g_s0, vec1 = whole(
            norm1_back_body,
            (shape((rows, model), BF16), shape((rows, model), BF16), shape((2, model))),
            (dq, dk, dv, wqkv, wqkv_oth, stream0, d_s1, g1),
            [pltpu.VMEM((rows, model), F32)],
            flops=6 * rows * model * model, nbytes=1e7,
        )
        g_s0_sib = swap(g_s0)
        rel_sums = whole(
            rel_body, shape((heads, slots)), (index_t, sums),
            flops=4 * heads * slots * area * 128, nbytes=2e6,
        )
        merge_part = weight_grad(g_s0, g_s0_sib, mn_own, mn_sib)
        d_merged, vec0 = whole(
            merge_back_body,
            (shape((2, rows, model)), shape((4, model))),
            (t_arr, g_s0, merge_weight, wm_oth, x, mg),
            [pltpu.VMEM((2, rows, model), F32)],
            flops=4 * rows * model * model, nbytes=1e7, smem_first=True,
        )
        pixels_grad = (
            d_merged.reshape(2, wins, PAD, 2, channels)[:, :, :area]
            .reshape(2, wins, side, side, 2, channels)
            .transpose(1, 2, 4, 3, 0, 5)
            .reshape(pixels.shape)
        )
        def sides(v):
            both = jnp.stack([v[..., :half], v[..., half:]])
            return take(both, t), take(both, 1 - t)

        n2, n1 = sides(vec2), sides(vec1)
        rel = rel_sums[:, :entries]
        keepers = [
            vec0[0:2], n1[0], qkv_sums[:, :half], rel[:heads_here], n2[0]
        ]
        leavers = [
            vec0[2:4], n1[1], qkv_sums[:, half:], rel[heads_here:], n2[1]
        ]
        back = swap(jnp.concatenate([v.reshape(-1) for v in leavers]))
        mine = jnp.concatenate([v.reshape(-1) for v in keepers]) + back
        vector = jnp.concatenate([mine, gb1.reshape(-1), gb2.reshape(-1)])
        vector = jnp.pad(vector, (0, -vector.size % 1024)).reshape(-1, 128)
        units = [(wg1, X_FIRST), (wg2, Y_FIRST), (qkv_part, X_FIRST), (proj_part, Y_FIRST),
                 (merge_part, Y_FIRST)]
        fc1_grad, fc2_grad, qkv_grad, proj_grad, merge_grad, vectors = sums_over_win(
            count, units, vector
        )
        vectors = vectors.reshape(-1)
        fc2_grad, proj_grad, merge_grad = fc2_grad.T, proj_grad.T, merge_grad.T
        qkv_grad = qkv_grad.reshape(-1, 3, half)
        parts, at = [], 0
        for v in keepers + [gb1, gb2]:
            parts.append(vectors[at : at + v.size].reshape(v.shape))
            at += v.size
        v0, v1, vq, vr, v2, vb1, vb2 = parts
        return (
            out, pixels_grad, v0[0], v0[1], merge_grad, v1[0], v1[1], qkv_grad, vq, vr.T,
            proj_grad, v2[2], v2[0], v2[1], fc1_grad, vb1[0], fc2_grad, vb2[0],
        )

    in_specs = (
        P(("win", "tp"), None, None, None), P("tp"), P("tp"), P("tp", None), P("tp"), P("tp"),
        P(None, None, "tp"), P(None, "tp"), P(None, "tp"), P("tp", None), P("tp"), P("tp"),
        P("tp"), P(None, "tp"), P("tp"), P("tp", None), P("tp"), P(), P("win"), P("win", "tp"),
    )
    out_specs = (
        P("win", "tp"), P(("win", "tp"), None, None, None), P("tp"), P("tp"), P("tp", "win"),
        P("tp"), P("tp"), P("win", None, "tp"), P(None, "tp"), P(None, "tp"), P("tp", "win"),
        P("tp"), P("tp"), P("tp"), P("win", "tp"), P("tp"), P("tp", "win"), P("tp"),
    )
    return jax.shard_map(shards, mesh=mesh, in_specs=in_specs, out_specs=out_specs, check_vma=False)
```

```python
from types import SimpleNamespace

import jax
import jax.numpy as jnp
from jax import lax
from jax.experimental import pallas as pl
from jax.experimental.pallas import tpu as pltpu
from jax.sharding import PartitionSpec as P

EPS = 1e-05
F32 = jnp.float32
BF16 = jnp.bfloat16
MESH = pl.DeviceIdType.MESH
PAD = 112
LIMIT = 63 * 1024 * 1024


def shape(dims, dtype=F32):
    return jax.ShapeDtypeStruct(tuple(dims), dtype)


def kernel_call(body, small, large, outs, scratch, large_outs, collective=None):
    names = [*small, *large, *outs, *scratch]
    free, vmem = pl.BlockSpec(memory_space=pl.ANY), pl.BlockSpec(memory_space=pltpu.VMEM)
    more = {} if collective is None else dict(collective_id=collective, has_side_effects=True)

    def run(*refs):
        body(SimpleNamespace(**dict(zip(names, refs, strict=True))))

    results = pl.pallas_call(
        run,
        out_shape=tuple(outs.values()),
        in_specs=[vmem] * len(small) + [free] * len(large),
        out_specs=tuple(free if n in large_outs else vmem for n in outs),
        scratch_shapes=list(scratch.values()),
        compiler_params=pltpu.CompilerParams(vmem_limit_bytes=LIMIT, **more),
    )(*small.values(), *large.values())
    return SimpleNamespace(**dict(zip(outs, results)))


def dot(a, b):
    return jnp.dot(a, b, preferred_element_type=F32)


def dot_nt(a, b):
    return lax.dot_general(a, b, (((1,), (1,)), ((), ())), preferred_element_type=F32)


def dot_tn(a, b):
    return lax.dot_general(a, b, (((0,), (0,)), ((), ())), preferred_element_type=F32)


def stats(x, width):
    mean = jnp.sum(x, 1, keepdims=True) * (1.0 / width)
    second = jnp.sum(x * x, 1, keepdims=True) * (1.0 / width)
    return mean, lax.rsqrt(second - mean * mean + EPS)


def norm_back(e, x, gain, width):
    mean, scale = stats(x, width)
    xhat = (x - mean) * scale
    scaled = e * gain
    first = jnp.sum(scaled, 1, keepdims=True) * (1.0 / width)
    cross = jnp.sum(scaled * xhat, 1, keepdims=True) * (1.0 / width)
    return scale * (scaled - first - xhat * cross), e * xhat


def steps(total, size, fn):
    @pl.loop(0, total // size)
    def _(step):
        fn(pl.ds(pl.multiple_of(step * size, size), size))


def add_to(ref, row, value):
    ref[row : row + 1, :] += jnp.sum(value, 0, keepdims=True)


def spread(rows, tokens, windows):
    row = lax.broadcasted_iota(jnp.int32, (rows, tokens), 0)
    col = lax.broadcasted_iota(jnp.int32, (rows, tokens), 1)
    area = tokens // windows
    w = row // PAD
    k = row - w * PAD
    real = k < area
    return (
        jnp.logical_and(real, w * area + k == col),
        jnp.logical_and(real, k * windows + w == col),
    )


def gather_rows(rows, tokens, windows):
    row = lax.broadcasted_iota(jnp.int32, (tokens, rows), 1)
    col = lax.broadcasted_iota(jnp.int32, (tokens, rows), 0)
    area = tokens // windows
    w = row // PAD
    k = row - w * PAD
    real = k < area
    return (
        jnp.logical_and(real, w * area + k == col),
        jnp.logical_and(real, k * windows + w == col),
    )


def ones(mask):
    return jnp.where(mask, 1.0, 0.0).astype(BF16)


class Link:
    def __init__(self, sends, recvs):
        self.sends, self.recvs = sends, recvs

    def copy(self, k, src, dst):
        return pltpu.make_async_remote_copy(
            src_ref=src,
            dst_ref=dst,
            send_sem=self.sends.at[k],
            recv_sem=self.recvs.at[k],
            device_id=(lax.axis_index("win"), 1 - lax.axis_index("tp")),
            device_id_type=MESH,
        )


def head_masks(rows, width, dim):
    lane = lax.broadcasted_iota(jnp.int32, (rows, width), 1) // dim
    return [lane == h for h in range(width // dim)]


def stacked(block, masks):
    return jnp.concatenate([jnp.where(m, block, 0.0).astype(BF16) for m in masks], 0)


def diagonal(a, b):
    zero = jnp.zeros((PAD, 128), BF16)
    rest = jnp.zeros((128 - PAD, 256), BF16)
    return jnp.concatenate(
        [jnp.concatenate([a, zero], 1), rest, jnp.concatenate([zero, b], 1), rest], 0
    )


def bias_of(bias, heads, g, per):
    return [bias[pl.ds(g * per + h, PAD, stride=heads), :] for h in range(per)]


def attention_forward(dim, heads, g, r):
    per = 128 // dim
    windows = r.qkvb.shape[1] // PAD
    scale = dim ** (-0.5)
    masks = head_masks(PAD, 128, dim)
    lanes = pl.ds(pl.multiple_of(g * 128, 128), 128)
    bias = bias_of(r.biasb, heads, g, per)
    done, sums = [], []
    for w in range(0, windows, 2):
        at = [pl.ds((w + u) * PAD, PAD) for u in range(2)]
        q, k, v = ([r.qkvb[s, a, lanes] for a in at] for s in range(3))
        both = dot_nt(
            jnp.concatenate([stacked(k[0], masks), stacked(k[1], masks)], 1),
            diagonal(q[0], q[1]),
        )
        for u in range(2):
            vt = v[u].T
            parts = []
            for h in range(per):
                s = both[h * PAD : (h + 1) * PAD, u * 128 : (u + 1) * 128] * scale + bias[h]
                top = jnp.max(s, 0, keepdims=True)
                e = jnp.exp(s - top)
                total = jnp.sum(e, 0, keepdims=True)
                p = (e * (1.0 / total)).astype(BF16)
                sums.append(top + jnp.log(total))
                parts.append(dot(vt[h * dim : (h + 1) * dim], p))
            done.append(jnp.concatenate(parts, 0).T[:PAD].astype(BF16))
    for w in range(windows):
        r.attb[pl.ds(w * PAD, PAD), lanes] = done[w]
    r.lse[g] = jnp.concatenate(sums, 0)


def attention_back(dim, heads, g, r):
    per = 128 // dim
    windows = r.qkvb.shape[1] // PAD
    scale = dim ** (-0.5)
    masks = head_masks(PAD, 128, dim)
    lanes = pl.ds(pl.multiple_of(g * 128, 128), 128)
    bias = bias_of(r.biasb, heads, g, per)
    totals, done = [None] * per, []
    for w in range(windows):
        at = pl.ds(w * PAD, PAD)
        q, k, v = r.qkvb[0, at, lanes], r.qkvb[1, at, lanes], r.qkvb[2, at, lanes]
        go = r.ex[0, at, lanes]
        both = dot_nt(
            jnp.concatenate([stacked(k, masks), stacked(v, masks)], 1), diagonal(q, go)
        )
        kt = k.T
        p_parts, g_parts, dqs = [], [], []
        for h in range(per):
            here = slice(h * PAD, (h + 1) * PAD)
            p = jnp.exp(
                both[here, :128] * scale + bias[h] - r.lse[g, pl.ds(w * per + h, 1), :]
            )
            dp = both[here, 128:]
            gs = (p * (dp - jnp.sum(dp * p, 0, keepdims=True))).astype(BF16)
            wide = gs.astype(F32)
            totals[h] = wide if w == 0 else totals[h] + wide
            p_parts.append(p.astype(BF16))
            g_parts.append(gs)
            dqs.append(dot(kt[h * dim : (h + 1) * dim], gs))
        back = dot(
            jnp.concatenate([jnp.concatenate(p_parts, 0), jnp.concatenate(g_parts, 0)], 1),
            diagonal(go, q),
        )
        dv, dk = back[:PAD, :128], back[:PAD, 128:]
        for h in range(1, per):
            here = slice(h * PAD, (h + 1) * PAD)
            dv = jnp.where(masks[h], back[here, :128], dv)
            dk = jnp.where(masks[h], back[here, 128:], dk)
        dq = jnp.concatenate(dqs, 0).T[:PAD] * scale
        done.append((dq.astype(BF16), (dk * scale).astype(BF16), dv.astype(BF16)))
    q_sum = jnp.zeros((1, 128), F32)
    v_sum = jnp.zeros((1, 128), F32)
    for w in range(windows):
        for s in range(3):
            r.qkvb[s, pl.ds(w * PAD, PAD), lanes] = done[w][s]
        q_sum += jnp.sum(done[w][0].astype(F32), 0, keepdims=True)
        v_sum += jnp.sum(done[w][2].astype(F32), 0, keepdims=True)
    for h in range(per):
        r.sums[pl.ds(g * per + h, PAD, stride=heads), :] = totals[h]
    r.vq[0:1, lanes] = q_sum
    r.vq[1:2, lanes] = v_sum


PAIRS = 4


def onehot_of(index, first, entries):
    rows = [index[pl.ds(first + u, 1), :] for u in range(PAIRS)]
    ids = lax.broadcasted_iota(jnp.int32, (entries, rows[0].shape[1]), 0)
    return jnp.concatenate([ones(ids == row) for row in rows], 1)


def bias_spread(area, heads, table, index, out):
    entries = table.shape[1]
    top = table.astype(BF16)
    both = jnp.concatenate([top, (table - top.astype(F32)).astype(BF16)], 0)

    @pl.loop(0, area // PAIRS)
    def _(i):
        value = dot(both, onehot_of(index, i * PAIRS, entries))
        value = value[:heads] + value[heads:]
        for u in range(PAIRS):
            at = pl.ds(pl.multiple_of((i * PAIRS + u) * heads, heads), heads)
            out[at, :] = value[:, u * 128 : (u + 1) * 128]

    out[pl.ds(area * heads, (PAD - area) * heads), :] = jnp.full(
        ((PAD - area) * heads, out.shape[1]), -1e30, F32
    )


def rel_sum(area, heads, index, sums, rel):
    entries = rel.shape[1]
    rel[...] = jnp.zeros_like(rel)

    @pl.loop(0, area // PAIRS)
    def _(i):
        hot = onehot_of(index, i * PAIRS, entries)
        s = jnp.concatenate(
            [
                sums[pl.ds(pl.multiple_of((i * PAIRS + u) * heads, heads), heads), :]
                for u in range(PAIRS)
            ],
            1,
        )
        top = s.astype(BF16)
        low = (s - top.astype(F32)).astype(BF16)
        both = dot_nt(jnp.concatenate([top, low], 0), hot)
        rel[...] += both[:heads] + both[heads:]


def win_sizes(count):
    side = 1
    while 4 * (side + 1) * (side + 1) <= count:
        side += 1
    return count // (side * side), side, side


def my_place(sizes):
    me = lax.axis_index("win")
    _, ny, nx = sizes
    return lax.div(me, ny * nx), lax.rem(lax.div(me, nx), ny), lax.rem(me, nx)


def wins_along(sizes, place, axis):
    z, y, x = place
    strides = (sizes[1] * sizes[2], sizes[2], 1)
    base = z * strides[0] + y * strides[1] + x
    found = []
    for d in range(1, sizes[axis]):
        c = lax.rem(place[axis] + d, sizes[axis])
        found.append((d, c, base + (c - place[axis]) * strides[axis]))
    return found


def enter(sizes=None, place=None):
    barrier = pltpu.get_barrier_semaphore()
    tp = lax.axis_index("tp")
    peers = [(lax.axis_index("win"), 1 - tp)]
    if sizes is not None:
        for axis in range(3):
            peers += [(w, tp) for _, _, w in wins_along(sizes, place, axis)]
    for peer in peers:
        pl.semaphore_signal(barrier, inc=1, device_id=peer, device_id_type=MESH)
    pl.semaphore_wait(barrier, len(peers))


class Scatter:
    def __init__(self, sizes, place, order, src, bufs, sends, recvs, unit):
        self.sizes, self.place, self.order = sizes, place, order
        self.src, self.bufs, self.sends, self.recvs, self.unit = src, bufs, sends, recvs, unit

    def pick(self, step, c):
        if step == 0:
            return self.src.at[:, :, c] if self.order[0] == 2 else self.src.at[:, c]
        before = self.bufs[step - 1].at[0]
        if step == 1:
            return before.at[:, c]
        return before.at[c]

    def copies(self, step):
        axis = self.order[step]
        tp = lax.axis_index("tp")
        made = []
        for d, c, w in wins_along(self.sizes, self.place, axis):
            made.append(
                pltpu.make_async_remote_copy(
                    src_ref=self.pick(step, c),
                    dst_ref=self.bufs[step].at[d - 1],
                    send_sem=self.sends.at[self.unit, step, d - 1],
                    recv_sem=self.recvs.at[self.unit, step, d - 1],
                    device_id=(w, tp),
                    device_id_type=MESH,
                )
            )
        return made

    def start(self, step):
        for copy in self.copies(step):
            copy.start()

    def wait_sent(self, step):
        for copy in self.copies(step):
            copy.wait_send()

    def finish(self, step, out=None):
        copies = self.copies(step)
        for copy in copies:
            copy.wait_recv()
        mine = self.pick(step, self.place[self.order[step]])
        buf = self.bufs[step]
        lead = mine.shape[:-2]
        rows, n = mine.shape[-2:]
        width = min(n, 512)
        if step == 2:
            for b in range(n // width):
                at = pl.ds(b * width, width)
                total = mine[:, at].astype(F32)
                for d in range(len(copies)):
                    total += buf[d, :, at].astype(F32)
                out[:, at] = total
            return
        count = 1
        for size in lead:
            count *= size

        @pl.loop(0, count)
        def _(i):
            where = (i,) if len(lead) == 1 else (lax.div(i, lead[1]), lax.rem(i, lead[1]))
            for b in range(n // width):
                at = pl.ds(b * width, width)
                total = mine[(*where, slice(None), at)].astype(F32)
                for d in range(len(copies)):
                    total += buf[(d, *where, slice(None), at)].astype(F32)
                buf[(0, *where, slice(None), at)] = total.astype(BF16)


X_FIRST, Y_FIRST = (2, 1, 0), (1, 2, 0)


def all_sum(sizes, place, src, bufs, sends, recvs):
    tp = lax.axis_index("tp")
    for step, axis in enumerate((2, 1, 0)):
        copies = []
        for d, c, w in wins_along(sizes, place, axis):
            copies.append(
                pltpu.make_async_remote_copy(
                    src_ref=src.at[step],
                    dst_ref=bufs.at[step, d - 1],
                    send_sem=sends.at[step, d - 1],
                    recv_sem=recvs.at[step, d - 1],
                    device_id=(w, tp),
                    device_id_type=MESH,
                )
            )
        for copy in copies:
            copy.start()
        total = src[step]
        for d, copy in enumerate(copies):
            copy.wait()
            total += bufs[step, d]
        src[step + 1] = total


def front_body(dim, heads, area, r):
    enter()
    t = lax.axis_index("tp")
    who = (t, 1 - t)
    rows, model = r.firstb.shape
    half = model // 2
    windows = rows // PAD
    tokens = windows * area
    link = Link(r.xsend, r.xrecv)
    own_cols = pl.ds(pl.multiple_of(t * half, half), half)
    oth_cols = pl.ds(pl.multiple_of((1 - t) * half, half), half)

    def load(k, src, dst):
        return pltpu.make_async_copy(src, dst, r.lsem.at[k])

    c_wm = link.copy(0, r.wm, r.wmb.at[1])
    c_wm.start()
    loads = [load(k, r.pixels.at[:, k % 2, :, k // 2], r.pix.at[k]) for k in range(4)]
    loads += [load(4, r.cot, r.cotb.at[0]), load(5, r.wm, r.wmb.at[0])]
    for one in loads:
        one.start()
    vx = r.vx
    vx[0] = jnp.zeros(vx.shape[1:], F32)
    for k, ref in enumerate((r.mg, r.ms)):
        for j in range(2):
            vx[0, 2 * k + j : 2 * k + j + 1, :] = ref[:, j * half : (j + 1) * half]
    for k, ref in enumerate((r.n1g, r.n1s, r.pb, r.n2g, r.n2s)):
        vx[0, 4 + k : 5 + k, :] = ref[...]
    vx[0, 9:11, :] = r.qb[...]
    vx[0, 16 : 16 + heads // 2, 0 : r.table.shape[1]] = r.table[...]
    c_vec = link.copy(1, vx.at[0], vx.at[1])
    c_vec.start()
    c_cot = link.copy(2, r.cot, r.cotb.at[1])
    c_cot.start()
    c_wq = link.copy(3, r.wqkv, r.wqb.at[1])
    c_wq.start()
    c_wp = link.copy(4, r.wp, r.wpb.at[pl.ds(half, half), :])
    c_wp.start()
    late = [load(6, r.wqkv, r.wqb.at[0]), load(7, r.wp, r.wpb.at[pl.ds(0, half), :])]
    for one in late:
        one.start()
    stores = []

    def store(src, dst):
        one = pltpu.make_async_copy(src, dst, r.ssem.at[len(stores)])
        stores.append(one)
        one.start()

    token_rows, pixel_rows = spread(rows, tokens, windows)
    pixel_rows = ones(pixel_rows)
    for k in range(4):
        loads[k].wait()
        r.xb[k] = dot(
            pixel_rows, r.pix[k].astype(F32).reshape(tokens, half).astype(BF16)
        ).astype(BF16)
    store(r.xb, r.x)

    c_vec.wait()
    mgo, nat = r.mgo, r.nat
    for side in range(2):
        for j in range(2):
            mgo[side, :, j * half : (j + 1) * half] = vx[side, j : j + 1, :]
            r.mso[side, :, j * half : (j + 1) * half] = vx[side, 2 + j : 3 + j, :]
        nat[0:5, (own_cols, oth_cols)[side]] = vx[side, 4:9, :]
    width = 2 * model

    def norm0(at):
        xs = [
            [r.xb[2 * who[i] + j, at, :].astype(F32) for j in range(2)] for i in range(2)
        ]

        def both(fn):
            return sum(jnp.sum(fn(x), 1, keepdims=True) for pair in xs for x in pair)

        mean = both(lambda x: x) * (1.0 / width)
        scale = lax.rsqrt(both(lambda x: x * x) * (1.0 / width) - mean * mean + EPS)
        for i in range(2):
            for j in range(2):
                cols = pl.ds(j * half, half)
                value = (xs[i][j] - mean) * scale * mgo[i, :, cols] + r.mso[i, :, cols]
                r.mnb[i, at, cols] = value.astype(BF16)

    steps(rows, 64, norm0)
    c_mn = link.copy(6, r.mnb.at[1], r.mn_sib)
    c_mn.start()
    store(r.mnb.at[0], r.mn_own)

    entries = r.tableb.shape[1]
    for side in range(2):
        r.tableb[side * (heads // 2) : (side + 1) * (heads // 2), :] = vx[
            side, 16 : 16 + heads // 2, 0:entries
        ]
    bias_spread(area, heads, r.tableb[...], r.index, r.biasb)
    store(r.biasb, r.bias)

    loads[4].wait()
    c_cot.wait()
    total = jnp.zeros((1, half), F32)
    for side in range(2):
        at = pl.ds(pl.multiple_of(who[side] * tokens, tokens), tokens)
        pick = ones(jnp.logical_and(token_rows, r.keep[who[side]] > 0))
        mine = dot(pick, r.cotb[0, at, :])
        total += jnp.sum(mine, 0, keepdims=True)
        here = pl.ds(side * rows, rows)
        r.gfb[here, own_cols] = mine.astype(BF16)
        r.gfb[here, oth_cols] = dot(pick, r.cotb[1, at, :]).astype(BF16)
    r.gb2[...] = total
    store(r.gfb, r.gf)

    loads[5].wait()

    def own_part(at):
        r.s0b[:, at] = dot(r.mnb[0], r.wmb[0, :, at])

    steps(model, 512, own_part)
    c_wm.wait()
    store(r.wmb.at[1], r.wm_oth)

    def oth_part(at):
        r.s0b[:, at] += dot(r.mnb[1], r.wmb[1, :, at])

    steps(model, 512, oth_part)
    store(r.s0b, r.stream0)

    def norm1(at):
        x = r.s0b[at, :]
        mean, scale = stats(x, model)
        r.firstb[at, :] = ((x - mean) * scale * nat[0:1, :] + nat[1:2, :]).astype(BF16)

    steps(rows, 112, norm1)
    c_first = link.copy(5, r.firstb, r.first_sib)
    c_first.start()
    store(r.firstb, r.first_own)

    late[0].wait()
    for side in range(2):
        if side == 1:
            c_wq.wait()
            store(r.wqb.at[1], r.wqkv_oth)
        for s in range(3):
            cols = pl.ds(side * half, half)
            value = dot(r.firstb[...], r.wqb[side, s])
            if s != 1:
                value += vx[side, 9 + s // 2 : 10 + s // 2, :]
            r.qkvb[s, :, cols] = value.astype(BF16)
    store(r.qkvb, r.qkv)

    @pl.loop(0, model // 128)
    def _(g):
        attention_forward(dim, heads, g, r)

    c_att = link.copy(7, r.attb.at[:, pl.ds(half, half)], r.att_sib)
    c_att.start()
    store(r.attb.at[:, pl.ds(0, half)], r.att_own)

    late[1].wait()
    c_wp.wait()
    store(r.wpb.at[pl.ds(half, half), :], r.wp_oth)

    def project(at):
        value = dot(r.attb[...], r.wpb[:, at]) + nat[2:3, at]
        r.s1b[:, at] = r.s0b[:, at] + value

    steps(model, 512, project)
    store(r.s1b, r.stream1)

    def norm2(at):
        x = r.s1b[at, :]
        mean, scale = stats(x, model)
        r.secb[at, :] = ((x - mean) * scale * nat[3:4, :] + nat[4:5, :]).astype(BF16)

    steps(rows, 112, norm2)
    store(r.secb, r.second)
    for one in (c_mn, c_first, c_att):
        one.wait()
    for one in stores:
        one.wait()


def front(dim, heads, area, windows, small, large):
    rows, tokens = windows * PAD, windows * area
    model = large["wm"].shape[1]
    half = model // 2
    side = large["pixels"].shape[0:3:2]
    slots = -(-small["table"].shape[1] // 128) * 128
    vm, dma = pltpu.VMEM, pltpu.SemaphoreType.DMA
    big = dict(
        x=shape((4, rows, half), BF16), gf=shape((2 * rows, model), BF16),
        stream0=shape((rows, model)), stream1=shape((rows, model)),
        second=shape((rows, model), BF16), qkv=shape((3, rows, model), BF16),
        bias=shape((PAD * heads, 128)), first_own=shape((rows, model), BF16),
        first_sib=shape((rows, model), BF16), mn_own=shape((rows, model), BF16),
        mn_sib=shape((rows, model), BF16), att_own=shape((rows, half), BF16),
        att_sib=shape((rows, half), BF16), wm_oth=shape((model, model), BF16),
        wqkv_oth=shape((3, model, half), BF16), wp_oth=shape((half, model), BF16),
    )
    outs = dict(
        big, gb2=shape((1, half)), nat=shape((8, model)), mgo=shape((2, 1, model)),
        lse=shape((model // 128, windows * 128 // dim, 128)),
    )
    scratch = dict(
        wmb=vm((2, model, model), BF16), wqb=vm((2, 3, model, half), BF16),
        wpb=vm((model, model), BF16), pix=vm((4, *side, windows, half), BF16),
        xb=vm((4, rows, half), BF16), cotb=vm((2, 2 * tokens, half), BF16),
        gfb=vm((2 * rows, model), BF16), mnb=vm((2, rows, model), BF16),
        s0b=vm((rows, model), F32), s1b=vm((rows, model), F32), firstb=vm((rows, model), BF16),
        qkvb=vm((3, rows, model), BF16), biasb=vm((PAD * heads, 128), F32),
        attb=vm((rows, model), BF16), secb=vm((rows, model), BF16),
        vx=vm((2, 32, half), F32), mso=vm((2, 1, model), F32), tableb=vm((heads, slots), F32),
        lsem=dma((8,)), ssem=dma((16,)), xsend=dma((8,)), xrecv=dma((8,)),
    )

    def body(r):
        front_body(dim, heads, area, r)

    return kernel_call(body, small, large, outs, scratch, big, collective=2)


CHUNK = 512


def back_body(sizes, dim, heads, area, r):
    place = my_place(sizes)
    t = lax.axis_index("tp")
    who = (t, 1 - t)
    sec, gf, facc, gacc, st, ex = r.sec, r.gfb, r.facc, r.gacc, r.st, r.ex
    w1b, w2b, cotb, qkvb = r.w1b, r.w2b, r.cotb, r.qkvb
    rows, model = st.shape
    half = model // 2
    hidden = r.fc1.shape[1]
    chunks = hidden // CHUNK
    windows = rows // PAD
    tokens = windows * area
    mine, theirs = pl.ds(0, rows), pl.ds(rows, rows)
    left, right = pl.ds(0, half), pl.ds(half, half)
    link = Link(r.xsend, r.xrecv)
    own_cols = pl.ds(pl.multiple_of(t * half, half), half)
    oth_cols = pl.ds(pl.multiple_of((1 - t) * half, half), half)
    part = model // (sizes[0] * sizes[1] * sizes[2])

    def load(k, src, dst):
        return pltpu.make_async_copy(src, dst, r.lsem.at[k])

    def unit(u, order):
        slot = u % 8 if isinstance(u, int) else lax.rem(u, 8)
        bufs = [buf.at[u] for buf in (r.buf0, r.buf1, r.buf2)]
        return Scatter(sizes, place, order, r.src.at[slot], bufs, r.rsend, r.rrecv, u)

    def pair(k):
        return unit(2 * k, X_FIRST), unit(2 * k + 1, Y_FIRST)

    def finish(k, step):
        for one in pair(k):
            one.finish(step)
            one.start(step + 1)

    def put(slot, value):
        r.src[slot] = value.astype(BF16).reshape(*sizes, part, CHUNK)

    enter(sizes, place)
    c_sec = link.copy(0, r.second, sec.at[theirs])
    c_sec.start()
    loads = [
        load(0, r.second, sec.at[mine]), load(1, r.gf, gf), load(3, r.stream1, st),
        load(4, r.qkv, qkvb),
    ]
    for one in loads:
        one.start()

    def weights(c):
        slot = lax.rem(c, 2)
        cols = pl.ds(pl.multiple_of(c * CHUNK, CHUNK), CHUNK)
        return (
            pltpu.make_async_copy(r.fc1.at[:, cols], w1b.at[slot], r.wsem.at[0, slot]),
            pltpu.make_async_copy(r.fc2.at[cols, :], w2b.at[slot], r.wsem.at[1, slot]),
        )

    for one in weights(0):
        one.start()
    for one in loads[0:2]:
        one.wait()
    c_sec.wait()

    blocks = CHUNK // 128
    hid, dact, act, gh = r.sums, r.biasb, r.act, r.gh

    @pl.loop(0, chunks)
    def _(c):
        slot = lax.rem(c, 2)
        for one in weights(c):
            one.wait()

        @pl.when(c + 1 < chunks)
        def _():
            for one in weights(c + 1):
                one.start()

        of = pl.ds(pl.multiple_of(c * CHUNK, CHUNK), CHUNK)
        value = dot(sec[...], w1b[slot]) + r.b1[:, of]
        for b in range(blocks):
            hid[b * 2 * rows : (b + 1) * 2 * rows, :] = value[:, b * 128 : (b + 1) * 128]
        value = dot_nt(gf[...], w2b[slot])
        for b in range(blocks):
            dact[b * 2 * rows : (b + 1) * 2 * rows, :] = value[:, b * 128 : (b + 1) * 128]
        for b in range(blocks):
            lanes = pl.ds(b * 128, 128)

            def gelu(at):
                here = pl.ds(pl.multiple_of(b * 2 * rows + at.start, 128), at.size)
                x = hid[here, :]
                cdf = 0.5 * (1.0 + lax.erf(x * 0.7071067811865476))
                pdf = jnp.exp(x * x * -0.5) * 0.3989422804014327
                act[at, lanes] = (x * cdf).astype(BF16)
                gh[at, lanes] = (dact[here, :] * (cdf + x * pdf)).astype(BF16)

            steps(2 * rows, 128, gelu)
        r.gb1[:, of] = jnp.sum(gh[...].astype(F32), 0, keepdims=True)
        put(lax.rem(2 * c, 8), dot_tn(sec[...], gh[...]))
        unit(2 * c, X_FIRST).start(0)
        put(lax.rem(2 * c + 1, 8), dot_tn(gf[...], act[...]))
        unit(2 * c + 1, Y_FIRST).start(0)

        @pl.when(c == 0)
        def _():
            facc[...] = dot(act[...], w2b[slot])
            gacc[...] = dot_nt(gh[...], w1b[slot])

        @pl.when(c > 0)
        def _():
            facc[...] += dot(act[...], w2b[slot])
            gacc[...] += dot_nt(gh[...], w1b[slot])

        @pl.when(c >= 2)
        def _():
            finish(c - 2, 0)

    load(5, r.bias, r.biasb).start()
    for k, src in enumerate((r.wp_own, r.wp_oth)):
        load(8 + k, src, w2b.at[k]).start()
    ex[0] = gacc[theirs].astype(BF16)
    c_g2 = link.copy(1, ex.at[0], ex.at[1])
    c_g2.start()
    load(3, r.stream1, st).wait()
    fsend, fland = r.fsend, r.fland
    fsend[0] = facc[theirs, oth_cols].astype(BF16)
    fsend[1] = (facc[mine, oth_cols] + st[:, oth_cols]).astype(BF16)
    c_feed = link.copy(2, fsend, fland)
    c_feed.start()
    v2 = r.v2
    v2[...] = jnp.zeros_like(v2)
    c_g2.wait()

    def norm2(at):
        e = gacc[at, :] + ex[1, at, :].astype(F32)
        dv, hat = norm_back(e, st[at, :], r.nat[3:4, :], model)
        d = gf[at, :].astype(F32) + dv
        gacc[at, :] = d
        low = d.astype(BF16)
        sec[at, :] = low
        add_to(v2, 0, hat)
        add_to(v2, 1, e)
        add_to(v2, 2, low.astype(F32))

    steps(rows, 112, norm2)
    c_att = link.copy(3, sec.at[mine], sec.at[theirs])
    c_att.start()
    load(10, r.first_own, gf.at[mine]).start()
    load(11, r.first_sib, gf.at[theirs]).start()
    for k, src in enumerate((r.wp_own, r.wp_oth)):
        load(8 + k, src, w2b.at[k]).wait()
        ex[0, :, (left, right)[k]] = dot_nt(sec[mine, :], w2b[k]).astype(BF16)

    c_feed.wait()
    token_rows = gather_rows(rows, tokens, windows)[0]
    outs = []
    for side in range(2):
        value = facc[side * rows : (side + 1) * rows, own_cols] + fland[side].astype(F32)
        if side == 0:
            value += st[:, own_cols]
        pick = ones(jnp.logical_and(token_rows, r.keep[who[side]] > 0))
        fsend[side, 0:tokens, :] = dot(pick, (value + r.b2[...]).astype(BF16)).astype(BF16)
        at = pl.ds(pl.multiple_of(who[side] * tokens, tokens), tokens)
        outs.append(load(14 + side, fsend.at[side, pl.ds(0, tokens), :], r.out.at[at, :]))
        outs[-1].start()
    load(6, r.att_own, fland.at[0]).start()
    load(7, r.att_sib, fland.at[1]).start()
    load(12, r.stream0, st).start()

    load(4, r.qkv, qkvb).wait()
    load(5, r.bias, r.biasb).wait()

    @pl.loop(0, model // 128)
    def _(g):
        attention_back(dim, heads, g, r)

        @pl.when(lax.rem(g, 4) == 0)
        def _():
            finish(chunks - 2 + lax.div(g, 4), 0)

        @pl.when(lax.rem(g, 2) == 1)
        def _():
            finish(lax.div(g, 2), 1)

    dland = cotb.at[pl.ds(0, 3)]
    c_qkv = link.copy(4, qkvb.at[:, :, right], dland)
    c_qkv.start()

    def slice_of(k):
        return (r.wqkv_own, r.wqkv_oth)[k // 3].at[k % 3]

    load(16, slice_of(0), w1b.at[0]).start()

    first_unit = 2 * chunks

    def free(u):
        unit(u - 8, X_FIRST if u % 2 == 0 else Y_FIRST).wait_sent(0)

    u_qkv = [first_unit, first_unit + 1, first_unit + 2]
    u_proj, u_merge = first_unit + 3, [first_unit + 4, first_unit + 5]
    c_att.wait()
    load(6, r.att_own, fland.at[0]).wait()
    load(7, r.att_sib, fland.at[1]).wait()
    free(u_proj)
    put(u_proj % 8, dot_tn(sec[mine, :], fland[0]) + dot_tn(sec[theirs, :], fland[1]))
    unit(u_proj, Y_FIRST).start(0)

    for k in range(6):
        load(16 + k % 2, slice_of(k), w1b.at[k % 2]).wait()
        if k + 1 < 6:
            load(16 + (k + 1) % 2, slice_of(k + 1), w1b.at[(k + 1) % 2]).start()
        value = dot_nt(qkvb[k % 3, :, (left, right)[k // 3]], w1b[k % 2])
        if k == 0:
            facc[theirs, :] = value
        else:
            facc[theirs, :] += value
    load(12, r.stream0, st).wait()
    v1 = r.v1
    v1[...] = jnp.zeros_like(v1)

    def norm1(at):
        e = facc[pl.ds(pl.multiple_of(rows + at.start, 16), at.size), :]
        dv, hat = norm_back(e, st[at, :], r.nat[0:1, :], model)
        sec[at, :] = (gacc[at, :] + dv).astype(BF16)
        add_to(v1, 0, hat)
        add_to(v1, 1, e)

    steps(rows, 112, norm1)
    c_s0 = link.copy(5, sec.at[mine], ex.at[1])
    c_s0.start()

    load(10, r.first_own, gf.at[mine]).wait()
    load(11, r.first_sib, gf.at[theirs]).wait()
    for k in range(2):
        load(8 + k, r.wm_own.at[(left, right)[k], :], w2b.at[k]).start()
    c_qkv.wait()
    for s in range(3):
        free(u_qkv[s])
        put(u_qkv[s] % 8, dot_tn(gf[mine, :], qkvb[s, :, left]) + dot_tn(gf[theirs, :], dland[s]))
        unit(u_qkv[s], X_FIRST if s % 2 == 0 else Y_FIRST).start(0)
    load(1, r.x, cotb).start()
    load(10, r.mn_own, gf.at[mine]).start()
    load(11, r.mn_sib, gf.at[theirs]).start()

    c_s0.wait()
    load(10, r.mn_own, gf.at[mine]).wait()
    load(11, r.mn_sib, gf.at[theirs]).wait()
    for k in range(2):
        cols = (left, right)[k]
        free(u_merge[k])
        put(u_merge[k] % 8, dot_tn(sec[mine, :], gf[mine, cols]) + dot_tn(ex[1], gf[theirs, cols]))
        unit(u_merge[k], (X_FIRST, Y_FIRST)[k]).start(0)
    last = chunks + 2
    finish(chunks + 1, 0)
    finish(chunks, 0)

    rel_sum(area, heads, r.index, r.sums, r.rel)
    finish(chunks + 1, 1)
    finish(chunks, 1)
    finish(last, 0)

    for k in range(4):
        load(8 + k % 2, (r.wm_own, r.wm_oth)[k // 2].at[(left, right)[k % 2], :],
             w2b.at[k % 2]).wait()
        facc[k // 2 * rows : (k // 2 + 1) * rows, (left, right)[k % 2]] = dot_nt(
            sec[mine, :], w2b[k % 2]
        )
        if k < 2:
            load(8 + k, r.wm_oth.at[(left, right)[k], :], w2b.at[k]).start()
    load(1, r.x, cotb).wait()
    v0 = r.v0
    v0[...] = jnp.zeros_like(v0)
    width = 2 * model

    def norm0(at):
        def both(fn):
            return sum(jnp.sum(fn(i, j), 1, keepdims=True) for i in range(2) for j in range(2))

        def cols(j):
            return (left, right)[j]

        def here(i):
            return pl.ds(pl.multiple_of(i * rows + at.start, 16), at.size)

        xs = [[cotb[2 * who[i] + j, at, :].astype(F32) for j in range(2)] for i in range(2)]
        es = [[facc[here(i), cols(j)] for j in range(2)] for i in range(2)]
        sc = [[es[i][j] * r.mgo[i, :, cols(j)] for j in range(2)] for i in range(2)]
        mean = both(lambda i, j: xs[i][j]) * (1.0 / width)
        second = both(lambda i, j: xs[i][j] * xs[i][j]) * (1.0 / width)
        scale = lax.rsqrt(second - mean * mean + EPS)
        hats = [[(xs[i][j] - mean) * scale for j in range(2)] for i in range(2)]
        low = both(lambda i, j: sc[i][j]) * (1.0 / width)
        cross = both(lambda i, j: sc[i][j] * hats[i][j]) * (1.0 / width)
        for i in range(2):
            for j in range(2):
                d = scale * (sc[i][j] - low - hats[i][j] * cross)
                qkvb[i, at, cols(j)] = d.astype(BF16)
                v0[2 * i : 2 * i + 1, cols(j)] += jnp.sum(es[i][j] * hats[i][j], 0, keepdims=True)
                v0[2 * i + 1 : 2 * i + 2, cols(j)] += jnp.sum(es[i][j], 0, keepdims=True)

    steps(rows, 64, norm0)
    finish(last, 1)

    vs, vx = r.vs, r.vx
    heads_here = heads // 2
    for side, dst in ((0, vs.at[0]), (1, vx.at[0])):
        cols = (own_cols, oth_cols)[side]
        dst[...] = jnp.zeros(dst.shape, F32)
        for i in range(2):
            for j in range(2):
                dst[2 * i + j : 2 * i + j + 1, :] = v0[
                    2 * side + i : 2 * side + i + 1, j * half : (j + 1) * half
                ]
        dst[4:6, :] = v1[:, cols]
        dst[6:8, :] = r.vq[:, (left, right)[side]]
        dst[8:11, :] = v2[0:3, cols]
        if side == 0:
            dst[11:12, :] = r.gb2[...]
            for j in range(hidden // half):
                dst[12 + j : 13 + j, :] = r.gb1[:, j * half : (j + 1) * half]
        dst[16 : 16 + heads_here, 0 : r.rel.shape[1]] = r.rel[
            side * heads_here : (side + 1) * heads_here, :
        ]
    c_vec = link.copy(6, vx.at[0], vx.at[1])
    c_vec.start()

    pixel_rows = ones(gather_rows(rows, tokens, windows)[1])
    for b in range(2):
        for a in range(2):
            value = dot(pixel_rows, qkvb[b, :, (left, right)[a]])
            if b == 1:
                outs[2 + a].wait()
            r.pix[a] = value.reshape(*r.pix.shape[1:])
            outs.append(load(2 * b + a, r.pix.at[a], r.pixels_grad.at[:, a, :, who[b]]))
            outs[-1].start()
    c_vec.wait()
    vs[0] += vx[1]
    all_sum(sizes, place, vs, r.vbuf, r.vsend, r.vrecv)
    v = vs.at[3]
    for i in range(2):
        for j in range(2):
            (r.o_mg, r.o_ms)[i][:, j * half : (j + 1) * half] = v[2 * i + j : 2 * i + j + 1, :]
    for k, ref in enumerate((r.o_n1g, r.o_n1s)):
        ref[...] = v[4 + k : 5 + k, :]
    r.o_qb[...] = v[6:8, :]
    for k, ref in enumerate((r.o_n2g, r.o_n2s, r.o_pb, r.o_b2)):
        ref[...] = v[8 + k : 9 + k, :]
    for j in range(hidden // half):
        r.o_b1[:, j * half : (j + 1) * half] = v[12 + j : 13 + j, :]
    r.o_rel[...] = v[16 : 16 + heads_here, 0 : r.o_rel.shape[1]]

    for k in range(chunks):
        at = pl.ds(k * CHUNK, CHUNK)
        unit(2 * k, X_FIRST).finish(2, r.o_fc1.at[:, at])
        unit(2 * k + 1, Y_FIRST).finish(2, r.o_fc2.at[:, at])
    for s in range(3):
        unit(u_qkv[s], X_FIRST if s % 2 == 0 else Y_FIRST).finish(2, r.o_qkv.at[s])
    unit(u_proj, Y_FIRST).finish(2, r.o_proj)
    for k in range(2):
        unit(u_merge[k], (X_FIRST, Y_FIRST)[k]).finish(2, r.o_merge.at[:, (left, right)[k]])
    for one in outs[:2] + outs[4:]:
        one.wait()
    for u in range(first_unit + 6):
        one = unit(u, X_FIRST if u % 2 == 0 else Y_FIRST)
        for step in range(3):
            if step > 0 or u >= first_unit + 6 - 8:
                one.wait_sent(step)


def back(count, dim, heads, area, windows, entries, small, large):
    sizes = win_sizes(count)
    rows, tokens = windows * PAD, windows * area
    hidden = large["fc1"].shape[1]
    model = large["fc1"].shape[0]
    half = model // 2
    side = int(area**0.5)
    slots = -(-entries // 128) * 128
    n_units = 2 * (hidden // CHUNK) + 6
    part = model // count
    most = max(sizes) - 1
    nz, ny, nx = sizes
    big = dict(
        out=shape((2 * tokens, half), BF16),
        pixels_grad=shape((side, 2, side, 2, windows, half)),
    )
    outs = dict(
        big, o_mg=shape((1, model)), o_ms=shape((1, model)),
        o_n1g=shape((1, half)), o_n1s=shape((1, half)), o_qb=shape((2, half)),
        o_n2g=shape((1, half)), o_n2s=shape((1, half)), o_pb=shape((1, half)),
        o_b1=shape((1, hidden)), o_b2=shape((1, half)), o_rel=shape((heads // 2, entries)),
        o_fc1=shape((part, hidden)), o_fc2=shape((part, hidden)), o_qkv=shape((3, part, half)),
        o_proj=shape((part, half)), o_merge=shape((part, model)),
    )
    vm, dma = pltpu.VMEM, pltpu.SemaphoreType.DMA
    scratch = dict(
        sec=vm((2 * rows, model), BF16), gfb=vm((2 * rows, model), BF16),
        facc=vm((2 * rows, model), F32), gacc=vm((2 * rows, model), F32),
        st=vm((rows, model), F32), ex=vm((2, rows, model), BF16),
        w1b=vm((2, model, CHUNK), BF16), w2b=vm((2, CHUNK, model), BF16),
        cotb=vm((4, rows, half), BF16), qkvb=vm((3, rows, model), BF16),
        biasb=vm((PAD * heads, 128), F32), sums=vm((PAD * heads, 128), F32),
        act=vm((2 * rows, CHUNK), BF16), gh=vm((2 * rows, CHUNK), BF16),
        fsend=vm((2, rows, half), BF16), fland=vm((2, rows, half), BF16),
        pix=vm((2, side, side, windows, half), F32),
        src=vm((8, nz, ny, nx, part, CHUNK), BF16),
        buf0=vm((n_units, nx - 1, nz, ny, part, CHUNK), BF16),
        buf1=vm((n_units, ny - 1, nz, part, CHUNK), BF16),
        buf2=vm((n_units, nz - 1, part, CHUNK), BF16),
        v0=vm((4, model), F32), v1=vm((2, model), F32), v2=vm((3, model), F32),
        vq=vm((2, model), F32), rel=vm((heads, slots), F32), gb1=vm((1, hidden), F32),
        vs=vm((4, 32, half), F32), vx=vm((2, 32, half), F32), vbuf=vm((3, most, 32, half), F32),
        lsem=dma((18,)), wsem=dma((2, 2)), xsend=dma((8,)), xrecv=dma((8,)),
        rsend=dma((n_units, 3, most)), rrecv=dma((n_units, 3, most)),
        vsend=dma((3, most)), vrecv=dma((3, most)),
    )

    def body(r):
        back_body(sizes, dim, heads, area, r)

    return kernel_call(body, small, large, outs, scratch, big, collective=1)


def hand_on(arrays):
    names = list(arrays)

    free = pl.BlockSpec(memory_space=pl.ANY)
    n = len(names)

    def run(*refs):
        given, taken, held, sem = refs[:n], refs[n : 2 * n], refs[2 * n : 3 * n], refs[3 * n]
        ins = [pltpu.make_async_copy(given[k], held[k], sem.at[0, k]) for k in range(n)]
        outs = [pltpu.make_async_copy(held[k], taken[k], sem.at[1, k]) for k in range(n)]
        for one in ins:
            one.start()
        for one, other in zip(ins, outs):
            one.wait()
            other.start()
        for one in outs:
            one.wait()

    results = pl.pallas_call(
        run,
        out_shape=tuple(shape(a.shape, a.dtype) for a in arrays.values()),
        in_specs=[free] * n,
        out_specs=(free,) * n,
        scratch_shapes=[pltpu.VMEM(a.shape, a.dtype) for a in arrays.values()]
        + [pltpu.SemaphoreType.DMA((2, n))],
    )(*arrays.values())
    return SimpleNamespace(**dict(zip(names, results)))


def solution(mesh):
    count = mesh.shape["win"]

    def shards(
        pixels, merge_gain, merge_shift, merge_weight, norm1_gain, norm1_shift, qkv_weight,
        qkv_bias, rel_table, proj_weight, proj_bias, norm2_gain, norm2_shift, fc1_weight,
        fc1_bias, fc2_weight, fc2_bias, rel_index, keep, cotangent,
    ):
        wins, height, _, channels = pixels.shape
        side = height // 2
        area = side * side
        rows = wins * PAD
        model = merge_weight.shape[1]
        half = model // 2
        heads = 2 * rel_table.shape[1]
        dim = half // rel_table.shape[1]
        hidden = fc1_weight.shape[1]

        def row(v):
            return v.reshape(1, -1)

        index = jnp.pad(rel_index.T, ((0, 0), (0, 128 - area)))
        kept = keep.reshape(2, 1, wins * area)
        kept_rows = jnp.pad(
            keep.reshape(2 * wins, area), ((0, 0), (0, PAD - area))
        ).reshape(2, 1, rows)
        wqkv = qkv_weight.transpose(1, 0, 2)
        a = front(
            dim, heads, area, wins,
            dict(
                mg=row(merge_gain), ms=row(merge_shift), n1g=row(norm1_gain),
                n1s=row(norm1_shift), pb=row(proj_bias), n2g=row(norm2_gain),
                n2s=row(norm2_shift), qb=qkv_bias, table=rel_table.T, index=index, keep=kept,
            ),
            dict(
                pixels=pixels.transpose(1, 2, 0, 3).reshape(side, 2, side, 2, wins, channels),
                wm=merge_weight, wqkv=wqkv, wp=proj_weight, cot=cotangent,
            ),
        )
        b = back(
            count, dim, heads, area, wins, rel_table.shape[0],
            dict(
                keep=kept_rows, b1=row(fc1_bias), b2=row(fc2_bias), nat=a.nat, mgo=a.mgo,
                lse=a.lse, index=index, gb2=a.gb2,
            ),
            dict(
                second=a.second, gf=a.gf, stream1=a.stream1, stream0=a.stream0,
                fc1=fc1_weight, fc2=fc2_weight, wp_own=proj_weight, wp_oth=a.wp_oth,
                wqkv_own=wqkv, wqkv_oth=a.wqkv_oth, wm_own=merge_weight, wm_oth=a.wm_oth,
                att_own=a.att_own, att_sib=a.att_sib, qkv=a.qkv, bias=a.bias,
                first_own=a.first_own, first_sib=a.first_sib, mn_own=a.mn_own, mn_sib=a.mn_sib,
                x=a.x,
            ),
        )
        f = hand_on(vars(b))

        def flat(v):
            return v.reshape(-1)

        pixels_grad = f.pixels_grad.reshape(height, height, wins, channels)
        return (
            f.out, pixels_grad.transpose(2, 0, 1, 3), flat(f.o_mg), flat(f.o_ms), f.o_merge.T,
            flat(f.o_n1g), flat(f.o_n1s), f.o_qkv.transpose(1, 0, 2), f.o_qb, f.o_rel.T,
            f.o_proj.T, flat(f.o_pb), flat(f.o_n2g), flat(f.o_n2s), f.o_fc1, flat(f.o_b1),
            f.o_fc2.T, flat(f.o_b2),
        )

    in_specs = (
        P(("win", "tp"), None, None, None), P("tp"), P("tp"), P("tp", None), P("tp"), P("tp"),
        P(None, None, "tp"), P(None, "tp"), P(None, "tp"), P("tp", None), P("tp"), P("tp"),
        P("tp"), P(None, "tp"), P("tp"), P("tp", None), P("tp"), P(), P("win"), P("win", "tp"),
    )
    out_specs = (
        P("win", "tp"), P(("win", "tp"), None, None, None), P("tp"), P("tp"), P("tp", "win"),
        P("tp"), P("tp"), P("win", None, "tp"), P(None, "tp"), P(None, "tp"), P("tp", "win"),
        P("tp"), P("tp"), P("tp"), P("win", "tp"), P("tp"), P("tp", "win"), P("tp"),
    )
    return jax.shard_map(shards, mesh=mesh, in_specs=in_specs, out_specs=out_specs, check_vma=False)
```

```python
from types import SimpleNamespace

import jax
import jax.numpy as jnp
from jax import lax
from jax.experimental import pallas as pl
from jax.experimental.pallas import tpu as pltpu
from jax.sharding import PartitionSpec as P

EPS = 1e-05
F32 = jnp.float32
BF16 = jnp.bfloat16
MESH = pl.DeviceIdType.MESH
PAD = 112
LIMIT = 63 * 1024 * 1024


def shape(dims, dtype=F32):
    return jax.ShapeDtypeStruct(tuple(dims), dtype)


def kernel_call(body, small, large, outs, scratch, large_outs, collective=None):
    names = [*small, *large, *outs, *scratch]
    free, vmem = pl.BlockSpec(memory_space=pl.ANY), pl.BlockSpec(memory_space=pltpu.VMEM)
    more = {} if collective is None else dict(collective_id=collective, has_side_effects=True)

    def run(*refs):
        body(SimpleNamespace(**dict(zip(names, refs, strict=True))))

    results = pl.pallas_call(
        run,
        out_shape=tuple(outs.values()),
        in_specs=[vmem] * len(small) + [free] * len(large),
        out_specs=tuple(free if n in large_outs else vmem for n in outs),
        scratch_shapes=list(scratch.values()),
        compiler_params=pltpu.CompilerParams(vmem_limit_bytes=LIMIT, **more),
    )(*small.values(), *large.values())
    return SimpleNamespace(**dict(zip(outs, results)))


def dot(a, b):
    return jnp.dot(a, b, preferred_element_type=F32)


def dot_nt(a, b):
    return lax.dot_general(a, b, (((1,), (1,)), ((), ())), preferred_element_type=F32)


def dot_tn(a, b):
    return lax.dot_general(a, b, (((0,), (0,)), ((), ())), preferred_element_type=F32)


def stats(x, width):
    mean = jnp.sum(x, 1, keepdims=True) * (1.0 / width)
    second = jnp.sum(x * x, 1, keepdims=True) * (1.0 / width)
    return mean, lax.rsqrt(second - mean * mean + EPS)


def norm_back(e, x, gain, width):
    mean, scale = stats(x, width)
    xhat = (x - mean) * scale
    scaled = e * gain
    first = jnp.sum(scaled, 1, keepdims=True) * (1.0 / width)
    cross = jnp.sum(scaled * xhat, 1, keepdims=True) * (1.0 / width)
    return scale * (scaled - first - xhat * cross), e * xhat


def steps(total, size, fn):
    @pl.loop(0, total // size)
    def _(step):
        fn(pl.ds(pl.multiple_of(step * size, size), size))


def add_to(ref, row, value):
    ref[row : row + 1, :] += jnp.sum(value, 0, keepdims=True)


def spread(rows, tokens, windows):
    row = lax.broadcasted_iota(jnp.int32, (rows, tokens), 0)
    col = lax.broadcasted_iota(jnp.int32, (rows, tokens), 1)
    area = tokens // windows
    w = row // PAD
    k = row - w * PAD
    real = k < area
    return (
        jnp.logical_and(real, w * area + k == col),
        jnp.logical_and(real, k * windows + w == col),
    )


def gather_rows(rows, tokens, windows):
    row = lax.broadcasted_iota(jnp.int32, (tokens, rows), 1)
    col = lax.broadcasted_iota(jnp.int32, (tokens, rows), 0)
    area = tokens // windows
    w = row // PAD
    k = row - w * PAD
    real = k < area
    return (
        jnp.logical_and(real, w * area + k == col),
        jnp.logical_and(real, k * windows + w == col),
    )


def ones(mask):
    return jnp.where(mask, 1.0, 0.0).astype(BF16)


class Link:
    def __init__(self, sends, recvs):
        self.sends, self.recvs = sends, recvs

    def copy(self, k, src, dst):
        return pltpu.make_async_remote_copy(
            src_ref=src,
            dst_ref=dst,
            send_sem=self.sends.at[k],
            recv_sem=self.recvs.at[k],
            device_id=(lax.axis_index("win"), 1 - lax.axis_index("tp")),
            device_id_type=MESH,
        )


def head_masks(rows, width, dim):
    lane = lax.broadcasted_iota(jnp.int32, (rows, width), 1) // dim
    return [lane == h for h in range(width // dim)]


def stacked(block, masks):
    return jnp.concatenate([jnp.where(m, block, 0.0).astype(BF16) for m in masks], 0)


def diagonal(a, b):
    zero = jnp.zeros((PAD, 128), BF16)
    rest = jnp.zeros((128 - PAD, 256), BF16)
    return jnp.concatenate(
        [jnp.concatenate([a, zero], 1), rest, jnp.concatenate([zero, b], 1), rest], 0
    )


def bias_of(bias, heads, g, per):
    return [bias[pl.ds(g * per + h, PAD, stride=heads), :] for h in range(per)]


def attention_forward(dim, heads, g, r):
    per = 128 // dim
    windows = r.qkvb.shape[1] // PAD
    scale = dim ** (-0.5)
    masks = head_masks(PAD, 128, dim)
    lanes = pl.ds(pl.multiple_of(g * 128, 128), 128)
    bias = bias_of(r.biasb, heads, g, per)
    done, sums = [], []
    for w in range(0, windows, 2):
        at = [pl.ds((w + u) * PAD, PAD) for u in range(2)]
        q, k, v = ([r.qkvb[s, a, lanes] for a in at] for s in range(3))
        both = dot_nt(
            jnp.concatenate([stacked(k[0], masks), stacked(k[1], masks)], 1),
            diagonal(q[0], q[1]),
        )
        for u in range(2):
            vt = v[u].T
            parts = []
            for h in range(per):
                s = both[h * PAD : (h + 1) * PAD, u * 128 : (u + 1) * 128] * scale + bias[h]
                top = jnp.max(s, 0, keepdims=True)
                e = jnp.exp(s - top)
                total = jnp.sum(e, 0, keepdims=True)
                p = (e * (1.0 / total)).astype(BF16)
                sums.append(top + jnp.log(total))
                parts.append(dot(vt[h * dim : (h + 1) * dim], p))
            done.append(jnp.concatenate(parts, 0).T[:PAD].astype(BF16))
    for w in range(windows):
        r.attb[pl.ds(w * PAD, PAD), lanes] = done[w]
    r.lse[g] = jnp.concatenate(sums, 0)


def attention_back(dim, heads, g, r):
    per = 128 // dim
    windows = r.qkvb.shape[1] // PAD
    scale = dim ** (-0.5)
    masks = head_masks(PAD, 128, dim)
    lanes = pl.ds(pl.multiple_of(g * 128, 128), 128)
    bias = bias_of(r.biasb, heads, g, per)
    totals, done = [None] * per, []
    for w in range(windows):
        at = pl.ds(w * PAD, PAD)
        q, k, v = r.qkvb[0, at, lanes], r.qkvb[1, at, lanes], r.qkvb[2, at, lanes]
        go = r.ex[0, at, lanes]
        both = dot_nt(
            jnp.concatenate([stacked(k, masks), stacked(v, masks)], 1), diagonal(q, go)
        )
        kt = k.T
        p_parts, g_parts, dqs = [], [], []
        for h in range(per):
            here = slice(h * PAD, (h + 1) * PAD)
            p = jnp.exp(
                both[here, :128] * scale + bias[h] - r.lse[g, pl.ds(w * per + h, 1), :]
            )
            dp = both[here, 128:]
            gs = (p * (dp - jnp.sum(dp * p, 0, keepdims=True))).astype(BF16)
            wide = gs.astype(F32)
            totals[h] = wide if w == 0 else totals[h] + wide
            p_parts.append(p.astype(BF16))
            g_parts.append(gs)
            dqs.append(dot(kt[h * dim : (h + 1) * dim], gs))
        back = dot(
            jnp.concatenate([jnp.concatenate(p_parts, 0), jnp.concatenate(g_parts, 0)], 1),
            diagonal(go, q),
        )
        dv, dk = back[:PAD, :128], back[:PAD, 128:]
        for h in range(1, per):
            here = slice(h * PAD, (h + 1) * PAD)
            dv = jnp.where(masks[h], back[here, :128], dv)
            dk = jnp.where(masks[h], back[here, 128:], dk)
        dq = jnp.concatenate(dqs, 0).T[:PAD] * scale
        done.append((dq.astype(BF16), (dk * scale).astype(BF16), dv.astype(BF16)))
    q_sum = jnp.zeros((1, 128), F32)
    v_sum = jnp.zeros((1, 128), F32)
    for w in range(windows):
        for s in range(3):
            r.qkvb[s, pl.ds(w * PAD, PAD), lanes] = done[w][s]
        q_sum += jnp.sum(done[w][0].astype(F32), 0, keepdims=True)
        v_sum += jnp.sum(done[w][2].astype(F32), 0, keepdims=True)
    for h in range(per):
        r.sums[pl.ds(g * per + h, PAD, stride=heads), :] = totals[h]
    r.vq[0:1, lanes] = q_sum
    r.vq[1:2, lanes] = v_sum


PAIRS = 4


def onehot_of(index, first, entries):
    rows = [index[pl.ds(first + u, 1), :] for u in range(PAIRS)]
    ids = lax.broadcasted_iota(jnp.int32, (entries, rows[0].shape[1]), 0)
    return jnp.concatenate([ones(ids == row) for row in rows], 1)


def bias_spread(area, heads, table, index, out):
    entries = table.shape[1]
    top = table.astype(BF16)
    both = jnp.concatenate([top, (table - top.astype(F32)).astype(BF16)], 0)

    @pl.loop(0, area // PAIRS)
    def _(i):
        value = dot(both, onehot_of(index, i * PAIRS, entries))
        value = value[:heads] + value[heads:]
        for u in range(PAIRS):
            at = pl.ds(pl.multiple_of((i * PAIRS + u) * heads, heads), heads)
            out[at, :] = value[:, u * 128 : (u + 1) * 128]

    out[pl.ds(area * heads, (PAD - area) * heads), :] = jnp.full(
        ((PAD - area) * heads, out.shape[1]), -1e30, F32
    )


def rel_sum(first, last, heads, index, sums, rel):
    entries = rel.shape[1]

    @pl.loop(first, last)
    def _(i):
        hot = onehot_of(index, i * PAIRS, entries)
        s = jnp.concatenate(
            [
                sums[pl.ds(pl.multiple_of((i * PAIRS + u) * heads, heads), heads), :]
                for u in range(PAIRS)
            ],
            1,
        )
        top = s.astype(BF16)
        low = (s - top.astype(F32)).astype(BF16)
        both = dot_nt(jnp.concatenate([top, low], 0), hot)
        rel[...] += both[:heads] + both[heads:]


def win_bits(count):
    total = count.bit_length() - 1
    side = 1
    while 4 * (side + 1) * (side + 1) <= count:
        side += 1
    wide = side.bit_length() - 1
    axes = [range(wide), range(wide, 2 * wide), range(2 * wide, total)]
    near = [axis[0] for axis in axes if len(axis)]
    far = [bit for axis in axes for bit in axis[1:]]
    return near, far


def orders_of(count, n_units):
    near, far = win_bits(count)
    x, y, z = near
    turns = [(x, y, z), (y, x, z), (z, x, y), (x, z, y), (y, z, x), (z, y, x)]
    later = [(x, y, z), (y, x, z), (z, x, y), (x, y, z), (y, x, z), (z, y, x)]
    return [(*(turns if u < 6 else later)[u % 6], *far) for u in range(n_units)]


def my_bit(bit):
    return lax.rem(lax.div(lax.axis_index("win"), 1 << bit), 2)


def partner(bit):
    return lax.axis_index("win") + (1 - 2 * my_bit(bit)) * (1 << bit), lax.axis_index("tp")


def enter(bits):
    barrier = pltpu.get_barrier_semaphore()
    peers = [(lax.axis_index("win"), 1 - lax.axis_index("tp"))]
    peers += [partner(bit) for bit in range(bits)]
    for peer in peers:
        pl.semaphore_signal(barrier, inc=1, device_id=peer, device_id_type=MESH)
    pl.semaphore_wait(barrier, len(peers))


class Scatter:
    def __init__(self, order, src, bufs, sends, recvs, unit):
        self.order, self.held = order, [src, *bufs]
        self.sends, self.recvs, self.unit = sends, recvs, unit

    def pick(self, step, value):
        left = [b for b in range(len(self.order)) if b not in self.order[:step]]
        dim = len(left) - 1 - left.index(self.order[step])
        return self.held[step].at[(*([slice(None)] * dim), value)]

    def copy(self, step):
        bit = self.order[step]
        return pltpu.make_async_remote_copy(
            src_ref=self.pick(step, 1 - my_bit(bit)),
            dst_ref=self.held[step + 1],
            send_sem=self.sends.at[self.unit, step],
            recv_sem=self.recvs.at[self.unit, step],
            device_id=partner(bit),
            device_id_type=MESH,
        )

    def finish(self, step, out=None):
        self.copy(step).wait_recv()
        mine = self.pick(step, my_bit(self.order[step]))
        got = self.held[step + 1]
        lead = got.shape[:-2]
        if not lead:
            out[...] = mine[...].astype(F32) + got[...].astype(F32)
            return

        @pl.loop(0, 1 << len(lead))
        def _(i):
            at = tuple(lax.rem(lax.div(i, 1 << k), 2) for k in reversed(range(len(lead))))
            got[at] = (mine[at].astype(F32) + got[at].astype(F32)).astype(BF16)

        self.copy(step + 1).start()


def front_body(dim, heads, area, r):
    enter(0)
    t = lax.axis_index("tp")
    who = (t, 1 - t)
    rows, model = r.firstb.shape
    half = model // 2
    windows = rows // PAD
    tokens = windows * area
    link = Link(r.xsend, r.xrecv)
    own_cols = pl.ds(pl.multiple_of(t * half, half), half)
    oth_cols = pl.ds(pl.multiple_of((1 - t) * half, half), half)

    def load(k, src, dst):
        return pltpu.make_async_copy(src, dst, r.lsem.at[k])

    c_wm = link.copy(0, r.wm, r.wmb.at[1])
    c_wm.start()
    loads = [load(k, r.pixels.at[:, k % 2, :, k // 2], r.pix.at[k]) for k in range(4)]
    loads += [load(4, r.cot, r.cotb.at[0]), load(5, r.wm, r.wmb.at[0])]
    for one in loads:
        one.start()
    vx = r.vx
    vx[0] = jnp.zeros(vx.shape[1:], F32)
    for k, ref in enumerate((r.mg, r.ms)):
        for j in range(2):
            vx[0, 2 * k + j : 2 * k + j + 1, :] = ref[:, j * half : (j + 1) * half]
    for k, ref in enumerate((r.n1g, r.n1s, r.pb, r.n2g, r.n2s)):
        vx[0, 4 + k : 5 + k, :] = ref[...]
    vx[0, 9:11, :] = r.qb[...]
    vx[0, 16 : 16 + heads // 2, 0 : r.table.shape[1]] = r.table[...]
    c_vec = link.copy(1, vx.at[0], vx.at[1])
    c_vec.start()
    c_cot = link.copy(2, r.cot, r.cotb.at[1])
    c_cot.start()
    c_wq = link.copy(3, r.wqkv, r.wqb.at[1])
    c_wq.start()
    c_wp = link.copy(4, r.wp, r.wpb.at[pl.ds(half, half), :])
    c_wp.start()
    late = [load(6, r.wqkv, r.wqb.at[0]), load(7, r.wp, r.wpb.at[pl.ds(0, half), :])]
    for one in late:
        one.start()
    stores = []

    def store(src, dst):
        one = pltpu.make_async_copy(src, dst, r.ssem.at[len(stores)])
        stores.append(one)
        one.start()

    token_rows, pixel_rows = spread(rows, tokens, windows)
    pixel_rows = ones(pixel_rows)
    for k in range(4):
        loads[k].wait()
        r.xb[k] = dot(
            pixel_rows, r.pix[k].astype(F32).reshape(tokens, half).astype(BF16)
        ).astype(BF16)
    store(r.xb, r.x)

    c_vec.wait()
    mgo, nat = r.mgo, r.nat
    for side in range(2):
        for j in range(2):
            mgo[side, :, j * half : (j + 1) * half] = vx[side, j : j + 1, :]
            r.mso[side, :, j * half : (j + 1) * half] = vx[side, 2 + j : 3 + j, :]
        nat[0:5, (own_cols, oth_cols)[side]] = vx[side, 4:9, :]
    width = 2 * model

    def norm0(at):
        xs = [
            [r.xb[2 * who[i] + j, at, :].astype(F32) for j in range(2)] for i in range(2)
        ]

        def both(fn):
            return sum(jnp.sum(fn(x), 1, keepdims=True) for pair in xs for x in pair)

        mean = both(lambda x: x) * (1.0 / width)
        scale = lax.rsqrt(both(lambda x: x * x) * (1.0 / width) - mean * mean + EPS)
        for i in range(2):
            for j in range(2):
                cols = pl.ds(j * half, half)
                value = (xs[i][j] - mean) * scale * mgo[i, :, cols] + r.mso[i, :, cols]
                r.mnb[i, at, cols] = value.astype(BF16)

    steps(rows, 64, norm0)
    c_mn = link.copy(6, r.mnb.at[1], r.mn_sib)
    c_mn.start()
    store(r.mnb.at[0], r.mn_own)

    entries = r.tableb.shape[1]
    for side in range(2):
        r.tableb[side * (heads // 2) : (side + 1) * (heads // 2), :] = vx[
            side, 16 : 16 + heads // 2, 0:entries
        ]
    bias_spread(area, heads, r.tableb[...], r.index, r.biasb)
    store(r.biasb, r.bias)

    loads[4].wait()
    c_cot.wait()
    total = jnp.zeros((1, half), F32)
    for side in range(2):
        at = pl.ds(pl.multiple_of(who[side] * tokens, tokens), tokens)
        pick = ones(jnp.logical_and(token_rows, r.keep[who[side]] > 0))
        mine = dot(pick, r.cotb[0, at, :])
        total += jnp.sum(mine, 0, keepdims=True)
        here = pl.ds(side * rows, rows)
        r.gfb[here, own_cols] = mine.astype(BF16)
        r.gfb[here, oth_cols] = dot(pick, r.cotb[1, at, :]).astype(BF16)
    r.gb2[...] = total
    store(r.gfb, r.gf)

    loads[5].wait()

    def own_part(at):
        r.s0b[:, at] = dot(r.mnb[0], r.wmb[0, :, at])

    steps(model, 512, own_part)
    c_wm.wait()
    store(r.wmb.at[1], r.wm_oth)

    def oth_part(at):
        r.s0b[:, at] += dot(r.mnb[1], r.wmb[1, :, at])

    steps(model, 512, oth_part)
    store(r.s0b, r.stream0)

    def norm1(at):
        x = r.s0b[at, :]
        mean, scale = stats(x, model)
        r.firstb[at, :] = ((x - mean) * scale * nat[0:1, :] + nat[1:2, :]).astype(BF16)

    steps(rows, 112, norm1)
    c_first = link.copy(5, r.firstb, r.first_sib)
    c_first.start()
    store(r.firstb, r.first_own)

    late[0].wait()
    for side in range(2):
        if side == 1:
            c_wq.wait()
            store(r.wqb.at[1], r.wqkv_oth)
        for s in range(3):
            cols = pl.ds(side * half, half)
            value = dot(r.firstb[...], r.wqb[side, s])
            if s != 1:
                value += vx[side, 9 + s // 2 : 10 + s // 2, :]
            r.qkvb[s, :, cols] = value.astype(BF16)
    store(r.qkvb, r.qkv)

    @pl.loop(0, model // 128)
    def _(g):
        attention_forward(dim, heads, g, r)

    c_att = link.copy(7, r.attb.at[:, pl.ds(half, half)], r.att_sib)
    c_att.start()
    store(r.attb.at[:, pl.ds(0, half)], r.att_own)

    late[1].wait()
    c_wp.wait()
    store(r.wpb.at[pl.ds(half, half), :], r.wp_oth)

    def project(at):
        value = dot(r.attb[...], r.wpb[:, at]) + nat[2:3, at]
        r.s1b[:, at] = r.s0b[:, at] + value

    steps(model, 512, project)
    store(r.s1b, r.stream1)

    def norm2(at):
        x = r.s1b[at, :]
        mean, scale = stats(x, model)
        r.secb[at, :] = ((x - mean) * scale * nat[3:4, :] + nat[4:5, :]).astype(BF16)

    steps(rows, 112, norm2)
    store(r.secb, r.second)
    for one in (c_mn, c_first, c_att):
        one.wait()
    for one in stores:
        one.wait()


def front(dim, heads, area, windows, small, large):
    rows, tokens = windows * PAD, windows * area
    model = large["wm"].shape[1]
    half = model // 2
    side = large["pixels"].shape[0:3:2]
    slots = -(-small["table"].shape[1] // 128) * 128
    vm, dma = pltpu.VMEM, pltpu.SemaphoreType.DMA
    big = dict(
        x=shape((4, rows, half), BF16), gf=shape((2 * rows, model), BF16),
        stream0=shape((rows, model)), stream1=shape((rows, model)),
        second=shape((rows, model), BF16), qkv=shape((3, rows, model), BF16),
        bias=shape((PAD * heads, 128)), first_own=shape((rows, model), BF16),
        first_sib=shape((rows, model), BF16), mn_own=shape((rows, model), BF16),
        mn_sib=shape((rows, model), BF16), att_own=shape((rows, half), BF16),
        att_sib=shape((rows, half), BF16), wm_oth=shape((model, model), BF16),
        wqkv_oth=shape((3, model, half), BF16), wp_oth=shape((half, model), BF16),
    )
    outs = dict(
        big, gb2=shape((1, half)), nat=shape((8, model)), mgo=shape((2, 1, model)),
        lse=shape((model // 128, windows * 128 // dim, 128)),
    )
    scratch = dict(
        wmb=vm((2, model, model), BF16), wqb=vm((2, 3, model, half), BF16),
        wpb=vm((model, model), BF16), pix=vm((4, *side, windows, half), BF16),
        xb=vm((4, rows, half), BF16), cotb=vm((2, 2 * tokens, half), BF16),
        gfb=vm((2 * rows, model), BF16), mnb=vm((2, rows, model), BF16),
        s0b=vm((rows, model), F32), s1b=vm((rows, model), F32), firstb=vm((rows, model), BF16),
        qkvb=vm((3, rows, model), BF16), biasb=vm((PAD * heads, 128), F32),
        attb=vm((rows, model), BF16), secb=vm((rows, model), BF16),
        vx=vm((2, 32, half), F32), mso=vm((2, 1, model), F32), tableb=vm((heads, slots), F32),
        lsem=dma((8,)), ssem=dma((16,)), xsend=dma((8,)), xrecv=dma((8,)),
    )

    def body(r):
        front_body(dim, heads, area, r)

    return kernel_call(body, small, large, outs, scratch, big, collective=2)


CHUNK = 512
PLAN = {
    2: ((0, 0), (1, 0)),
    3: ((2, 0),),
    7: ((3, 0),),
    9: ((4, 0),),
    11: ((1, 1),),
    12: ((5, 0),),
    13: ((0, 1),),
    15: ((3, 1),),
    17: ((6, 0),),
    19: ((4, 1),),
    20: ((7, 0), (1, 2)),
    21: ((2, 1),),
    25: ((5, 1), (4, 2)),
    27: ((3, 2),),
    29: ((7, 1), (8, 0)),
    30: ((6, 1), (5, 2)),
    31: ((0, 2),),
    32: ((2, 2),),
    33: ((1, 3),),
    34: ((4, 3), (3, 3)),
    35: ((7, 2), (9, 0)),
    36: ((10, 0),),
    37: ((8, 1),),
    40: (
        (11, 0), (6, 2), (-1, 0), (13, 0), (5, 3), (-1, 1),
        (12, 0), (0, 3), (-1, 2), (9, 1), (2, 3), (-1, 3),
        (8, 2), (10, 1), (-1, 4), (7, 3), (6, 3), (11, 1),
        (13, 1), (9, 2), (8, 3), (11, 2), (10, 2), (12, 1),
        (13, 2), (9, 3), (11, 3), (10, 3), (12, 2), (13, 3),
        (12, 3),
    ),
}


def back_body(bits, orders, dim, heads, area, r):
    t = lax.axis_index("tp")
    who = (t, 1 - t)
    sec, gf, facc, gacc, st, ex = r.sec, r.gfb, r.facc, r.gacc, r.st, r.ex
    w1b, w2b, cotb, qkvb = r.w1b, r.w2b, r.cotb, r.qkvb
    rows, model = st.shape
    half = model // 2
    hidden = r.fc1.shape[1]
    chunks = hidden // CHUNK
    windows = rows // PAD
    tokens = windows * area
    mine, theirs = pl.ds(0, rows), pl.ds(rows, rows)
    left, right = pl.ds(0, half), pl.ds(half, half)
    link = Link(r.xsend, r.xrecv)
    own_cols = pl.ds(pl.multiple_of(t * half, half), half)
    oth_cols = pl.ds(pl.multiple_of((1 - t) * half, half), half)
    part = model // (1 << bits)

    def load(k, src, dst):
        return pltpu.make_async_copy(src, dst, r.lsem.at[k])

    def unit(u):
        bufs = [buf.at[u] for buf in r.bufs]
        return Scatter(orders[u], r.src.at[u % 8], bufs, r.rsend, r.rrecv, u)

    def put(u, value):
        if u >= 8:
            unit(u - 8).copy(0).wait_send()
        r.src[u % 8] = value.astype(BF16).reshape(*([2] * bits), part, CHUNK)
        unit(u).copy(0).start()

    def held(u):
        return st.at[u // 2 * part : (u // 2 + 1) * part, (left, right)[u % 2]]

    def result(u):
        if u < 2 * chunks:
            return (r.o_fc1, r.o_fc2)[u % 2].at[:, pl.ds(u // 2 * CHUNK, CHUNK)]
        u -= 2 * chunks
        if u == 0:
            return r.o_proj
        if u < 4:
            return r.o_qkv.at[u - 1]
        return r.o_merge.at[:, (left, right)[u - 4]]

    last_step = bits - 1
    copies = [
        pltpu.make_async_remote_copy(
            src_ref=r.vs.at[bit],
            dst_ref=r.vbuf.at[bit],
            send_sem=r.vsend.at[bit],
            recv_sem=r.vrecv.at[bit],
            device_id=partner(bit),
            device_id_type=MESH,
        )
        for bit in range(bits)
    ]

    def vectors(step):
        if step == 0:
            link.copy(6, r.vx.at[0], r.vx.at[1]).wait()
            r.vs[0] += r.vx[1]
        else:
            copies[step - 1].wait()
            r.vs[step] = r.vs[step - 1] + r.vbuf[step - 1]
        if step < bits:
            copies[step].start()

    def pump(place):
        for u, step in PLAN.get(place, ()):
            if u < 0:
                vectors(step)
                continue
            unit(u).finish(step, held(u))
            if step == last_step:
                write(u).start()

    def write(u):
        return pltpu.make_async_copy(held(u), result(u), r.osem.at[u])

    enter(bits)
    c_sec = link.copy(0, r.second, sec.at[theirs])
    c_sec.start()
    loads = [
        load(0, r.second, sec.at[mine]), load(1, r.gf, gf), load(3, r.stream1, st),
        load(4, r.qkv, qkvb),
    ]
    for one in loads:
        one.start()

    def weights(c):
        slot = lax.rem(c, 2)
        cols = pl.ds(pl.multiple_of(c * CHUNK, CHUNK), CHUNK)
        return (
            pltpu.make_async_copy(r.fc1.at[:, cols], w1b.at[slot], r.wsem.at[0, slot]),
            pltpu.make_async_copy(r.fc2.at[cols, :], w2b.at[slot], r.wsem.at[1, slot]),
        )

    for one in weights(0):
        one.start()
    for one in loads[0:2]:
        one.wait()
    c_sec.wait()

    blocks = CHUNK // 128
    hid, dact, act, gh = r.sums, r.biasb, r.act, r.gh

    @pl.loop(0, chunks)
    def _(c):
        slot = lax.rem(c, 2)
        for one in weights(c):
            one.wait()

        @pl.when(c + 1 < chunks)
        def _():
            for one in weights(c + 1):
                one.start()

        of = pl.ds(pl.multiple_of(c * CHUNK, CHUNK), CHUNK)
        value = dot(sec[...], w1b[slot]) + r.b1[:, of]
        for b in range(blocks):
            hid[b * 2 * rows : (b + 1) * 2 * rows, :] = value[:, b * 128 : (b + 1) * 128]
        value = dot_nt(gf[...], w2b[slot])
        for b in range(blocks):
            dact[b * 2 * rows : (b + 1) * 2 * rows, :] = value[:, b * 128 : (b + 1) * 128]
        for b in range(blocks):
            lanes = pl.ds(b * 128, 128)

            def gelu(at):
                here = pl.ds(pl.multiple_of(b * 2 * rows + at.start, 128), at.size)
                x = hid[here, :]
                cdf = 0.5 * (1.0 + lax.erf(x * 0.7071067811865476))
                pdf = jnp.exp(x * x * -0.5) * 0.3989422804014327
                act[at, lanes] = (x * cdf).astype(BF16)
                gh[at, lanes] = (dact[here, :] * (cdf + x * pdf)).astype(BF16)

            steps(2 * rows, 128, gelu)
        r.gb1[:, of] = jnp.sum(gh[...].astype(F32), 0, keepdims=True)
        for k, value in enumerate((dot_tn(sec[...], gh[...]), dot_tn(gf[...], act[...]))):
            r.src[2 * c + k] = value.astype(BF16).reshape(*([2] * bits), part, CHUNK)
            for j in range(chunks):

                @pl.when(c == j)
                def _():
                    unit(2 * j + k).copy(0).start()

        for j in range(chunks):

            @pl.when(c == j)
            def _():
                pump(j)

        @pl.when(c == 0)
        def _():
            facc[...] = dot(act[...], w2b[slot])
            gacc[...] = dot_nt(gh[...], w1b[slot])

        @pl.when(c > 0)
        def _():
            facc[...] += dot(act[...], w2b[slot])
            gacc[...] += dot_nt(gh[...], w1b[slot])

        for j in range(chunks):

            @pl.when(c == j)
            def _():
                pump(chunks + j)

    load(5, r.bias, r.biasb).start()
    load(6, r.att_own, act.at[mine]).start()
    load(7, r.att_sib, act.at[theirs]).start()
    for k, src in enumerate((r.wp_own, r.wp_oth)):
        load(8 + k, src, w2b.at[k]).start()
    ex[0] = gacc[theirs].astype(BF16)
    c_g2 = link.copy(1, ex.at[0], ex.at[1])
    c_g2.start()
    load(3, r.stream1, st).wait()
    fsend, fland = gh, cotb.at[pl.ds(3, 2)]
    fsend[mine, :] = facc[theirs, oth_cols].astype(BF16)
    fsend[theirs, :] = (facc[mine, oth_cols] + st[:, oth_cols]).astype(BF16)
    c_feed = [
        link.copy(k, fsend.at[(mine, theirs)[k - 7]], fland.at[k - 7]) for k in (7, 8)
    ]
    for one in c_feed:
        one.start()

    def fold(at):
        own = facc[at, own_cols] + st[at, own_cols]
        oth = facc[pl.ds(pl.multiple_of(rows + at.start, 16), at.size), own_cols]
        facc[at, left] = own
        facc[at, right] = oth

    pump(8)
    v2 = r.v2
    v2[...] = jnp.zeros_like(v2)
    c_g2.wait()

    def norm2(at):
        e = gacc[at, :] + ex[1, at, :].astype(F32)
        dv, hat = norm_back(e, st[at, :], r.nat[3:4, :], model)
        d = gf[at, :].astype(F32) + dv
        gacc[at, :] = d
        low = d.astype(BF16)
        sec[at, :] = low
        add_to(v2, 0, hat)
        add_to(v2, 1, e)
        add_to(v2, 2, low.astype(F32))

    steps(rows, 112, norm2)
    c_att = link.copy(3, sec.at[mine], sec.at[theirs])
    c_att.start()
    load(10, r.first_own, gf.at[mine]).start()
    load(11, r.first_sib, gf.at[theirs]).start()
    pump(9)
    steps(rows, 112, fold)
    pump(10)
    for k, src in enumerate((r.wp_own, r.wp_oth)):
        load(8 + k, src, w2b.at[k]).wait()
        ex[0, :, (left, right)[k]] = dot_nt(sec[mine, :], w2b[k]).astype(BF16)

    pump(11)

    first_unit = 2 * chunks
    u_proj, u_qkv = first_unit, first_unit + 1
    u_merge = first_unit + 4
    load(6, r.att_own, act.at[mine]).wait()
    load(7, r.att_sib, act.at[theirs]).wait()
    c_att.wait()
    put(u_proj, dot_tn(sec[...], act[...]))
    pump(12)

    s0 = facc.at[theirs]
    load(12, r.stream0, s0).start()
    load(4, r.qkv, qkvb).wait()
    load(5, r.bias, r.biasb).wait()

    @pl.loop(0, model // 128)
    def _(g):
        attention_back(dim, heads, g, r)

        for k in range(8):

            @pl.when(g == k)
            def _():
                pump(13 + k)

    dland = cotb.at[pl.ds(0, 3)]
    c_qkv = link.copy(4, qkvb.at[:, :, right], dland)
    c_qkv.start()

    def slice_of(k):
        return (r.wqkv_own, r.wqkv_oth)[k // 3].at[k % 3]

    load(16, slice_of(0), w1b.at[0]).start()

    for k in range(6):
        load(16 + k % 2, slice_of(k), w1b.at[k % 2]).wait()
        if k + 1 < 6:
            load(16 + (k + 1) % 2, slice_of(k + 1), w1b.at[(k + 1) % 2]).start()
        value = dot_nt(qkvb[k % 3, :, (left, right)[k // 3]], w1b[k % 2])
        if k == 0:
            gacc[theirs, :] = value
        else:
            gacc[theirs, :] += value
        pump(21 + k)
    load(12, r.stream0, s0).wait()
    v1 = r.v1
    v1[...] = jnp.zeros_like(v1)

    def norm1(at):
        e = gacc[pl.ds(pl.multiple_of(rows + at.start, 16), at.size), :]
        dv, hat = norm_back(e, s0[at, :], r.nat[0:1, :], model)
        sec[at, :] = (gacc[at, :] + dv).astype(BF16)
        add_to(v1, 0, hat)
        add_to(v1, 1, e)

    steps(rows, 112, norm1)
    c_s0 = link.copy(5, sec.at[mine], ex.at[1])
    c_s0.start()

    load(10, r.first_own, gf.at[mine]).wait()
    load(11, r.first_sib, gf.at[theirs]).wait()
    for k in range(2):
        load(8 + k, r.wm_own.at[(left, right)[k], :], w2b.at[k]).start()
    c_qkv.wait()
    pump(27)
    for s in range(3):
        put(u_qkv + s, dot_tn(gf[mine, :], qkvb[s, :, left]) + dot_tn(gf[theirs, :], dland[s]))
        pump(28 + s)
    load(10, r.mn_own, gf.at[mine]).start()
    load(11, r.mn_sib, gf.at[theirs]).start()

    c_s0.wait()
    load(10, r.mn_own, gf.at[mine]).wait()
    load(11, r.mn_sib, gf.at[theirs]).wait()
    for k in range(2):
        cols = (left, right)[k]
        put(u_merge + k, dot_tn(sec[mine, :], gf[mine, cols]) + dot_tn(ex[1], gf[theirs, cols]))
        pump(31 + k)

    for one in c_feed:
        one.wait()
    token_rows = gather_rows(rows, tokens, windows)[0]
    outs = []
    for side in range(2):
        value = facc[mine, (left, right)[side]] + fland[side].astype(F32)
        pick = ones(jnp.logical_and(token_rows, r.keep[who[side]] > 0))
        fsend[side * rows : side * rows + tokens, :] = dot(pick, (value + r.b2[...]).astype(BF16)).astype(BF16)
        at = pl.ds(pl.multiple_of(who[side] * tokens, tokens), tokens)
        outs.append(load(14 + side, fsend.at[pl.ds(side * rows, tokens), :], r.out.at[at, :]))
        outs[-1].start()
    load(1, r.x, cotb.at[pl.ds(0, 4)]).start()
    pump(33)

    r.rel[...] = jnp.zeros_like(r.rel)
    for k in range(2):
        rel_sum(k * 12, (area // PAIRS if k else 12), heads, r.index, r.sums, r.rel)
        pump(34 + k)

    for k in range(4):
        load(8 + k % 2, (r.wm_own, r.wm_oth)[k // 2].at[(left, right)[k % 2], :],
             w2b.at[k % 2]).wait()
        facc[k // 2 * rows : (k // 2 + 1) * rows, (left, right)[k % 2]] = dot_nt(
            sec[mine, :], w2b[k % 2]
        )
        if k < 2:
            load(8 + k, r.wm_oth.at[(left, right)[k], :], w2b.at[k]).start()
    pump(36)
    load(1, r.x, cotb.at[pl.ds(0, 4)]).wait()
    v0 = r.v0
    v0[...] = jnp.zeros_like(v0)
    width = 2 * model

    def norm0(at):
        def both(fn):
            return sum(jnp.sum(fn(i, j), 1, keepdims=True) for i in range(2) for j in range(2))

        def cols(j):
            return (left, right)[j]

        def here(i):
            return pl.ds(pl.multiple_of(i * rows + at.start, 16), at.size)

        xs = [[cotb[2 * who[i] + j, at, :].astype(F32) for j in range(2)] for i in range(2)]
        es = [[facc[here(i), cols(j)] for j in range(2)] for i in range(2)]
        sc = [[es[i][j] * r.mgo[i, :, cols(j)] for j in range(2)] for i in range(2)]
        mean = both(lambda i, j: xs[i][j]) * (1.0 / width)
        second = both(lambda i, j: xs[i][j] * xs[i][j]) * (1.0 / width)
        scale = lax.rsqrt(second - mean * mean + EPS)
        hats = [[(xs[i][j] - mean) * scale for j in range(2)] for i in range(2)]
        low = both(lambda i, j: sc[i][j]) * (1.0 / width)
        cross = both(lambda i, j: sc[i][j] * hats[i][j]) * (1.0 / width)
        for i in range(2):
            for j in range(2):
                d = scale * (sc[i][j] - low - hats[i][j] * cross)
                qkvb[i, at, cols(j)] = d.astype(BF16)
                v0[2 * i : 2 * i + 1, cols(j)] += jnp.sum(es[i][j] * hats[i][j], 0, keepdims=True)
                v0[2 * i + 1 : 2 * i + 2, cols(j)] += jnp.sum(es[i][j], 0, keepdims=True)

    steps(rows, 64, norm0)
    pump(37)

    vs, vx = r.vs, r.vx
    heads_here = heads // 2
    for side, dst in ((0, vs.at[0]), (1, vx.at[0])):
        cols = (own_cols, oth_cols)[side]
        dst[...] = jnp.zeros(dst.shape, F32)
        for i in range(2):
            for j in range(2):
                dst[2 * i + j : 2 * i + j + 1, :] = v0[
                    2 * side + i : 2 * side + i + 1, j * half : (j + 1) * half
                ]
        dst[4:6, :] = v1[:, cols]
        dst[6:8, :] = r.vq[:, (left, right)[side]]
        dst[8:11, :] = v2[0:3, cols]
        if side == 0:
            dst[11:12, :] = r.gb2[...]
            for j in range(hidden // half):
                dst[12 + j : 13 + j, :] = r.gb1[:, j * half : (j + 1) * half]
        dst[16 : 16 + heads_here, 0 : r.rel.shape[1]] = r.rel[
            side * heads_here : (side + 1) * heads_here, :
        ]
    link.copy(6, vx.at[0], vx.at[1]).start()
    pump(38)

    outs[0].wait()
    pixel_rows = ones(gather_rows(rows, tokens, windows)[1])
    for b in range(2):
        for a in range(2):
            value = dot(pixel_rows, qkvb[b, :, (left, right)[a]])
            outs[-1].wait()
            r.pix[...] = value.reshape(*r.pix.shape)
            outs.append(load(2 * b + a, r.pix, r.pixels_grad.at[:, a, :, who[b]]))
            outs[-1].start()
    pump(39)
    pump(40)
    v = vs.at[bits]
    for i in range(2):
        for j in range(2):
            (r.o_mg, r.o_ms)[i][:, j * half : (j + 1) * half] = v[2 * i + j : 2 * i + j + 1, :]
    for k, ref in enumerate((r.o_n1g, r.o_n1s)):
        ref[...] = v[4 + k : 5 + k, :]
    r.o_qb[...] = v[6:8, :]
    for k, ref in enumerate((r.o_n2g, r.o_n2s, r.o_pb, r.o_b2)):
        ref[...] = v[8 + k : 9 + k, :]
    for j in range(hidden // half):
        r.o_b1[:, j * half : (j + 1) * half] = v[12 + j : 13 + j, :]
    r.o_rel[...] = v[16 : 16 + heads_here, 0 : r.o_rel.shape[1]]

    outs[-1].wait()
    for u in range(first_unit + 6):
        write(u).wait()
        for step in range(bits):
            if step > 0 or u >= first_unit + 6 - 8:
                unit(u).copy(step).wait_send()


def back(count, dim, heads, area, windows, entries, small, large):
    bits = count.bit_length() - 1
    rows, tokens = windows * PAD, windows * area
    hidden = large["fc1"].shape[1]
    model = large["fc1"].shape[0]
    half = model // 2
    side = int(area**0.5)
    slots = -(-entries // 128) * 128
    n_units = 2 * (hidden // CHUNK) + 6
    part = model // count
    orders = orders_of(count, n_units)
    big = dict(
        out=shape((2 * tokens, half), BF16),
        pixels_grad=shape((side, 2, side, 2, windows, half)),
        o_fc1=shape((part, hidden)), o_fc2=shape((part, hidden)), o_qkv=shape((3, part, half)),
        o_proj=shape((part, half)), o_merge=shape((part, model)),
    )
    outs = dict(
        big, o_mg=shape((1, model)), o_ms=shape((1, model)),
        o_n1g=shape((1, half)), o_n1s=shape((1, half)), o_qb=shape((2, half)),
        o_n2g=shape((1, half)), o_n2s=shape((1, half)), o_pb=shape((1, half)),
        o_b1=shape((1, hidden)), o_b2=shape((1, half)), o_rel=shape((heads // 2, entries)),
    )
    vm, dma = pltpu.VMEM, pltpu.SemaphoreType.DMA
    scratch = dict(
        sec=vm((2 * rows, model), BF16), gfb=vm((2 * rows, model), BF16),
        facc=vm((2 * rows, model), F32), gacc=vm((2 * rows, model), F32),
        st=vm((rows, model), F32), ex=vm((2, rows, model), BF16),
        w1b=vm((2, model, CHUNK), BF16), w2b=vm((2, CHUNK, model), BF16),
        cotb=vm((5, rows, half), BF16), qkvb=vm((3, rows, model), BF16),
        biasb=vm((PAD * heads, 128), F32), sums=vm((PAD * heads, 128), F32),
        act=vm((2 * rows, CHUNK), BF16), gh=vm((2 * rows, CHUNK), BF16),
        pix=vm((side, side, windows, half), F32),
        src=vm((8, *([2] * bits), part, CHUNK), BF16),
        bufs=[vm((n_units, *([2] * k), part, CHUNK), BF16) for k in reversed(range(bits))],
        v0=vm((4, model), F32), v1=vm((2, model), F32), v2=vm((3, model), F32),
        vq=vm((2, model), F32), rel=vm((heads, slots), F32), gb1=vm((1, hidden), F32),
        vs=vm((bits + 1, 32, half), F32), vx=vm((2, 32, half), F32), vbuf=vm((bits, 32, half), F32),
        lsem=dma((18,)), wsem=dma((2, 2)), xsend=dma((9,)), xrecv=dma((9,)), osem=dma((n_units,)),
        rsend=dma((n_units, bits)), rrecv=dma((n_units, bits)),
        vsend=dma((bits,)), vrecv=dma((bits,)),
    )

    def body(r):
        back_body(bits, orders, dim, heads, area, r)

    return kernel_call(body, small, large, outs, scratch, big, collective=1)


def hand_on(arrays):
    names = list(arrays)

    free = pl.BlockSpec(memory_space=pl.ANY)
    n = len(names)

    def run(*refs):
        given, taken, held, sem = refs[:n], refs[n : 2 * n], refs[2 * n : 3 * n], refs[3 * n]
        ins = [pltpu.make_async_copy(given[k], held[k], sem.at[0, k]) for k in range(n)]
        outs = [pltpu.make_async_copy(held[k], taken[k], sem.at[1, k]) for k in range(n)]
        for one in ins:
            one.start()
        for one, other in zip(ins, outs):
            one.wait()
            other.start()
        for one in outs:
            one.wait()

    results = pl.pallas_call(
        run,
        out_shape=tuple(shape(a.shape, a.dtype) for a in arrays.values()),
        in_specs=[free] * n,
        out_specs=(free,) * n,
        scratch_shapes=[pltpu.VMEM(a.shape, a.dtype) for a in arrays.values()]
        + [pltpu.SemaphoreType.DMA((2, n))],
    )(*arrays.values())
    return SimpleNamespace(**dict(zip(names, results)))


def solution(mesh):
    count = mesh.shape["win"]

    def shards(
        pixels, merge_gain, merge_shift, merge_weight, norm1_gain, norm1_shift, qkv_weight,
        qkv_bias, rel_table, proj_weight, proj_bias, norm2_gain, norm2_shift, fc1_weight,
        fc1_bias, fc2_weight, fc2_bias, rel_index, keep, cotangent,
    ):
        wins, height, _, channels = pixels.shape
        side = height // 2
        area = side * side
        rows = wins * PAD
        model = merge_weight.shape[1]
        half = model // 2
        heads = 2 * rel_table.shape[1]
        dim = half // rel_table.shape[1]
        hidden = fc1_weight.shape[1]

        def row(v):
            return v.reshape(1, -1)

        index = jnp.pad(rel_index.T, ((0, 0), (0, 128 - area)))
        kept = keep.reshape(2, 1, wins * area)
        kept_rows = jnp.pad(
            keep.reshape(2 * wins, area), ((0, 0), (0, PAD - area))
        ).reshape(2, 1, rows)
        wqkv = qkv_weight.transpose(1, 0, 2)
        a = front(
            dim, heads, area, wins,
            dict(
                mg=row(merge_gain), ms=row(merge_shift), n1g=row(norm1_gain),
                n1s=row(norm1_shift), pb=row(proj_bias), n2g=row(norm2_gain),
                n2s=row(norm2_shift), qb=qkv_bias, table=rel_table.T, index=index, keep=kept,
            ),
            dict(
                pixels=pixels.transpose(1, 2, 0, 3).reshape(side, 2, side, 2, wins, channels),
                wm=merge_weight, wqkv=wqkv, wp=proj_weight, cot=cotangent,
            ),
        )
        b = back(
            count, dim, heads, area, wins, rel_table.shape[0],
            dict(
                keep=kept_rows, b1=row(fc1_bias), b2=row(fc2_bias), nat=a.nat, mgo=a.mgo,
                lse=a.lse, index=index, gb2=a.gb2,
            ),
            dict(
                second=a.second, gf=a.gf, stream1=a.stream1, stream0=a.stream0,
                fc1=fc1_weight, fc2=fc2_weight, wp_own=proj_weight, wp_oth=a.wp_oth,
                wqkv_own=wqkv, wqkv_oth=a.wqkv_oth, wm_own=merge_weight, wm_oth=a.wm_oth,
                att_own=a.att_own, att_sib=a.att_sib, qkv=a.qkv, bias=a.bias,
                first_own=a.first_own, first_sib=a.first_sib, mn_own=a.mn_own, mn_sib=a.mn_sib,
                x=a.x,
            ),
        )
        f = hand_on(vars(b))

        def flat(v):
            return v.reshape(-1)

        pixels_grad = f.pixels_grad.reshape(height, height, wins, channels)
        return (
            f.out, pixels_grad.transpose(2, 0, 1, 3), flat(f.o_mg), flat(f.o_ms), f.o_merge.T,
            flat(f.o_n1g), flat(f.o_n1s), f.o_qkv.transpose(1, 0, 2), f.o_qb, f.o_rel.T,
            f.o_proj.T, flat(f.o_pb), flat(f.o_n2g), flat(f.o_n2s), f.o_fc1, flat(f.o_b1),
            f.o_fc2.T, flat(f.o_b2),
        )

    in_specs = (
        P(("win", "tp"), None, None, None), P("tp"), P("tp"), P("tp", None), P("tp"), P("tp"),
        P(None, None, "tp"), P(None, "tp"), P(None, "tp"), P("tp", None), P("tp"), P("tp"),
        P("tp"), P(None, "tp"), P("tp"), P("tp", None), P("tp"), P(), P("win"), P("win", "tp"),
    )
    out_specs = (
        P("win", "tp"), P(("win", "tp"), None, None, None), P("tp"), P("tp"), P("tp", "win"),
        P("tp"), P("tp"), P("win", None, "tp"), P(None, "tp"), P(None, "tp"), P("tp", "win"),
        P("tp"), P("tp"), P("tp"), P("win", "tp"), P("tp"), P("tp", "win"), P("tp"),
    )
    return jax.shard_map(shards, mesh=mesh, in_specs=in_specs, out_specs=out_specs, check_vma=False)
```

```python
from types import SimpleNamespace

import jax
import jax.numpy as jnp
from jax import lax
from jax.experimental import pallas as pl
from jax.experimental.pallas import tpu as pltpu
from jax.sharding import PartitionSpec as P

EPS = 1e-05
F32 = jnp.float32
BF16 = jnp.bfloat16
MESH = pl.DeviceIdType.MESH
PAD = 112
LIMIT = 63 * 1024 * 1024


def shape(dims, dtype=F32):
    return jax.ShapeDtypeStruct(tuple(dims), dtype)


def kernel_call(body, small, large, outs, scratch, large_outs, collective=None):
    names = [*small, *large, *outs, *scratch]
    free, vmem = pl.BlockSpec(memory_space=pl.ANY), pl.BlockSpec(memory_space=pltpu.VMEM)
    more = {} if collective is None else dict(collective_id=collective, has_side_effects=True)

    def run(*refs):
        body(SimpleNamespace(**dict(zip(names, refs, strict=True))))

    results = pl.pallas_call(
        run,
        out_shape=tuple(outs.values()),
        in_specs=[vmem] * len(small) + [free] * len(large),
        out_specs=tuple(free if n in large_outs else vmem for n in outs),
        scratch_shapes=list(scratch.values()),
        compiler_params=pltpu.CompilerParams(vmem_limit_bytes=LIMIT, **more),
    )(*small.values(), *large.values())
    return SimpleNamespace(**dict(zip(outs, results)))


def dot(a, b):
    return jnp.dot(a, b, preferred_element_type=F32)


def dot_nt(a, b):
    return lax.dot_general(a, b, (((1,), (1,)), ((), ())), preferred_element_type=F32)


def dot_tn(a, b):
    return lax.dot_general(a, b, (((0,), (0,)), ((), ())), preferred_element_type=F32)


def stats(x, width):
    mean = jnp.sum(x, 1, keepdims=True) * (1.0 / width)
    second = jnp.sum(x * x, 1, keepdims=True) * (1.0 / width)
    return mean, lax.rsqrt(second - mean * mean + EPS)


def norm_back(e, x, gain, width):
    mean, scale = stats(x, width)
    xhat = (x - mean) * scale
    scaled = e * gain
    first = jnp.sum(scaled, 1, keepdims=True) * (1.0 / width)
    cross = jnp.sum(scaled * xhat, 1, keepdims=True) * (1.0 / width)
    return scale * (scaled - first - xhat * cross), e * xhat


def steps(total, size, fn):
    @pl.loop(0, total // size)
    def _(step):
        fn(pl.ds(pl.multiple_of(step * size, size), size))


def add_to(ref, row, value):
    ref[row : row + 1, :] += jnp.sum(value, 0, keepdims=True)


def spread(rows, tokens, windows):
    row = lax.broadcasted_iota(jnp.int32, (rows, tokens), 0)
    col = lax.broadcasted_iota(jnp.int32, (rows, tokens), 1)
    area = tokens // windows
    w = row // PAD
    k = row - w * PAD
    real = k < area
    return (
        jnp.logical_and(real, w * area + k == col),
        jnp.logical_and(real, k * windows + w == col),
    )


def gather_rows(rows, tokens, windows):
    row = lax.broadcasted_iota(jnp.int32, (tokens, rows), 1)
    col = lax.broadcasted_iota(jnp.int32, (tokens, rows), 0)
    area = tokens // windows
    w = row // PAD
    k = row - w * PAD
    real = k < area
    return (
        jnp.logical_and(real, w * area + k == col),
        jnp.logical_and(real, k * windows + w == col),
    )


def ones(mask):
    return jnp.where(mask, 1.0, 0.0).astype(BF16)


class Link:
    def __init__(self, sends, recvs):
        self.sends, self.recvs = sends, recvs

    def copy(self, k, src, dst):
        return pltpu.make_async_remote_copy(
            src_ref=src,
            dst_ref=dst,
            send_sem=self.sends.at[k],
            recv_sem=self.recvs.at[k],
            device_id=(lax.axis_index("win"), 1 - lax.axis_index("tp")),
            device_id_type=MESH,
        )


def head_masks(rows, width, dim):
    lane = lax.broadcasted_iota(jnp.int32, (rows, width), 1) // dim
    return [lane == h for h in range(width // dim)]


def stacked(block, masks):
    return jnp.concatenate([jnp.where(m, block, 0.0).astype(BF16) for m in masks], 0)


def diagonal(a, b):
    zero = jnp.zeros((PAD, 128), BF16)
    rest = jnp.zeros((128 - PAD, 256), BF16)
    return jnp.concatenate(
        [jnp.concatenate([a, zero], 1), rest, jnp.concatenate([zero, b], 1), rest], 0
    )


def bias_of(bias, heads, g, per):
    first = lax.rem(g * per + lax.axis_index("tp") * (heads // 2), heads)
    return [bias[pl.ds(first + h, PAD, stride=heads), :] for h in range(per)]


def attention_forward(dim, heads, g, r):
    per = 128 // dim
    windows = r.qkvb.shape[1] // PAD
    scale = dim ** (-0.5)
    masks = head_masks(PAD, 128, dim)
    lanes = pl.ds(pl.multiple_of(g * 128, 128), 128)
    bias = bias_of(r.biasb, heads, g, per)
    done, sums = [], []
    for w in range(0, windows, 2):
        at = [pl.ds((w + u) * PAD, PAD) for u in range(2)]
        q, k, v = ([r.qkvb[s, a, lanes] for a in at] for s in range(3))
        both = dot_nt(
            jnp.concatenate([stacked(k[0], masks), stacked(k[1], masks)], 1),
            diagonal(q[0], q[1]),
        )
        for u in range(2):
            parts = []
            for h in range(per):
                s = both[h * PAD : (h + 1) * PAD, u * 128 : (u + 1) * 128] * scale + bias[h]
                top = jnp.max(s, 0, keepdims=True)
                e = jnp.exp(s - top)
                total = jnp.sum(e, 0, keepdims=True)
                parts.append((e * (1.0 / total)).astype(BF16))
                sums.append(top + jnp.log(total))
            value = dot_tn(jnp.concatenate(parts, 0), stacked(v[u], masks))
            done.append(value[:PAD].astype(BF16))
    for w in range(windows):
        r.attb[pl.ds(w * PAD, PAD), lanes] = done[w]
    r.lse[g] = jnp.concatenate(sums, 0)


def attention_back(dim, heads, g, r):
    per = 128 // dim
    windows = r.qkvb.shape[1] // PAD
    scale = dim ** (-0.5)
    masks = head_masks(PAD, 128, dim)
    lanes = pl.ds(pl.multiple_of(g * 128, 128), 128)
    bias = bias_of(r.biasb, heads, g, per)
    totals, done = [None] * per, []
    for w in range(windows):
        at = pl.ds(w * PAD, PAD)
        q, k, v = r.qkvb[0, at, lanes], r.qkvb[1, at, lanes], r.qkvb[2, at, lanes]
        go = r.ex[0, at, lanes]
        both = dot_nt(
            jnp.concatenate([stacked(k, masks), stacked(v, masks)], 1), diagonal(q, go)
        )
        kt = k.T
        p_parts, g_parts, dqs = [], [], []
        for h in range(per):
            here = slice(h * PAD, (h + 1) * PAD)
            p = jnp.exp(
                both[here, :128] * scale + bias[h] - r.lse[g, pl.ds(w * per + h, 1), :]
            )
            dp = both[here, 128:]
            gs = (p * (dp - jnp.sum(dp * p, 0, keepdims=True))).astype(BF16)
            wide = gs.astype(F32)
            totals[h] = wide if w == 0 else totals[h] + wide
            p_parts.append(p.astype(BF16))
            g_parts.append(gs)
            dqs.append(dot(kt[h * dim : (h + 1) * dim], gs))
        back = dot(
            jnp.concatenate([jnp.concatenate(p_parts, 0), jnp.concatenate(g_parts, 0)], 1),
            diagonal(go, q),
        )
        dv, dk = back[:PAD, :128], back[:PAD, 128:]
        for h in range(1, per):
            here = slice(h * PAD, (h + 1) * PAD)
            dv = jnp.where(masks[h], back[here, :128], dv)
            dk = jnp.where(masks[h], back[here, 128:], dk)
        dq = jnp.concatenate(dqs, 0).T[:PAD] * scale
        done.append((dq.astype(BF16), (dk * scale).astype(BF16), dv.astype(BF16)))
    q_sum = jnp.zeros((1, 128), F32)
    v_sum = jnp.zeros((1, 128), F32)
    for w in range(windows):
        for s in range(3):
            r.qkvb[s, pl.ds(w * PAD, PAD), lanes] = done[w][s]
        q_sum += jnp.sum(done[w][0].astype(F32), 0, keepdims=True)
        v_sum += jnp.sum(done[w][2].astype(F32), 0, keepdims=True)
    for h in range(per):
        r.sums[pl.ds(g * per + h, PAD, stride=heads), :] = totals[h]
    r.vq[0:1, lanes] = q_sum
    r.vq[1:2, lanes] = v_sum


PAIRS = 4


def onehot_of(index, first, entries):
    rows = [index[pl.ds(first + u, 1), :] for u in range(PAIRS)]
    ids = lax.broadcasted_iota(jnp.int32, (entries, rows[0].shape[1]), 0)
    return jnp.concatenate([ones(ids == row) for row in rows], 1)


def bias_spread(first, count, heads, table, index, out):
    entries = table.shape[1]
    top = table.astype(BF16)
    both = jnp.concatenate([top, (table - top.astype(F32)).astype(BF16)], 0)

    @pl.loop(0, count)
    def _(k):
        i = first + k
        value = dot(both, onehot_of(index, i * PAIRS, entries))
        value = value[:heads] + value[heads:]
        for u in range(PAIRS):
            at = pl.ds(pl.multiple_of((i * PAIRS + u) * heads, heads), heads)
            out[at, :] = value[:, u * 128 : (u + 1) * 128]


def rel_sum(first, last, heads, index, sums, rel):
    entries = rel.shape[1]

    @pl.loop(first, last)
    def _(i):
        hot = onehot_of(index, i * PAIRS, entries)
        s = jnp.concatenate(
            [
                sums[pl.ds(pl.multiple_of((i * PAIRS + u) * heads, heads), heads), :]
                for u in range(PAIRS)
            ],
            1,
        )
        top = s.astype(BF16)
        low = (s - top.astype(F32)).astype(BF16)
        both = dot_nt(jnp.concatenate([top, low], 0), hot)
        rel[...] += both[:heads] + both[heads:]


def win_bits(count):
    total = count.bit_length() - 1
    side = 1
    while 4 * (side + 1) * (side + 1) <= count:
        side += 1
    wide = side.bit_length() - 1
    axes = [range(wide), range(wide, 2 * wide), range(2 * wide, total)]
    near = [axis[0] for axis in axes if len(axis)]
    far = [bit for axis in axes for bit in axis[1:]]
    return near, far


TURNS = (((0,1,2,3),(1,0,2,3),(2,0,1,3),(0,2,1,3),(1,2,0,3),(2,1,0,3),(0,1,2,3),(1,0,2,3),(2,0,1,3),(0,1,2,3),(1,0,2,3),(2,1,0,3),(0,1,2,3),(0,1,2,3),(1,0,2,3),(1,0,2,3)))


def orders_of(count):
    near, far = win_bits(count)
    axes = [*near, *reversed(far)]
    return [(*[axes[k] for k in turn], *axes[4:]) for turn in TURNS]


def my_bit(bit):
    return lax.rem(lax.div(lax.axis_index("win"), 1 << bit), 2)


def partner(bit):
    return lax.axis_index("win") + (1 - 2 * my_bit(bit)) * (1 << bit), lax.axis_index("tp")


def enter(bits):
    barrier = pltpu.get_barrier_semaphore()
    peers = [(lax.axis_index("win"), 1 - lax.axis_index("tp"))]
    peers += [partner(bit) for bit in range(bits)]
    for peer in peers:
        pl.semaphore_signal(barrier, inc=1, device_id=peer, device_id_type=MESH)
    pl.semaphore_wait(barrier, len(peers))


class Scatter:
    def __init__(self, order, held, sends, recvs, unit):
        self.order, self.held = order, held
        self.sends, self.recvs, self.unit = sends, recvs, unit

    def pick(self, step, value):
        left = [b for b in range(len(self.order)) if b not in self.order[:step]]
        dim = len(left) - 1 - left.index(self.order[step])
        return self.held[step].at[(*([slice(None)] * dim), value)]

    def copy(self, step):
        bit = self.order[step]
        return pltpu.make_async_remote_copy(
            src_ref=self.pick(step, 1 - my_bit(bit)),
            dst_ref=self.held[step + 1],
            send_sem=self.sends.at[self.unit, step],
            recv_sem=self.recvs.at[self.unit, step],
            device_id=partner(bit),
            device_id_type=MESH,
        )

    def finish(self, step, out=None):
        self.copy(step).wait_recv()
        mine = self.pick(step, my_bit(self.order[step]))
        got = self.held[step + 1]
        lead = got.shape[:-2]
        if not lead:
            out[...] = mine[...].astype(F32) + got[...].astype(F32)
            return

        @pl.loop(0, 1 << len(lead))
        def _(i):
            at = tuple(lax.rem(lax.div(i, 1 << k), 2) for k in reversed(range(len(lead))))
            got[at] = (mine[at].astype(F32) + got[at].astype(F32)).astype(BF16)

        self.copy(step + 1).start()


def front_body(dim, heads, area, r):
    enter(0)
    t = lax.axis_index("tp")
    who = (t, 1 - t)
    rows, model = r.firstb.shape
    half = model // 2
    windows = rows // PAD
    tokens = windows * area
    link = Link(r.xsend, r.xrecv)
    own_cols = pl.ds(pl.multiple_of(t * half, half), half)
    oth_cols = pl.ds(pl.multiple_of((1 - t) * half, half), half)

    def load(k, src, dst):
        return pltpu.make_async_copy(src, dst, r.lsem.at[k])

    c_wm = link.copy(0, r.wm, r.wmb.at[1])
    c_wm.start()
    loads = [load(k, r.pixels.at[:, k % 2, :, k // 2], r.pix.at[k]) for k in range(4)]
    loads += [load(4, r.cot, r.cotb.at[0]), load(5, r.wm, r.wmb.at[0])]
    for one in loads:
        one.start()
    vx = r.vx
    vx[0] = jnp.zeros(vx.shape[1:], F32)
    for k, ref in enumerate((r.mg, r.ms)):
        for j in range(2):
            vx[0, 2 * k + j : 2 * k + j + 1, :] = ref[:, j * half : (j + 1) * half]
    for k, ref in enumerate((r.n1g, r.n1s, r.pb, r.n2g, r.n2s)):
        vx[0, 4 + k : 5 + k, :] = ref[...]
    vx[0, 9:11, :] = r.qb[...]
    vx[0, 16 : 16 + heads // 2, 0 : r.table.shape[1]] = r.table[...]
    c_vec = link.copy(1, vx.at[0], vx.at[1])
    c_vec.start()
    c_wq = link.copy(3, r.wqkv, r.wqb.at[1])
    c_wq.start()
    late = [load(6, r.wqkv, r.wqb.at[0]), load(7, r.wp, r.wpb.at[pl.ds(0, half), :])]
    for one in late:
        one.start()
    stores = []

    def store(src, dst):
        one = pltpu.make_async_copy(src, dst, r.ssem.at[len(stores)])
        stores.append(one)
        one.start()

    token_rows, pixel_rows = spread(rows, tokens, windows)
    pixel_rows = ones(pixel_rows)
    kept = r.keep[...].astype(F32).reshape(1, 2 * tokens)
    kept = (kept[:, :tokens], kept[:, tokens:])
    for side in range(2):
        wide = jnp.broadcast_to(kept[side], (8, tokens)).astype(BF16)
        r.kept_rows[side] = dot_nt(wide, ones(token_rows))
    r.square[...] = jnp.zeros_like(r.square)
    r.square[0:area, 0:area] = r.rel_index[...].astype(F32)
    r.index[...] = r.square[...].T.astype(jnp.int32)
    for k in range(4):
        loads[k].wait()
        r.xb[k] = dot(
            pixel_rows, r.pix[k].astype(F32).reshape(tokens, half).astype(BF16)
        ).astype(BF16)
    store(r.xb, r.x)

    c_vec.wait()
    mgo, nat = r.mgo, r.nat
    for side in range(2):
        for j in range(2):
            mgo[side, :, j * half : (j + 1) * half] = vx[side, j : j + 1, :]
            r.mso[side, :, j * half : (j + 1) * half] = vx[side, 2 + j : 3 + j, :]
        nat[0:5, (own_cols, oth_cols)[side]] = vx[side, 4:9, :]
    width = 2 * model

    def norm0(at):
        xs = [
            [r.xb[2 * who[i] + j, at, :].astype(F32) for j in range(2)] for i in range(2)
        ]

        def both(fn):
            return sum(jnp.sum(fn(x), 1, keepdims=True) for pair in xs for x in pair)

        mean = both(lambda x: x) * (1.0 / width)
        scale = lax.rsqrt(both(lambda x: x * x) * (1.0 / width) - mean * mean + EPS)
        for i in range(2):
            for j in range(2):
                cols = pl.ds(j * half, half)
                value = (xs[i][j] - mean) * scale * mgo[i, :, cols] + r.mso[i, :, cols]
                r.mnb[i, at, cols] = value.astype(BF16)

    steps(rows, 64, norm0)
    store(r.mnb.at[0], r.mn_own)

    entries = r.tableb.shape[1]
    for side in range(2):
        at = pl.ds(pl.multiple_of(who[side] * (heads // 2), heads // 2), heads // 2)
        r.tableb[at, :] = vx[side, 16 : 16 + heads // 2, 0:entries]
    turns = area // PAIRS
    share = turns // 2 + 1
    bias_spread(t * (turns - share), share, heads, r.tableb[...], r.index, r.biasb)
    size = (turns - share) * PAIRS * heads
    at = pl.ds(pl.multiple_of(t * share * PAIRS * heads, PAIRS * heads), size)
    c_bias = link.copy(8, r.biasb.at[at, :], r.biasb.at[at, :])
    c_bias.start()
    r.biasb[pl.ds(area * heads, (PAD - area) * heads), :] = jnp.full(
        ((PAD - area) * heads, 128), -1e30, F32
    )
    c_cot = link.copy(2, r.cot, r.cotb.at[1])
    c_cot.start()
    c_wp = link.copy(4, r.wp, r.wpb.at[pl.ds(half, half), :])
    c_wp.start()
    c_mn = link.copy(6, r.mnb.at[1], r.mn_sib)
    c_mn.start()

    loads[5].wait()

    def own_part(at):
        r.s0b[:, at] = dot(r.mnb[0], r.wmb[0, :, at])

    steps(model, 512, own_part)
    c_wm.wait()
    store(r.wmb.at[1], r.wm_oth)

    def oth_part(at):
        r.s0b[:, at] += dot(r.mnb[1], r.wmb[1, :, at])

    steps(model, 512, oth_part)
    store(r.s0b, r.stream0)

    def norm1(at):
        x = r.s0b[at, :]
        mean, scale = stats(x, model)
        r.firstb[at, :] = ((x - mean) * scale * nat[0:1, :] + nat[1:2, :]).astype(BF16)

    steps(rows, 112, norm1)
    c_first = link.copy(5, r.firstb, r.first_sib)
    c_first.start()
    store(r.firstb, r.first_own)

    late[0].wait()
    for side in range(2):
        if side == 1:
            c_wq.wait()
            store(r.wqb.at[1], r.wqkv_oth)
        for s in range(3):
            cols = pl.ds(side * half, half)
            value = dot(r.firstb[...], r.wqb[side, s])
            if s != 1:
                value += vx[side, 9 + s // 2 : 10 + s // 2, :]
            r.qkvb[s, :, cols] = value.astype(BF16)
    store(r.qkvb, r.qkv)

    c_bias.wait()
    store(r.biasb, r.bias)

    @pl.loop(0, model // 128, unroll=2)
    def _(g):
        attention_forward(dim, heads, g, r)

    c_att = link.copy(7, r.attb.at[:, pl.ds(half, half)], r.att_sib)
    c_att.start()
    store(r.attb.at[:, pl.ds(0, half)], r.att_own)

    late[1].wait()
    c_wp.wait()
    store(r.wpb.at[pl.ds(half, half), :], r.wp_oth)

    def project(at):
        value = dot(r.attb[...], r.wpb[:, at]) + nat[2:3, at]
        r.s1b[:, at] = r.s0b[:, at] + value

    steps(model, 512, project)
    store(r.s1b, r.stream1)

    def norm2(at):
        x = r.s1b[at, :]
        mean, scale = stats(x, model)
        r.secb[at, :] = ((x - mean) * scale * nat[3:4, :] + nat[4:5, :]).astype(BF16)

    steps(rows, 112, norm2)
    c_sec = link.copy(9, r.secb, r.second_sib)
    c_sec.start()
    store(r.secb, r.second)

    loads[4].wait()
    c_cot.wait()
    total = jnp.zeros((1, half), F32)
    for side in range(2):
        at = pl.ds(pl.multiple_of(who[side] * tokens, tokens), tokens)
        pick = ones(jnp.logical_and(token_rows, jnp.where(who[side] == 0, kept[0], kept[1]) > 0))
        mine = dot(pick, r.cotb[0, at, :])
        total += jnp.sum(mine, 0, keepdims=True)
        here = pl.ds(side * rows, rows)
        r.gfb[here, own_cols] = mine.astype(BF16)
        r.gfb[here, oth_cols] = dot(pick, r.cotb[1, at, :]).astype(BF16)
    r.gb2[...] = total
    store(r.gfb, r.gf)
    for one in (c_mn, c_first, c_att, c_sec):
        one.wait()
    for one in stores:
        one.wait()


def front(dim, heads, area, windows, small, large):
    rows, tokens = windows * PAD, windows * area
    model = large["wm"].shape[1]
    half = model // 2
    side = large["pixels"].shape[0:3:2]
    slots = -(-small["table"].shape[1] // 128) * 128
    vm, dma = pltpu.VMEM, pltpu.SemaphoreType.DMA
    big = dict(
        x=shape((4, rows, half), BF16), gf=shape((2 * rows, model), BF16),
        stream0=shape((rows, model)), stream1=shape((rows, model)),
        second=shape((rows, model), BF16), second_sib=shape((rows, model), BF16), qkv=shape((3, rows, model), BF16),
        bias=shape((PAD * heads, 128)), first_own=shape((rows, model), BF16),
        first_sib=shape((rows, model), BF16), mn_own=shape((rows, model), BF16),
        mn_sib=shape((rows, model), BF16), att_own=shape((rows, half), BF16),
        att_sib=shape((rows, half), BF16), wm_oth=shape((model, model), BF16),
        wqkv_oth=shape((3, model, half), BF16), wp_oth=shape((half, model), BF16),
    )
    outs = dict(
        big, gb2=shape((1, half)), nat=shape((8, model)), mgo=shape((2, 1, model)),
        lse=shape((model // 128, windows * 128 // dim, 128)),
        kept_rows=shape((2, 8, rows)), index=shape((128, 128), jnp.int32),
    )
    scratch = dict(
        wmb=vm((2, model, model), BF16), wqb=vm((2, 3, model, half), BF16),
        wpb=vm((model, model), BF16), pix=vm((4, *side, windows, half), BF16),
        xb=vm((4, rows, half), BF16), cotb=vm((2, 2 * tokens, half), BF16),
        gfb=vm((2 * rows, model), BF16), mnb=vm((2, rows, model), BF16),
        s0b=vm((rows, model), F32), s1b=vm((rows, model), F32), firstb=vm((rows, model), BF16),
        qkvb=vm((3, rows, model), BF16), biasb=vm((PAD * heads, 128), F32),
        attb=vm((rows, model), BF16), secb=vm((rows, model), BF16),
        vx=vm((2, 32, half), F32), mso=vm((2, 1, model), F32), tableb=vm((heads, slots), F32),
        square=vm((128, 128), F32),
        lsem=dma((8,)), ssem=dma((16,)), xsend=dma((10,)), xrecv=dma((10,)),
    )

    def body(r):
        front_body(dim, heads, area, r)

    return kernel_call(body, small, large, outs, scratch, big, collective=2)


CHUNK = 512
PLAN = {
    3: ((0, 0), (1, 0)),
    8: ((2, 0),),
    11: ((3, 0),),
    12: ((4, 0),),
    15: ((5, 0),),
    17: ((6, 0),),
    18: ((3, 1), (7, 0)),
    20: ((1, 1),),
    21: ((2, 1),),
    22: ((8, 0),),
    23: ((5, 1),),
    26: ((7, 1),),
    27: ((4, 1),),
    28: ((0, 1),),
    31: ((6, 1), (1, 2), (3, 2), (0, 2)),
    33: ((9, 0),),
    35: ((10, 0), (8, 1), (11, 0), (2, 2), (5, 2), (7, 2), (4, 2)),
    36: ((6, 2), (14, 0)),
    37: ((1, 3), (12, 0), (3, 3)),
    38: ((15, 0),),
    39: ((0, 3),),
    40: (
        (13, 0), (2, 3), (-1, 0), (9, 1), (5, 3), (-1, 1),
        (8, 2), (10, 1), (-1, 2), (7, 3), (14, 1), (-1, 3),
        (4, 3), (11, 1), (-1, 4), (15, 1), (6, 3), (12, 1),
        (9, 2), (11, 2), (13, 1), (8, 3), (10, 2), (14, 2),
        (15, 2), (12, 2), (9, 3), (11, 3), (13, 2), (10, 3),
        (14, 3), (15, 3), (12, 3), (13, 3),
    ),
}


def back_body(bits, orders, dim, heads, area, r):
    n_units = len(orders)
    t = lax.axis_index("tp")
    who = (t, 1 - t)
    sec, gf, facc, gacc, st, ex = r.sec, r.gfb, r.facc, r.gacc, r.st, r.ex
    w1b, w2b, cotb, qkvb = r.w1b, r.w2b, r.cotb, r.qkvb
    rows, model = st.shape
    half = model // 2
    hidden = r.fc1.shape[1]
    chunks = hidden // CHUNK
    windows = rows // PAD
    tokens = windows * area
    mine, theirs = pl.ds(0, rows), pl.ds(rows, rows)
    left, right = pl.ds(0, half), pl.ds(half, half)
    link = Link(r.xsend, r.xrecv)
    own_cols = pl.ds(pl.multiple_of(t * half, half), half)
    oth_cols = pl.ds(pl.multiple_of((1 - t) * half, half), half)
    part = model // (1 << bits)

    def load(k, src, dst):
        return pltpu.make_async_copy(src, dst, r.lsem.at[k])

    whole_units = 2 * chunks + 4

    def place_of(u):
        if u < whole_units:
            return u, pl.ds(0, CHUNK)
        u -= whole_units
        return whole_units + u // 2, pl.ds(u % 2 * (CHUNK // 2), CHUNK // 2)

    def unit(u):
        block, cols = place_of(u)
        lead = tuple([slice(None)] * bits)
        held = [r.src.at[(block % 8, *lead, slice(None), cols)]]
        for k, buf in enumerate(r.bufs):
            held.append(buf.at[(block, *lead[k + 1 :], slice(None), cols)])
        return Scatter(orders[u], held, r.rsend, r.rrecv, u)

    def put(block, value):
        if block >= 8:
            unit(block - 8).copy(0).wait_send()
        r.src[block % 8] = value.astype(BF16).reshape(*([2] * bits), part, CHUNK)
        for u in range(n_units):
            if place_of(u)[0] == block:
                unit(u).copy(0).start()

    def held(u):
        block, cols = place_of(u)
        at = pl.ds(block % 2 * CHUNK + cols.start, cols.size)
        return st.at[block // 2 * part : (block // 2 + 1) * part, at]

    def result(u):
        if u < 2 * chunks:
            return (r.o_fc1, r.o_fc2)[u % 2].at[:, pl.ds(u // 2 * CHUNK, CHUNK)]
        u -= 2 * chunks
        if u == 0:
            return r.o_proj
        if u < 4:
            return r.o_qkv.at[u - 1]
        return r.o_merge.at[:, pl.ds((u - 4) * (CHUNK // 2), CHUNK // 2)]

    last_step = bits - 1
    copies = [
        pltpu.make_async_remote_copy(
            src_ref=r.vs.at[bit],
            dst_ref=r.vbuf.at[bit],
            send_sem=r.vsend.at[bit],
            recv_sem=r.vrecv.at[bit],
            device_id=partner(bit),
            device_id_type=MESH,
        )
        for bit in range(bits)
    ]

    def vectors(step):
        if step == 0:
            link.copy(6, r.vx.at[0], r.vx.at[1]).wait()
            r.vs[0] += r.vx[1]
        else:
            copies[step - 1].wait()
            r.vs[step] = r.vs[step - 1] + r.vbuf[step - 1]
        if step < bits:
            copies[step].start()

    def pump(place):
        for u, step in PLAN.get(place, ()):
            if u < 0:
                vectors(step)
                continue
            unit(u).finish(step, held(u))
            if step == last_step:
                write(u).start()

    def write(u):
        return pltpu.make_async_copy(held(u), result(u), r.osem.at[u])

    loads = [load(0, r.second, sec.at[mine]), load(2, r.second_sib, sec.at[theirs])]
    for one in loads:
        one.start()

    def weights(c):
        slot = lax.rem(c, 2)
        cols = pl.ds(pl.multiple_of(c * CHUNK, CHUNK), CHUNK)
        return (
            pltpu.make_async_copy(r.fc1.at[:, cols], w1b.at[slot], r.wsem.at[0, slot]),
            pltpu.make_async_copy(r.fc2.at[cols, :], w2b.at[slot], r.wsem.at[1, slot]),
        )

    for one in weights(0):
        one.start()
    late = [load(1, r.gf, gf), load(3, r.stream1, st), load(4, r.qkv, qkvb)]
    for one in late:
        one.start()
    enter(bits)
    for one in (*loads, late[0]):
        one.wait()

    blocks = CHUNK // 128
    hid, dact, act, gh = r.sums, r.biasb, r.act, r.gh

    def save(c):
        return load(13, act, r.acts.at[c])

    @pl.loop(0, chunks)
    def _(c):
        slot = lax.rem(c, 2)
        for one in weights(c):
            one.wait()

        @pl.when(c + 1 < chunks)
        def _():
            for one in weights(c + 1):
                one.start()

        of = pl.ds(pl.multiple_of(c * CHUNK, CHUNK), CHUNK)
        value = dot(sec[...], w1b[slot]) + r.b1[:, of]
        for b in range(blocks):
            hid[b * 2 * rows : (b + 1) * 2 * rows, :] = value[:, b * 128 : (b + 1) * 128]
        value = dot_nt(gf[...], w2b[slot])
        for b in range(blocks):
            dact[b * 2 * rows : (b + 1) * 2 * rows, :] = value[:, b * 128 : (b + 1) * 128]
        @pl.when(c > 0)
        def _():
            save(c - 1).wait()

        for b in range(blocks):
            lanes = pl.ds(b * 128, 128)

            def gelu(at):
                here = pl.ds(pl.multiple_of(b * 2 * rows + at.start, 128), at.size)
                x = hid[here, :]
                cdf = 0.5 * (1.0 + lax.erf(x * 0.7071067811865476))
                pdf = jnp.exp(x * x * -0.5) * 0.3989422804014327
                act[at, lanes] = (x * cdf).astype(BF16)
                gh[at, lanes] = (dact[here, :] * (cdf + x * pdf)).astype(BF16)

            steps(2 * rows, 128, gelu)
        save(c).start()
        r.gb1[:, of] = jnp.sum(gh[...].astype(F32), 0, keepdims=True)
        for k, value in enumerate((dot_tn(sec[...], gh[...]), dot_tn(gf[...], act[...]))):
            r.src[2 * c + k] = value.astype(BF16).reshape(*([2] * bits), part, CHUNK)
            for j in range(chunks):

                @pl.when(c == j)
                def _():
                    unit(2 * j + k).copy(0).start()

        for j in range(chunks):

            @pl.when(c == j)
            def _():
                pump(j)

        @pl.when(c == 0)
        def _():
            gacc[...] = dot_nt(gh[...], w1b[slot])

        @pl.when(c > 0)
        def _():
            gacc[...] += dot_nt(gh[...], w1b[slot])

        for j in range(chunks):

            @pl.when(c == j)
            def _():
                pump(chunks + j)

    load(5, r.bias, r.biasb).start()
    save(chunks - 1).wait()
    load(6, r.att_own, act.at[mine]).start()
    load(7, r.att_sib, act.at[theirs]).start()
    for k, src in enumerate((r.wp_own, r.wp_oth)):
        load(8 + k, src, w2b.at[k]).start()
    ex[0] = gacc[theirs].astype(BF16)
    c_g2 = link.copy(1, ex.at[0], ex.at[1])
    c_g2.start()
    load(3, r.stream1, st).wait()
    pump(8)
    v2 = r.v2
    v2[...] = jnp.zeros_like(v2)
    c_g2.wait()

    def norm2(at):
        e = gacc[at, :] + ex[1, at, :].astype(F32)
        dv, hat = norm_back(e, st[at, :], r.nat[3:4, :], model)
        d = gf[at, :].astype(F32) + dv
        gacc[at, :] = d
        low = d.astype(BF16)
        sec[at, :] = low
        add_to(v2, 0, hat)
        add_to(v2, 1, e)
        add_to(v2, 2, low.astype(F32))

    steps(rows, 112, norm2)
    c_att = link.copy(3, sec.at[mine], sec.at[theirs])
    c_att.start()
    load(10, r.first_own, gf.at[mine]).start()
    load(11, r.first_sib, gf.at[theirs]).start()
    pump(9)
    pump(10)
    for k, src in enumerate((r.wp_own, r.wp_oth)):
        load(8 + k, src, w2b.at[k]).wait()
        ex[0, :, (left, right)[k]] = dot_nt(sec[mine, :], w2b[k]).astype(BF16)

    pump(11)

    first_unit = 2 * chunks
    u_proj, u_qkv = first_unit, first_unit + 1
    u_merge = first_unit + 4
    load(6, r.att_own, act.at[mine]).wait()
    load(7, r.att_sib, act.at[theirs]).wait()
    c_att.wait()
    put(u_proj, dot_tn(sec[...], act[...]))
    pump(12)

    s0 = facc.at[theirs]
    load(12, r.stream0, s0).start()
    load(4, r.qkv, qkvb).wait()
    load(5, r.bias, r.biasb).wait()

    dland = cotb.at[pl.ds(0, 3)]
    c_qkv = link.copy(4, qkvb.at[:, :, right], dland)
    groups = model // 128

    @pl.loop(0, groups)
    def _(g):
        attention_back(dim, heads, lax.rem(g + groups // 2, groups), r)

        @pl.when(g == groups // 2 - 1)
        def _():
            c_qkv.start()


        for k in range(8):

            @pl.when(g == k)
            def _():
                pump(13 + k)

    def slice_of(k):
        return (r.wqkv_own, r.wqkv_oth)[k // 3].at[k % 3]

    load(16, slice_of(0), w1b.at[0]).start()

    load(10, r.first_own, gf.at[mine]).wait()
    load(11, r.first_sib, gf.at[theirs]).wait()
    c_qkv.wait()
    for s in range(3):
        put(u_qkv + s, dot_tn(gf[mine, :], qkvb[s, :, left]) + dot_tn(gf[theirs, :], dland[s]))
        pump(28 + s)
    load(10, r.mn_own, gf.at[mine]).start()
    load(11, r.mn_sib, gf.at[theirs]).start()

    kept = (act, gh)

    def feed_loads(c):
        slot = c % 2
        rows_of = pl.ds(c * CHUNK, CHUNK)
        return (
            load(18 + slot, r.acts.at[c], kept[slot]),
            load(20 + slot, r.fc2.at[rows_of, :], w2b.at[slot]),
        )

    def feed(c):
        for one in feed_loads(c):
            one.wait()
        value = dot(kept[c % 2][...], w2b[c % 2])
        if c == 0:
            facc[...] = value
        else:
            facc[...] += value
        if c + 2 < chunks:
            for one in feed_loads(c + 2):
                one.start()

    for c in range(2):
        for one in feed_loads(c):
            one.start()

    for k in range(6):
        load(16 + k % 2, slice_of(k), w1b.at[k % 2]).wait()
        if k + 1 < 6:
            load(16 + (k + 1) % 2, slice_of(k + 1), w1b.at[(k + 1) % 2]).start()
        value = dot_nt(qkvb[k % 3, :, (left, right)[k // 3]], w1b[k % 2])
        if k == 0:
            gacc[theirs, :] = value
        else:
            gacc[theirs, :] += value
        pump(21 + k)
    load(12, r.stream0, s0).wait()
    v1 = r.v1
    v1[...] = jnp.zeros_like(v1)

    def norm1(at):
        e = gacc[pl.ds(pl.multiple_of(rows + at.start, 16), at.size), :]
        dv, hat = norm_back(e, s0[at, :], r.nat[0:1, :], model)
        sec[at, :] = (gacc[at, :] + dv).astype(BF16)
        add_to(v1, 0, hat)
        add_to(v1, 1, e)

    steps(rows, 112, norm1)
    c_s0 = link.copy(5, sec.at[mine], ex.at[1])
    c_s0.start()
    again = gacc.at[theirs]
    load(22, r.stream1, again).start()
    pump(27)
    feed(0)
    feed(1)

    c_s0.wait()
    load(10, r.mn_own, gf.at[mine]).wait()
    load(11, r.mn_sib, gf.at[theirs]).wait()
    for k in range(2):
        cols = (left, right)[k]
        put(u_merge + k, dot_tn(sec[mine, :], gf[mine, cols]) + dot_tn(ex[1], gf[theirs, cols]))
        pump(31 + k)

    for c in range(2, chunks):
        feed(c)
    for k in range(2):
        load(8 + k, r.wm_own.at[(left, right)[k], :], w2b.at[k]).start()
    load(22, r.stream1, again).wait()
    fsend, fland = gh, cotb.at[pl.ds(3, 2)]
    fsend[mine, :] = facc[theirs, oth_cols].astype(BF16)
    fsend[theirs, :] = (facc[mine, oth_cols] + again[:, oth_cols]).astype(BF16)
    c_feed = [
        link.copy(k, fsend.at[(mine, theirs)[k - 7]], fland.at[k - 7]) for k in (7, 8)
    ]
    for one in c_feed:
        one.start()
    pump(33)

    r.rel[...] = jnp.zeros_like(r.rel)
    for k in range(2):
        rel_sum(k * 12, (area // PAIRS if k else 12), heads, r.index, r.sums, r.rel)
        pump(34 + k)
        if k == 1:
            continue
        for one in c_feed:
            one.wait()
        token_rows = gather_rows(rows, tokens, windows)[0]
        outs = []
        for side in range(2):
            value = facc[(mine, theirs)[side], own_cols] + fland[side].astype(F32)
            if side == 0:
                value += again[:, own_cols]
            pick = ones(jnp.logical_and(token_rows, r.keep[who[side], 0:1, :] > 0))
            value = dot(pick, (value + r.b2[...]).astype(BF16)).astype(BF16)
            fsend[side * rows : side * rows + tokens, :] = value
            at = pl.ds(pl.multiple_of(who[side] * tokens, tokens), tokens)
            outs.append(load(14 + side, fsend.at[pl.ds(side * rows, tokens), :], r.out.at[at, :]))
            outs[-1].start()
        load(1, r.x, cotb.at[pl.ds(0, 4)]).start()

    for k in range(4):
        load(8 + k % 2, (r.wm_own, r.wm_oth)[k // 2].at[(left, right)[k % 2], :],
             w2b.at[k % 2]).wait()
        facc[k // 2 * rows : (k // 2 + 1) * rows, (left, right)[k % 2]] = dot_nt(
            sec[mine, :], w2b[k % 2]
        )
        if k < 2:
            load(8 + k, r.wm_oth.at[(left, right)[k], :], w2b.at[k]).start()
    pump(36)
    load(1, r.x, cotb.at[pl.ds(0, 4)]).wait()
    v0 = r.v0
    v0[...] = jnp.zeros_like(v0)
    width = 2 * model

    def norm0(at):
        def both(fn):
            return sum(jnp.sum(fn(i, j), 1, keepdims=True) for i in range(2) for j in range(2))

        def cols(j):
            return (left, right)[j]

        def here(i):
            return pl.ds(pl.multiple_of(i * rows + at.start, 16), at.size)

        xs = [[cotb[2 * who[i] + j, at, :].astype(F32) for j in range(2)] for i in range(2)]
        es = [[facc[here(i), cols(j)] for j in range(2)] for i in range(2)]
        sc = [[es[i][j] * r.mgo[i, :, cols(j)] for j in range(2)] for i in range(2)]
        mean = both(lambda i, j: xs[i][j]) * (1.0 / width)
        second = both(lambda i, j: xs[i][j] * xs[i][j]) * (1.0 / width)
        scale = lax.rsqrt(second - mean * mean + EPS)
        hats = [[(xs[i][j] - mean) * scale for j in range(2)] for i in range(2)]
        low = both(lambda i, j: sc[i][j]) * (1.0 / width)
        cross = both(lambda i, j: sc[i][j] * hats[i][j]) * (1.0 / width)
        for i in range(2):
            for j in range(2):
                d = scale * (sc[i][j] - low - hats[i][j] * cross)
                qkvb[i, at, cols(j)] = d.astype(BF16)
                v0[2 * i : 2 * i + 1, cols(j)] += jnp.sum(es[i][j] * hats[i][j], 0, keepdims=True)
                v0[2 * i + 1 : 2 * i + 2, cols(j)] += jnp.sum(es[i][j], 0, keepdims=True)

    steps(rows, 64, norm0)
    pump(37)

    vs, vx = r.vs, r.vx
    heads_here = heads // 2
    for side, dst in ((0, vs.at[0]), (1, vx.at[0])):
        cols = (own_cols, oth_cols)[side]
        dst[...] = jnp.zeros(dst.shape, F32)
        for i in range(2):
            for j in range(2):
                dst[2 * i + j : 2 * i + j + 1, :] = v0[
                    2 * side + i : 2 * side + i + 1, j * half : (j + 1) * half
                ]
        dst[4:6, :] = v1[:, cols]
        dst[6:8, :] = r.vq[:, (left, right)[side]]
        dst[8:11, :] = v2[0:3, cols]
        if side == 0:
            dst[11:12, :] = r.gb2[...]
            for j in range(hidden // half):
                dst[12 + j : 13 + j, :] = r.gb1[:, j * half : (j + 1) * half]
        dst[16 : 16 + heads_here, 0 : r.rel.shape[1]] = r.rel[
            side * heads_here : (side + 1) * heads_here, :
        ]
    link.copy(6, vx.at[0], vx.at[1]).start()
    pump(38)

    outs[0].wait()
    pixel_rows = ones(gather_rows(rows, tokens, windows)[1])
    for b in range(2):
        for a in range(2):
            value = dot(pixel_rows, qkvb[b, :, (left, right)[a]])
            outs[-1].wait()
            r.pix[...] = value.reshape(*r.pix.shape)
            outs.append(load(2 * b + a, r.pix, r.pixels_grad.at[:, a, :, who[b]]))
            outs[-1].start()
    pump(39)
    pump(40)
    r.o_vec[...] = vs[bits]
    outs[-1].wait()
    for u in range(n_units):
        write(u).wait()
        for step in range(bits):
            if step > 0 or u >= first_unit - 2:
                unit(u).copy(step).wait_send()


def back(count, dim, heads, area, windows, entries, small, large):
    bits = count.bit_length() - 1
    rows, tokens = windows * PAD, windows * area
    hidden = large["fc1"].shape[1]
    model = large["fc1"].shape[0]
    half = model // 2
    side = int(area**0.5)
    slots = -(-entries // 128) * 128
    n_blocks = 2 * (hidden // CHUNK) + 6
    n_units = n_blocks + 2
    part = model // count
    orders = orders_of(count)
    big = dict(
        out=shape((2 * tokens, half), BF16),
        pixels_grad=shape((side, 2, side, 2, windows, half)),
        o_fc1=shape((part, hidden)), o_fc2=shape((part, hidden)), o_qkv=shape((3, part, half)),
        o_proj=shape((part, half)), o_merge=shape((part, model)),
        acts=shape((hidden // CHUNK, 2 * rows, CHUNK), BF16),
    )
    outs = dict(big, o_vec=shape((32, half)))
    vm, dma = pltpu.VMEM, pltpu.SemaphoreType.DMA
    scratch = dict(
        sec=vm((2 * rows, model), BF16), gfb=vm((2 * rows, model), BF16),
        facc=vm((2 * rows, model), F32), gacc=vm((2 * rows, model), F32),
        st=vm((rows, model), F32), ex=vm((2, rows, model), BF16),
        w1b=vm((2, model, CHUNK), BF16), w2b=vm((2, CHUNK, model), BF16),
        cotb=vm((5, rows, half), BF16), qkvb=vm((3, rows, model), BF16),
        biasb=vm((PAD * heads, 128), F32), sums=vm((PAD * heads, 128), F32),
        act=vm((2 * rows, CHUNK), BF16), gh=vm((2 * rows, CHUNK), BF16),
        pix=vm((side, side, windows, half), F32),
        src=vm((8, *([2] * bits), part, CHUNK), BF16),
        bufs=[vm((n_blocks, *([2] * k), part, CHUNK), BF16) for k in reversed(range(bits))],
        v0=vm((4, model), F32), v1=vm((2, model), F32), v2=vm((3, model), F32),
        vq=vm((2, model), F32), rel=vm((heads, slots), F32), gb1=vm((1, hidden), F32),
        vs=vm((bits + 1, 32, half), F32), vx=vm((2, 32, half), F32), vbuf=vm((bits, 32, half), F32),
        lsem=dma((23,)), wsem=dma((2, 2)), xsend=dma((9,)), xrecv=dma((9,)), osem=dma((n_units,)),
        rsend=dma((n_units, bits)), rrecv=dma((n_units, bits)),
        vsend=dma((bits,)), vrecv=dma((bits,)),
    )

    def body(r):
        back_body(bits, orders, dim, heads, area, r)

    return kernel_call(body, small, large, outs, scratch, big, collective=1)


def hand_on(large, vec, hidden, heads, entries):
    names, n = list(large), len(large)
    half = vec.shape[1]
    model = 2 * half
    free = pl.BlockSpec(memory_space=pl.ANY)
    small = dict(
        mg=(0, model), ms=(2, model), n1g=(4, half), n1s=(5, half), n2g=(8, half),
        n2s=(9, half), pb=(10, half), b2=(11, half), b1=(12, hidden),
    )
    tiny_shapes = [shape((1, width)) for _, width in small.values()]
    tiny_shapes += [shape((2, half)), shape((heads // 2, entries))]
    m = len(tiny_shapes)

    def run(*refs):
        given, taken = refs[: n + 1], refs[n + 1 : 2 * n + 1 + m]
        held, v, sem = refs[2 * n + 1 + m : -2], refs[-2], refs[-1]
        ins = [pltpu.make_async_copy(given[n], v, sem.at[0, n])]
        ins += [pltpu.make_async_copy(given[k], held[k], sem.at[0, k]) for k in range(n)]
        outs = [pltpu.make_async_copy(held[k], taken[k], sem.at[1, k]) for k in range(n + m)]
        for one in ins:
            one.start()
        ins[0].wait()
        for ref, (row, width) in zip(held[n:], small.values()):
            for j in range(width // half):
                ref[:, j * half : (j + 1) * half] = v[row + j : row + j + 1, :]
        held[-2][...] = v[6:8, :]
        held[-1][...] = v[16 : 16 + heads // 2, 0:entries]
        for one in outs[n:]:
            one.start()
        for one, other in zip(ins[1:], outs):
            one.wait()
            other.start()
        for one in outs:
            one.wait()

    shapes = [*[shape(a.shape, a.dtype) for a in large.values()], *tiny_shapes]
    results = pl.pallas_call(
        run,
        out_shape=tuple(shapes),
        in_specs=[free] * (n + 1),
        out_specs=(free,) * (n + m),
        scratch_shapes=[pltpu.VMEM(a.shape, a.dtype) for a in shapes]
        + [pltpu.VMEM(vec.shape, F32), pltpu.SemaphoreType.DMA((2, n + m))],
    )(*large.values(), vec)
    return SimpleNamespace(**dict(zip([*names, *small, "qb", "rel"], results)))


def solution(mesh):
    count = mesh.shape["win"]

    def shards(
        pixels, merge_gain, merge_shift, merge_weight, norm1_gain, norm1_shift, qkv_weight,
        qkv_bias, rel_table, proj_weight, proj_bias, norm2_gain, norm2_shift, fc1_weight,
        fc1_bias, fc2_weight, fc2_bias, rel_index, keep, cotangent,
    ):
        wins, height, _, channels = pixels.shape
        side = height // 2
        area = side * side
        rows = wins * PAD
        model = merge_weight.shape[1]
        half = model // 2
        heads = 2 * rel_table.shape[1]
        dim = half // rel_table.shape[1]
        hidden = fc1_weight.shape[1]

        def row(v):
            return v.reshape(1, -1)

        wqkv = qkv_weight.transpose(1, 0, 2)
        a = front(
            dim, heads, area, wins,
            dict(
                mg=row(merge_gain), ms=row(merge_shift), n1g=row(norm1_gain),
                n1s=row(norm1_shift), pb=row(proj_bias), n2g=row(norm2_gain),
                n2s=row(norm2_shift), qb=qkv_bias, table=rel_table.T, rel_index=rel_index, keep=keep,
            ),
            dict(
                pixels=pixels.transpose(1, 2, 0, 3).reshape(side, 2, side, 2, wins, channels),
                wm=merge_weight, wqkv=wqkv, wp=proj_weight, cot=cotangent,
            ),
        )
        b = back(
            count, dim, heads, area, wins, rel_table.shape[0],
            dict(
                keep=a.kept_rows, b1=row(fc1_bias), b2=row(fc2_bias), nat=a.nat, mgo=a.mgo,
                lse=a.lse, index=a.index, gb2=a.gb2,
            ),
            dict(
                second=a.second, second_sib=a.second_sib, gf=a.gf, stream1=a.stream1, stream0=a.stream0,
                fc1=fc1_weight, fc2=fc2_weight, wp_own=proj_weight, wp_oth=a.wp_oth,
                wqkv_own=wqkv, wqkv_oth=a.wqkv_oth, wm_own=merge_weight, wm_oth=a.wm_oth,
                att_own=a.att_own, att_sib=a.att_sib, qkv=a.qkv, bias=a.bias,
                first_own=a.first_own, first_sib=a.first_sib, mn_own=a.mn_own, mn_sib=a.mn_sib,
                x=a.x,
            ),
        )
        large = vars(b)
        vec = large.pop("o_vec")
        large.pop("acts")
        f = hand_on(large, vec, hidden, heads, rel_table.shape[0])

        def flat(v):
            return v.reshape(-1)

        pixels_grad = f.pixels_grad.reshape(height, height, wins, channels)
        return (
            f.out, pixels_grad.transpose(2, 0, 1, 3), flat(f.mg), flat(f.ms), f.o_merge.T,
            flat(f.n1g), flat(f.n1s), f.o_qkv.transpose(1, 0, 2), f.qb, f.rel.T,
            f.o_proj.T, flat(f.pb), flat(f.n2g), flat(f.n2s), f.o_fc1, flat(f.b1),
            f.o_fc2.T, flat(f.b2),
        )

    in_specs = (
        P(("win", "tp"), None, None, None), P("tp"), P("tp"), P("tp", None), P("tp"), P("tp"),
        P(None, None, "tp"), P(None, "tp"), P(None, "tp"), P("tp", None), P("tp"), P("tp"),
        P("tp"), P(None, "tp"), P("tp"), P("tp", None), P("tp"), P(), P("win"), P("win", "tp"),
    )
    out_specs = (
        P("win", "tp"), P(("win", "tp"), None, None, None), P("tp"), P("tp"), P("tp", "win"),
        P("tp"), P("tp"), P("win", None, "tp"), P(None, "tp"), P(None, "tp"), P("tp", "win"),
        P("tp"), P("tp"), P("tp"), P("win", "tp"), P("tp"), P("tp", "win"), P("tp"),
    )
    return jax.shard_map(shards, mesh=mesh, in_specs=in_specs, out_specs=out_specs, check_vma=False)
```

```python
from types import SimpleNamespace

import jax
import jax.numpy as jnp
from jax import lax
from jax.experimental import pallas as pl
from jax.experimental.pallas import tpu as pltpu
from jax.sharding import PartitionSpec as P

EPS = 1e-05
F32 = jnp.float32
BF16 = jnp.bfloat16
MESH = pl.DeviceIdType.MESH
PAD = 112
LIMIT = 63 * 1024 * 1024


def shape(dims, dtype=F32):
    return jax.ShapeDtypeStruct(tuple(dims), dtype)


def kernel_call(body, small, large, outs, scratch, large_outs, collective=None):
    names = [*small, *large, *outs, *scratch]
    free, vmem = pl.BlockSpec(memory_space=pl.ANY), pl.BlockSpec(memory_space=pltpu.VMEM)
    more = {} if collective is None else dict(collective_id=collective, has_side_effects=True)

    def run(*refs):
        body(SimpleNamespace(**dict(zip(names, refs, strict=True))))

    results = pl.pallas_call(
        run,
        out_shape=tuple(outs.values()),
        in_specs=[vmem] * len(small) + [free] * len(large),
        out_specs=tuple(free if n in large_outs else vmem for n in outs),
        scratch_shapes=list(scratch.values()),
        compiler_params=pltpu.CompilerParams(vmem_limit_bytes=LIMIT, **more),
    )(*small.values(), *large.values())
    return SimpleNamespace(**dict(zip(outs, results)))


def dot(a, b):
    return jnp.dot(a, b, preferred_element_type=F32)


def dot_nt(a, b):
    return lax.dot_general(a, b, (((1,), (1,)), ((), ())), preferred_element_type=F32)


def dot_tn(a, b):
    return lax.dot_general(a, b, (((0,), (0,)), ((), ())), preferred_element_type=F32)


def stats(x, width):
    mean = jnp.sum(x, 1, keepdims=True) * (1.0 / width)
    second = jnp.sum(x * x, 1, keepdims=True) * (1.0 / width)
    return mean, lax.rsqrt(second - mean * mean + EPS)


def norm_back(e, x, gain, width):
    mean, scale = stats(x, width)
    xhat = (x - mean) * scale
    scaled = e * gain
    first = jnp.sum(scaled, 1, keepdims=True) * (1.0 / width)
    cross = jnp.sum(scaled * xhat, 1, keepdims=True) * (1.0 / width)
    return scale * (scaled - first - xhat * cross), e * xhat


def steps(total, size, fn):
    @pl.loop(0, total // size)
    def _(step):
        fn(pl.ds(pl.multiple_of(step * size, size), size))


def add_to(ref, row, value):
    ref[row : row + 1, :] += jnp.sum(value, 0, keepdims=True)


def spread(rows, tokens, windows):
    row = lax.broadcasted_iota(jnp.int32, (rows, tokens), 0)
    col = lax.broadcasted_iota(jnp.int32, (rows, tokens), 1)
    area = tokens // windows
    w = row // PAD
    k = row - w * PAD
    real = k < area
    return (
        jnp.logical_and(real, w * area + k == col),
        jnp.logical_and(real, k * windows + w == col),
    )


def gather_rows(rows, tokens, windows):
    row = lax.broadcasted_iota(jnp.int32, (tokens, rows), 1)
    col = lax.broadcasted_iota(jnp.int32, (tokens, rows), 0)
    area = tokens // windows
    w = row // PAD
    k = row - w * PAD
    real = k < area
    return (
        jnp.logical_and(real, w * area + k == col),
        jnp.logical_and(real, k * windows + w == col),
    )


def ones(mask):
    return jnp.where(mask, 1.0, 0.0).astype(BF16)


class Link:
    def __init__(self, sends, recvs):
        self.sends, self.recvs = sends, recvs

    def copy(self, k, src, dst):
        return pltpu.make_async_remote_copy(
            src_ref=src,
            dst_ref=dst,
            send_sem=self.sends.at[k],
            recv_sem=self.recvs.at[k],
            device_id=(lax.axis_index("win"), 1 - lax.axis_index("tp")),
            device_id_type=MESH,
        )


def head_masks(rows, width, dim):
    lane = lax.broadcasted_iota(jnp.int32, (rows, width), 1) // dim
    return [lane == h for h in range(width // dim)]


def stacked(block, masks):
    return jnp.concatenate([jnp.where(m, block, 0.0).astype(BF16) for m in masks], 0)


def diagonal(a, b):
    zero = jnp.zeros((PAD, 128), BF16)
    rest = jnp.zeros((128 - PAD, 256), BF16)
    return jnp.concatenate(
        [jnp.concatenate([a, zero], 1), rest, jnp.concatenate([zero, b], 1), rest], 0
    )


def bias_of(bias, heads, g, per):
    first = lax.rem(g * per + lax.axis_index("tp") * (heads // 2), heads)
    return [bias[pl.ds(first + h, PAD, stride=heads), :] for h in range(per)]


def attention_forward(dim, heads, g, r):
    per = 128 // dim
    windows = r.qkvb.shape[1] // PAD
    scale = dim ** (-0.5)
    masks = head_masks(PAD, 128, dim)
    lanes = pl.ds(pl.multiple_of(g * 128, 128), 128)
    bias = bias_of(r.biasb, heads, g, per)
    done, sums = [], []
    for w in range(0, windows, 2):
        at = [pl.ds((w + u) * PAD, PAD) for u in range(2)]
        q, k, v = ([r.qkvb[s, a, lanes] for a in at] for s in range(3))
        both = dot_nt(
            jnp.concatenate([stacked(k[0], masks), stacked(k[1], masks)], 1),
            diagonal(q[0], q[1]),
        )
        for u in range(2):
            parts = []
            for h in range(per):
                s = both[h * PAD : (h + 1) * PAD, u * 128 : (u + 1) * 128] * scale + bias[h]
                top = jnp.max(s, 0, keepdims=True)
                e = jnp.exp(s - top)
                total = jnp.sum(e, 0, keepdims=True)
                parts.append((e * (1.0 / total)).astype(BF16))
                sums.append(top + jnp.log(total))
            value = dot_tn(jnp.concatenate(parts, 0), stacked(v[u], masks))
            done.append(value[:PAD].astype(BF16))
    for w in range(windows):
        r.attb[pl.ds(w * PAD, PAD), lanes] = done[w]
    r.lse[g] = jnp.concatenate(sums, 0)


def attention_back(dim, heads, g, r):
    per = 128 // dim
    windows = r.qkvb.shape[1] // PAD
    scale = dim ** (-0.5)
    masks = head_masks(PAD, 128, dim)
    lanes = pl.ds(pl.multiple_of(g * 128, 128), 128)
    bias = bias_of(r.biasb, heads, g, per)
    totals, done = [None] * per, []
    for w in range(windows):
        at = pl.ds(w * PAD, PAD)
        q, k, v = r.qkvb[0, at, lanes], r.qkvb[1, at, lanes], r.qkvb[2, at, lanes]
        go = r.ex[0, at, lanes]
        both = dot_nt(
            jnp.concatenate([stacked(k, masks), stacked(v, masks)], 1), diagonal(q, go)
        )
        kt = k.T
        p_parts, g_parts, dqs = [], [], []
        for h in range(per):
            here = slice(h * PAD, (h + 1) * PAD)
            p = jnp.exp(
                both[here, :128] * scale + bias[h] - r.lse[g, pl.ds(w * per + h, 1), :]
            )
            dp = both[here, 128:]
            gs = (p * (dp - jnp.sum(dp * p, 0, keepdims=True))).astype(BF16)
            wide = gs.astype(F32)
            totals[h] = wide if w == 0 else totals[h] + wide
            p_parts.append(p.astype(BF16))
            g_parts.append(gs)
            dqs.append(dot(kt[h * dim : (h + 1) * dim], gs))
        back = dot(
            jnp.concatenate([jnp.concatenate(p_parts, 0), jnp.concatenate(g_parts, 0)], 1),
            diagonal(go, q),
        )
        dv, dk = back[:PAD, :128], back[:PAD, 128:]
        for h in range(1, per):
            here = slice(h * PAD, (h + 1) * PAD)
            dv = jnp.where(masks[h], back[here, :128], dv)
            dk = jnp.where(masks[h], back[here, 128:], dk)
        dq = jnp.concatenate(dqs, 0).T[:PAD] * scale
        done.append((dq.astype(BF16), (dk * scale).astype(BF16), dv.astype(BF16)))
    q_sum = jnp.zeros((1, 128), F32)
    v_sum = jnp.zeros((1, 128), F32)
    for w in range(windows):
        for s in range(3):
            r.qkvb[s, pl.ds(w * PAD, PAD), lanes] = done[w][s]
        q_sum += jnp.sum(done[w][0].astype(F32), 0, keepdims=True)
        v_sum += jnp.sum(done[w][2].astype(F32), 0, keepdims=True)
    for h in range(per):
        r.sums[pl.ds(g * per + h, PAD, stride=heads), :] = totals[h]
    r.vq[0:1, lanes] = q_sum
    r.vq[1:2, lanes] = v_sum


PAIRS = 4


def onehot_of(index, first, entries):
    rows = [index[pl.ds(first + u, 1), :] for u in range(PAIRS)]
    ids = lax.broadcasted_iota(jnp.int32, (entries, rows[0].shape[1]), 0)
    return jnp.concatenate([ones(ids == row) for row in rows], 1)


def bias_spread(first, count, heads, table, index, out):
    entries = table.shape[1]
    top = table.astype(BF16)
    both = jnp.concatenate([top, (table - top.astype(F32)).astype(BF16)], 0)

    @pl.loop(0, count)
    def _(k):
        i = first + k
        value = dot(both, onehot_of(index, i * PAIRS, entries))
        value = value[:heads] + value[heads:]
        for u in range(PAIRS):
            at = pl.ds(pl.multiple_of((i * PAIRS + u) * heads, heads), heads)
            out[at, :] = value[:, u * 128 : (u + 1) * 128]


def rel_sum(first, last, heads, index, sums, rel):
    entries = rel.shape[1]

    @pl.loop(first, last)
    def _(i):
        hot = onehot_of(index, i * PAIRS, entries)
        s = jnp.concatenate(
            [
                sums[pl.ds(pl.multiple_of((i * PAIRS + u) * heads, heads), heads), :]
                for u in range(PAIRS)
            ],
            1,
        )
        top = s.astype(BF16)
        low = (s - top.astype(F32)).astype(BF16)
        both = dot_nt(jnp.concatenate([top, low], 0), hot)
        rel[...] += both[:heads] + both[heads:]


def win_bits(count):
    total = count.bit_length() - 1
    side = 1
    while 4 * (side + 1) * (side + 1) <= count:
        side += 1
    wide = side.bit_length() - 1
    axes = [range(wide), range(wide, 2 * wide), range(2 * wide, total)]
    near = [axis[0] for axis in axes if len(axis)]
    far = [bit for axis in axes for bit in axis[1:]]
    return near, far


TURNS = (((0,1,2,3),(1,0,2,3),(2,0,1,3),(0,1,2,3),(1,0,2,3),(2,1,0,3),(0,1,2,3),(1,0,2,3),(2,0,1,3),(0,1,2,3),(1,0,2,3),(2,1,0,3),(2,0,1,3),(0,1,2,3),(2,1,0,3),(1,0,2,3)))


def orders_of(count):
    near, far = win_bits(count)
    axes = [*near, *reversed(far)]
    return [(*[axes[k] for k in turn], *axes[4:]) for turn in TURNS]


def my_bit(bit):
    return lax.rem(lax.div(lax.axis_index("win"), 1 << bit), 2)


def partner(bit):
    return lax.axis_index("win") + (1 - 2 * my_bit(bit)) * (1 << bit), lax.axis_index("tp")


def enter(bits):
    barrier = pltpu.get_barrier_semaphore()
    peers = [(lax.axis_index("win"), 1 - lax.axis_index("tp"))]
    peers += [partner(bit) for bit in range(bits)]
    for peer in peers:
        pl.semaphore_signal(barrier, inc=1, device_id=peer, device_id_type=MESH)
    pl.semaphore_wait(barrier, len(peers))


class Scatter:
    def __init__(self, order, held, sends, recvs, unit):
        self.order, self.held = order, held
        self.sends, self.recvs, self.unit = sends, recvs, unit

    def pick(self, step, value):
        left = [b for b in range(len(self.order)) if b not in self.order[:step]]
        dim = len(left) - 1 - left.index(self.order[step])
        return self.held[step].at[(*([slice(None)] * dim), value)]

    def copy(self, step):
        bit = self.order[step]
        return pltpu.make_async_remote_copy(
            src_ref=self.pick(step, 1 - my_bit(bit)),
            dst_ref=self.held[step + 1],
            send_sem=self.sends.at[self.unit, step],
            recv_sem=self.recvs.at[self.unit, step],
            device_id=partner(bit),
            device_id_type=MESH,
        )

    def finish(self, step, out=None):
        self.copy(step).wait_recv()
        mine = self.pick(step, my_bit(self.order[step]))
        got = self.held[step + 1]
        lead = got.shape[:-2]
        if not lead:
            out[...] = mine[...].astype(F32) + got[...].astype(F32)
            return

        @pl.loop(0, 1 << len(lead))
        def _(i):
            at = tuple(lax.rem(lax.div(i, 1 << k), 2) for k in reversed(range(len(lead))))
            got[at] = (mine[at].astype(F32) + got[at].astype(F32)).astype(BF16)

        self.copy(step + 1).start()


def front_body(dim, heads, area, r):
    enter(0)
    t = lax.axis_index("tp")
    who = (t, 1 - t)
    rows, model = r.firstb.shape
    half = model // 2
    windows = rows // PAD
    tokens = windows * area
    link = Link(r.xsend, r.xrecv)
    own_cols = pl.ds(pl.multiple_of(t * half, half), half)
    oth_cols = pl.ds(pl.multiple_of((1 - t) * half, half), half)

    def load(k, src, dst):
        return pltpu.make_async_copy(src, dst, r.lsem.at[k])

    c_wm = link.copy(0, r.wm, r.wmb.at[1])
    c_wm.start()
    loads = [load(k, r.pixels.at[:, k % 2, :, k // 2], r.pix.at[k]) for k in range(4)]
    loads += [load(4, r.cot, r.cotb.at[0]), load(5, r.wm, r.wmb.at[0])]
    for one in loads:
        one.start()
    vx = r.vx
    vx[0] = jnp.zeros(vx.shape[1:], F32)
    for k, ref in enumerate((r.mg, r.ms)):
        for j in range(2):
            vx[0, 2 * k + j : 2 * k + j + 1, :] = ref[:, j * half : (j + 1) * half]
    for k, ref in enumerate((r.n1g, r.n1s, r.pb, r.n2g, r.n2s)):
        vx[0, 4 + k : 5 + k, :] = ref[...]
    vx[0, 9:11, :] = r.qb[...]
    vx[0, 16 : 16 + heads // 2, 0 : r.table.shape[1]] = r.table[...]
    c_vec = link.copy(1, vx.at[0], vx.at[1])
    c_vec.start()
    c_wq = link.copy(3, r.wqkv, r.wqb.at[1])
    c_wq.start()
    late = [load(6, r.wqkv, r.wqb.at[0]), load(7, r.wp, r.wpb.at[pl.ds(0, half), :])]
    for one in late:
        one.start()
    stores = []

    def store(src, dst):
        one = pltpu.make_async_copy(src, dst, r.ssem.at[len(stores)])
        stores.append(one)
        one.start()

    token_rows, pixel_rows = spread(rows, tokens, windows)
    pixel_rows = ones(pixel_rows)
    kept = r.keep[...].astype(F32).reshape(1, 2 * tokens)
    kept = (kept[:, :tokens], kept[:, tokens:])
    for side in range(2):
        wide = jnp.broadcast_to(kept[side], (8, tokens)).astype(BF16)
        r.kept_rows[side] = dot_nt(wide, ones(token_rows))
    r.square[...] = jnp.zeros_like(r.square)
    r.square[0:area, 0:area] = r.rel_index[...].astype(F32)
    r.index[...] = r.square[...].T.astype(jnp.int32)
    for k in range(4):
        loads[k].wait()
        r.xb[k] = dot(
            pixel_rows, r.pix[k].astype(F32).reshape(tokens, half).astype(BF16)
        ).astype(BF16)
    store(r.xb, r.x)

    c_vec.wait()
    mgo, nat = r.mgo, r.nat
    for side in range(2):
        for j in range(2):
            mgo[side, :, j * half : (j + 1) * half] = vx[side, j : j + 1, :]
            r.mso[side, :, j * half : (j + 1) * half] = vx[side, 2 + j : 3 + j, :]
        nat[0:5, (own_cols, oth_cols)[side]] = vx[side, 4:9, :]
    width = 2 * model

    def norm0(at):
        xs = [
            [r.xb[2 * who[i] + j, at, :].astype(F32) for j in range(2)] for i in range(2)
        ]

        def both(fn):
            return sum(jnp.sum(fn(x), 1, keepdims=True) for pair in xs for x in pair)

        mean = both(lambda x: x) * (1.0 / width)
        scale = lax.rsqrt(both(lambda x: x * x) * (1.0 / width) - mean * mean + EPS)
        for i in range(2):
            for j in range(2):
                cols = pl.ds(j * half, half)
                value = (xs[i][j] - mean) * scale * mgo[i, :, cols] + r.mso[i, :, cols]
                r.mnb[i, at, cols] = value.astype(BF16)

    steps(rows, 64, norm0)
    store(r.mnb.at[0], r.mn_own)

    entries = r.tableb.shape[1]
    for side in range(2):
        at = pl.ds(pl.multiple_of(who[side] * (heads // 2), heads // 2), heads // 2)
        r.tableb[at, :] = vx[side, 16 : 16 + heads // 2, 0:entries]
    turns = area // PAIRS
    share = turns // 2 + 1
    bias_spread(t * (turns - share), share, heads, r.tableb[...], r.index, r.biasb)
    size = (turns - share) * PAIRS * heads
    at = pl.ds(pl.multiple_of(t * share * PAIRS * heads, PAIRS * heads), size)
    c_bias = link.copy(8, r.biasb.at[at, :], r.biasb.at[at, :])
    c_bias.start()
    r.biasb[pl.ds(area * heads, (PAD - area) * heads), :] = jnp.full(
        ((PAD - area) * heads, 128), -1e30, F32
    )
    c_cot = link.copy(2, r.cot, r.cotb.at[1])
    c_cot.start()
    c_wp = link.copy(4, r.wp, r.wpb.at[pl.ds(half, half), :])
    c_wp.start()
    c_mn = link.copy(6, r.mnb.at[1], r.mn_sib)
    c_mn.start()

    loads[5].wait()

    def own_part(at):
        r.s0b[:, at] = dot(r.mnb[0], r.wmb[0, :, at])

    steps(model, 512, own_part)
    c_wm.wait()
    store(r.wmb.at[1], r.wm_oth)

    def oth_part(at):
        r.s0b[:, at] += dot(r.mnb[1], r.wmb[1, :, at])

    steps(model, 512, oth_part)
    store(r.s0b, r.stream0)

    def norm1(at):
        x = r.s0b[at, :]
        mean, scale = stats(x, model)
        r.firstb[at, :] = ((x - mean) * scale * nat[0:1, :] + nat[1:2, :]).astype(BF16)

    steps(rows, 112, norm1)
    c_first = link.copy(5, r.firstb, r.first_sib)
    c_first.start()
    store(r.firstb, r.first_own)

    late[0].wait()
    for side in range(2):
        if side == 1:
            c_wq.wait()
            store(r.wqb.at[1], r.wqkv_oth)
        for s in range(3):
            cols = pl.ds(side * half, half)
            value = dot(r.firstb[...], r.wqb[side, s])
            if s != 1:
                value += vx[side, 9 + s // 2 : 10 + s // 2, :]
            r.qkvb[s, :, cols] = value.astype(BF16)
    store(r.qkvb, r.qkv)

    c_bias.wait()
    store(r.biasb, r.bias)

    @pl.loop(0, model // 128, unroll=2)
    def _(g):
        attention_forward(dim, heads, g, r)

    c_att = link.copy(7, r.attb.at[:, pl.ds(half, half)], r.att_sib)
    c_att.start()
    store(r.attb.at[:, pl.ds(0, half)], r.att_own)

    late[1].wait()
    c_wp.wait()
    store(r.wpb.at[pl.ds(half, half), :], r.wp_oth)

    def project(at):
        value = dot(r.attb[...], r.wpb[:, at]) + nat[2:3, at]
        r.s1b[:, at] = r.s0b[:, at] + value

    steps(model, 512, project)
    store(r.s1b, r.stream1)

    def norm2(at):
        x = r.s1b[at, :]
        mean, scale = stats(x, model)
        r.secb[at, :] = ((x - mean) * scale * nat[3:4, :] + nat[4:5, :]).astype(BF16)

    steps(rows, 112, norm2)
    c_sec = link.copy(9, r.secb, r.second_sib)
    c_sec.start()
    store(r.secb, r.second)

    loads[4].wait()
    c_cot.wait()
    total = jnp.zeros((1, half), F32)
    for side in range(2):
        at = pl.ds(pl.multiple_of(who[side] * tokens, tokens), tokens)
        pick = ones(jnp.logical_and(token_rows, jnp.where(who[side] == 0, kept[0], kept[1]) > 0))
        mine = dot(pick, r.cotb[0, at, :])
        total += jnp.sum(mine, 0, keepdims=True)
        here = pl.ds(side * rows, rows)
        r.gfb[here, own_cols] = mine.astype(BF16)
        r.gfb[here, oth_cols] = dot(pick, r.cotb[1, at, :]).astype(BF16)
    r.gb2[...] = total
    store(r.gfb, r.gf)
    for one in (c_mn, c_first, c_att, c_sec):
        one.wait()
    for one in stores:
        one.wait()


def front(dim, heads, area, windows, small, large):
    rows, tokens = windows * PAD, windows * area
    model = large["wm"].shape[1]
    half = model // 2
    side = large["pixels"].shape[0:3:2]
    slots = -(-small["table"].shape[1] // 128) * 128
    vm, dma = pltpu.VMEM, pltpu.SemaphoreType.DMA
    big = dict(
        x=shape((4, rows, half), BF16), gf=shape((2 * rows, model), BF16),
        stream0=shape((rows, model)), stream1=shape((rows, model)),
        second=shape((rows, model), BF16), second_sib=shape((rows, model), BF16), qkv=shape((3, rows, model), BF16),
        bias=shape((PAD * heads, 128)), first_own=shape((rows, model), BF16),
        first_sib=shape((rows, model), BF16), mn_own=shape((rows, model), BF16),
        mn_sib=shape((rows, model), BF16), att_own=shape((rows, half), BF16),
        att_sib=shape((rows, half), BF16), wm_oth=shape((model, model), BF16),
        wqkv_oth=shape((3, model, half), BF16), wp_oth=shape((half, model), BF16),
    )
    outs = dict(
        big, gb2=shape((1, half)), nat=shape((8, model)), mgo=shape((2, 1, model)),
        lse=shape((model // 128, windows * 128 // dim, 128)),
        kept_rows=shape((2, 8, rows)), index=shape((128, 128), jnp.int32),
    )
    scratch = dict(
        wmb=vm((2, model, model), BF16), wqb=vm((2, 3, model, half), BF16),
        wpb=vm((model, model), BF16), pix=vm((4, *side, windows, half), BF16),
        xb=vm((4, rows, half), BF16), cotb=vm((2, 2 * tokens, half), BF16),
        gfb=vm((2 * rows, model), BF16), mnb=vm((2, rows, model), BF16),
        s0b=vm((rows, model), F32), s1b=vm((rows, model), F32), firstb=vm((rows, model), BF16),
        qkvb=vm((3, rows, model), BF16), biasb=vm((PAD * heads, 128), F32),
        attb=vm((rows, model), BF16), secb=vm((rows, model), BF16),
        vx=vm((2, 32, half), F32), mso=vm((2, 1, model), F32), tableb=vm((heads, slots), F32),
        square=vm((128, 128), F32),
        lsem=dma((8,)), ssem=dma((16,)), xsend=dma((10,)), xrecv=dma((10,)),
    )

    def body(r):
        front_body(dim, heads, area, r)

    return kernel_call(body, small, large, outs, scratch, big, collective=2)


CHUNK = 512
PLAN = {
    3: ((0, 0), (1, 0)),
    8: ((2, 0),),
    11: ((3, 0),),
    12: ((4, 0),),
    15: ((5, 0),),
    17: ((6, 0),),
    18: ((7, 0),),
    20: ((1, 1),),
    23: ((3, 1), (1, 2)),
    27: ((4, 1), (0, 2)),
    29: ((8, 0), (0, 1)),
    30: ((2, 1),),
    31: ((5, 1), (7, 1)),
    32: ((6, 1),),
    34: ((11, 0), (3, 2)),
    35: ((9, 0), (1, 3), (4, 2), (10, 0), (0, 3), (2, 2), (8, 1)),
    36: ((12, 0),),
    37: ((15, 0), (13, 0), (7, 2)),
    39: ((5, 2),),
    40: (
        (11, 1), (14, 0), (-1, 0), (10, 1), (6, 2), (-1, 1),
        (9, 1), (12, 1), (-1, 2), (3, 3), (8, 2), (-1, 3),
        (15, 1), (4, 3), (-1, 4), (13, 1), (11, 2), (2, 3),
        (14, 1), (7, 3), (12, 2), (14, 2), (5, 3), (10, 2),
        (6, 3), (9, 2), (8, 3), (15, 2), (13, 2), (11, 3),
        (12, 3), (14, 3), (10, 3), (9, 3), (15, 3), (13, 3),
    ),
}


def back_body(bits, orders, dim, heads, area, r):
    n_units = len(orders)
    t = lax.axis_index("tp")
    who = (t, 1 - t)
    sec, gf, facc, gacc, st, ex = r.sec, r.gfb, r.facc, r.gacc, r.st, r.ex
    w1b, w2b, cotb, qkvb = r.w1b, r.w2b, r.cotb, r.qkvb
    rows, model = st.shape
    half = model // 2
    hidden = r.fc1.shape[1]
    chunks = hidden // CHUNK
    windows = rows // PAD
    tokens = windows * area
    mine, theirs = pl.ds(0, rows), pl.ds(rows, rows)
    left, right = pl.ds(0, half), pl.ds(half, half)
    link = Link(r.xsend, r.xrecv)
    own_cols = pl.ds(pl.multiple_of(t * half, half), half)
    oth_cols = pl.ds(pl.multiple_of((1 - t) * half, half), half)
    part = model // (1 << bits)

    def load(k, src, dst):
        return pltpu.make_async_copy(src, dst, r.lsem.at[k])

    whole_units = 2 * chunks + 4

    def place_of(u):
        if u < whole_units:
            return u, pl.ds(0, CHUNK)
        u -= whole_units
        return whole_units + u // 2, pl.ds(u % 2 * (CHUNK // 2), CHUNK // 2)

    def unit(u):
        block, cols = place_of(u)
        lead = tuple([slice(None)] * bits)
        held = [r.src.at[(block % 8, *lead, slice(None), cols)]]
        for k, buf in enumerate(r.bufs):
            held.append(buf.at[(block, *lead[k + 1 :], slice(None), cols)])
        return Scatter(orders[u], held, r.rsend, r.rrecv, u)

    def put(block, value):
        if block >= 8:
            unit(block - 8).copy(0).wait_send()
        r.src[block % 8] = value.astype(BF16).reshape(*([2] * bits), part, CHUNK)
        for u in range(n_units):
            if place_of(u)[0] == block:
                unit(u).copy(0).start()

    def held(u):
        block, cols = place_of(u)
        at = pl.ds(block % 2 * CHUNK + cols.start, cols.size)
        return st.at[block // 2 * part : (block // 2 + 1) * part, at]

    def result(u):
        if u < 2 * chunks:
            return (r.o_fc1, r.o_fc2)[u % 2].at[:, pl.ds(u // 2 * CHUNK, CHUNK)]
        u -= 2 * chunks
        if u == 0:
            return r.o_proj
        if u < 4:
            return r.o_qkv.at[u - 1]
        return r.o_merge.at[:, pl.ds((u - 4) * (CHUNK // 2), CHUNK // 2)]

    last_step = bits - 1
    copies = [
        pltpu.make_async_remote_copy(
            src_ref=r.vs.at[bit],
            dst_ref=r.vbuf.at[bit],
            send_sem=r.vsend.at[bit],
            recv_sem=r.vrecv.at[bit],
            device_id=partner(bit),
            device_id_type=MESH,
        )
        for bit in range(bits)
    ]

    def vectors(step):
        if step == 0:
            link.copy(6, r.vx.at[0], r.vx.at[1]).wait()
            r.vs[0] += r.vx[1]
        else:
            copies[step - 1].wait()
            r.vs[step] = r.vs[step - 1] + r.vbuf[step - 1]
        if step < bits:
            copies[step].start()

    def pump(place):
        for u, step in PLAN.get(place, ()):
            if u < 0:
                vectors(step)
                continue
            unit(u).finish(step, held(u))
            if step == last_step:
                write(u).start()

    def write(u):
        return pltpu.make_async_copy(held(u), result(u), r.osem.at[u])

    loads = [load(0, r.second, sec.at[mine]), load(2, r.second_sib, sec.at[theirs])]
    for one in loads:
        one.start()

    def weights(c):
        slot = lax.rem(c, 2)
        cols = pl.ds(pl.multiple_of(c * CHUNK, CHUNK), CHUNK)
        return (
            pltpu.make_async_copy(r.fc1.at[:, cols], w1b.at[slot], r.wsem.at[0, slot]),
            pltpu.make_async_copy(r.fc2.at[cols, :], w2b.at[slot], r.wsem.at[1, slot]),
        )

    for one in weights(0):
        one.start()
    late = [load(1, r.gf, gf), load(3, r.stream1, st), load(4, r.qkv, qkvb)]
    for one in late:
        one.start()
    enter(bits)
    for one in (*loads, late[0]):
        one.wait()

    blocks = CHUNK // 128
    hid, dact, act, gh = r.sums, r.biasb, r.act, r.gh

    def save(c):
        return load(13, act, r.acts.at[c])

    @pl.loop(0, chunks)
    def _(c):
        slot = lax.rem(c, 2)
        for one in weights(c):
            one.wait()

        @pl.when(c + 1 < chunks)
        def _():
            for one in weights(c + 1):
                one.start()

        of = pl.ds(pl.multiple_of(c * CHUNK, CHUNK), CHUNK)
        value = dot(sec[...], w1b[slot]) + r.b1[:, of]
        for b in range(blocks):
            hid[b * 2 * rows : (b + 1) * 2 * rows, :] = value[:, b * 128 : (b + 1) * 128]
        value = dot_nt(gf[...], w2b[slot])
        for b in range(blocks):
            dact[b * 2 * rows : (b + 1) * 2 * rows, :] = value[:, b * 128 : (b + 1) * 128]
        @pl.when(c > 0)
        def _():
            save(c - 1).wait()

        for b in range(blocks):
            lanes = pl.ds(b * 128, 128)

            def gelu(at):
                here = pl.ds(pl.multiple_of(b * 2 * rows + at.start, 128), at.size)
                x = hid[here, :]
                cdf = 0.5 * (1.0 + lax.erf(x * 0.7071067811865476))
                pdf = jnp.exp(x * x * -0.5) * 0.3989422804014327
                act[at, lanes] = (x * cdf).astype(BF16)
                gh[at, lanes] = (dact[here, :] * (cdf + x * pdf)).astype(BF16)

            steps(2 * rows, 128, gelu)
        save(c).start()
        r.gb1[:, of] = jnp.sum(gh[...].astype(F32), 0, keepdims=True)
        for k, value in enumerate((dot_tn(sec[...], gh[...]), dot_tn(gf[...], act[...]))):
            r.src[2 * c + k] = value.astype(BF16).reshape(*([2] * bits), part, CHUNK)
            for j in range(chunks):

                @pl.when(c == j)
                def _():
                    unit(2 * j + k).copy(0).start()

        for j in range(chunks):

            @pl.when(c == j)
            def _():
                pump(j)

        @pl.when(c == 0)
        def _():
            gacc[...] = dot_nt(gh[...], w1b[slot])

        @pl.when(c > 0)
        def _():
            gacc[...] += dot_nt(gh[...], w1b[slot])

        for j in range(chunks):

            @pl.when(c == j)
            def _():
                pump(chunks + j)

    load(5, r.bias, r.biasb).start()
    save(chunks - 1).wait()
    load(6, r.att_own, act.at[mine]).start()
    load(7, r.att_sib, act.at[theirs]).start()
    for k, src in enumerate((r.wp_own, r.wp_oth)):
        load(8 + k, src, w2b.at[k]).start()
    ex[0] = gacc[theirs].astype(BF16)
    c_g2 = link.copy(1, ex.at[0], ex.at[1])
    c_g2.start()
    load(3, r.stream1, st).wait()
    pump(8)
    v2 = r.v2
    v2[...] = jnp.zeros_like(v2)
    c_g2.wait()

    def norm2(at):
        e = gacc[at, :] + ex[1, at, :].astype(F32)
        dv, hat = norm_back(e, st[at, :], r.nat[3:4, :], model)
        d = gf[at, :].astype(F32) + dv
        gacc[at, :] = d
        low = d.astype(BF16)
        sec[at, :] = low
        add_to(v2, 0, hat)
        add_to(v2, 1, e)
        add_to(v2, 2, low.astype(F32))

    steps(rows, 112, norm2)
    c_att = link.copy(3, sec.at[mine], sec.at[theirs])
    c_att.start()
    load(10, r.first_own, gf.at[mine]).start()
    load(11, r.first_sib, gf.at[theirs]).start()
    pump(9)
    pump(10)
    for k, src in enumerate((r.wp_own, r.wp_oth)):
        load(8 + k, src, w2b.at[k]).wait()
        ex[0, :, (left, right)[k]] = dot_nt(sec[mine, :], w2b[k]).astype(BF16)

    pump(11)

    first_unit = 2 * chunks
    u_proj, u_qkv = first_unit, first_unit + 1
    u_merge = first_unit + 4
    load(6, r.att_own, act.at[mine]).wait()
    load(7, r.att_sib, act.at[theirs]).wait()
    c_att.wait()
    put(u_proj, dot_tn(sec[...], act[...]))
    pump(12)

    s0 = facc.at[theirs]
    load(12, r.stream0, s0).start()
    load(4, r.qkv, qkvb).wait()
    load(5, r.bias, r.biasb).wait()

    dland = cotb.at[pl.ds(0, 3)]
    c_qkv = link.copy(4, qkvb.at[:, :, right], dland)
    groups = model // 128

    @pl.loop(0, groups)
    def _(g):
        attention_back(dim, heads, lax.rem(g + groups // 2, groups), r)

        @pl.when(g == groups // 2 - 1)
        def _():
            c_qkv.start()


        for k in range(8):

            @pl.when(g == k)
            def _():
                pump(13 + k)

    def slice_of(k):
        return (r.wqkv_own, r.wqkv_oth)[k // 3].at[k % 3]

    load(16, slice_of(0), w1b.at[0]).start()

    load(10, r.first_own, gf.at[mine]).wait()
    load(11, r.first_sib, gf.at[theirs]).wait()
    c_qkv.wait()
    for s in range(3):
        put(u_qkv + s, dot_tn(gf[mine, :], qkvb[s, :, left]) + dot_tn(gf[theirs, :], dland[s]))
        pump(28 + s)
    load(10, r.mn_own, gf.at[mine]).start()
    load(11, r.mn_sib, gf.at[theirs]).start()

    kept = (act, gh)

    def feed_loads(c):
        slot = c % 2
        rows_of = pl.ds(c * CHUNK, CHUNK)
        return (
            load(18 + slot, r.acts.at[c], kept[slot]),
            load(20 + slot, r.fc2.at[rows_of, :], w2b.at[slot]),
        )

    def feed(c):
        for one in feed_loads(c):
            one.wait()
        value = dot(kept[c % 2][...], w2b[c % 2])
        if c == 0:
            facc[...] = value
        else:
            facc[...] += value
        if c + 2 < chunks:
            for one in feed_loads(c + 2):
                one.start()

    for c in range(2):
        for one in feed_loads(c):
            one.start()

    for k in range(6):
        load(16 + k % 2, slice_of(k), w1b.at[k % 2]).wait()
        if k + 1 < 6:
            load(16 + (k + 1) % 2, slice_of(k + 1), w1b.at[(k + 1) % 2]).start()
        value = dot_nt(qkvb[k % 3, :, (left, right)[k // 3]], w1b[k % 2])
        if k == 0:
            gacc[theirs, :] = value
        else:
            gacc[theirs, :] += value
        pump(21 + k)
    load(12, r.stream0, s0).wait()
    v1 = r.v1
    v1[...] = jnp.zeros_like(v1)

    def norm1(at):
        e = gacc[pl.ds(pl.multiple_of(rows + at.start, 16), at.size), :]
        dv, hat = norm_back(e, s0[at, :], r.nat[0:1, :], model)
        sec[at, :] = (gacc[at, :] + dv).astype(BF16)
        add_to(v1, 0, hat)
        add_to(v1, 1, e)

    steps(rows, 112, norm1)
    c_s0 = link.copy(5, sec.at[mine], ex.at[1])
    c_s0.start()
    again = gacc.at[theirs]
    load(22, r.stream1, again).start()
    pump(27)
    feed(0)
    feed(1)

    c_s0.wait()
    load(10, r.mn_own, gf.at[mine]).wait()
    load(11, r.mn_sib, gf.at[theirs]).wait()
    for k in range(2):
        cols = (left, right)[k]
        put(u_merge + k, dot_tn(sec[mine, :], gf[mine, cols]) + dot_tn(ex[1], gf[theirs, cols]))
        pump(31 + k)

    for c in range(2, chunks):
        feed(c)
    for k in range(2):
        load(8 + k, r.wm_own.at[(left, right)[k], :], w2b.at[k]).start()
    load(22, r.stream1, again).wait()
    fsend, fland = gh, cotb.at[pl.ds(3, 2)]
    fsend[mine, :] = facc[theirs, oth_cols].astype(BF16)
    fsend[theirs, :] = (facc[mine, oth_cols] + again[:, oth_cols]).astype(BF16)
    c_feed = [
        link.copy(k, fsend.at[(mine, theirs)[k - 7]], fland.at[k - 7]) for k in (7, 8)
    ]
    for one in c_feed:
        one.start()
    pump(33)

    r.rel[...] = jnp.zeros_like(r.rel)
    for k in range(2):
        rel_sum(k * 12, (area // PAIRS if k else 12), heads, r.index, r.sums, r.rel)
        pump(34 + k)
        if k == 1:
            continue
        for one in c_feed:
            one.wait()
        token_rows = gather_rows(rows, tokens, windows)[0]
        outs = []
        for side in range(2):
            value = facc[(mine, theirs)[side], own_cols] + fland[side].astype(F32)
            if side == 0:
                value += again[:, own_cols]
            pick = ones(jnp.logical_and(token_rows, r.keep[who[side], 0:1, :] > 0))
            value = dot(pick, (value + r.b2[...]).astype(BF16)).astype(BF16)
            fsend[side * rows : side * rows + tokens, :] = value
            at = pl.ds(pl.multiple_of(who[side] * tokens, tokens), tokens)
            outs.append(load(14 + side, fsend.at[pl.ds(side * rows, tokens), :], r.out.at[at, :]))
            outs[-1].start()
        load(1, r.x, cotb.at[pl.ds(0, 4)]).start()

    for k in range(4):
        load(8 + k % 2, (r.wm_own, r.wm_oth)[k // 2].at[(left, right)[k % 2], :],
             w2b.at[k % 2]).wait()
        facc[k // 2 * rows : (k // 2 + 1) * rows, (left, right)[k % 2]] = dot_nt(
            sec[mine, :], w2b[k % 2]
        )
        if k < 2:
            load(8 + k, r.wm_oth.at[(left, right)[k], :], w2b.at[k]).start()
    pump(36)
    load(1, r.x, cotb.at[pl.ds(0, 4)]).wait()
    v0 = r.v0
    v0[...] = jnp.zeros_like(v0)
    width = 2 * model

    def norm0(at):
        def both(fn):
            return sum(jnp.sum(fn(i, j), 1, keepdims=True) for i in range(2) for j in range(2))

        def cols(j):
            return (left, right)[j]

        def here(i):
            return pl.ds(pl.multiple_of(i * rows + at.start, 16), at.size)

        xs = [[cotb[2 * who[i] + j, at, :].astype(F32) for j in range(2)] for i in range(2)]
        es = [[facc[here(i), cols(j)] for j in range(2)] for i in range(2)]
        sc = [[es[i][j] * r.mgo[i, :, cols(j)] for j in range(2)] for i in range(2)]
        mean = both(lambda i, j: xs[i][j]) * (1.0 / width)
        second = both(lambda i, j: xs[i][j] * xs[i][j]) * (1.0 / width)
        scale = lax.rsqrt(second - mean * mean + EPS)
        hats = [[(xs[i][j] - mean) * scale for j in range(2)] for i in range(2)]
        low = both(lambda i, j: sc[i][j]) * (1.0 / width)
        cross = both(lambda i, j: sc[i][j] * hats[i][j]) * (1.0 / width)
        for i in range(2):
            for j in range(2):
                d = scale * (sc[i][j] - low - hats[i][j] * cross)
                qkvb[i, at, cols(j)] = d.astype(BF16)
                v0[2 * i : 2 * i + 1, cols(j)] += jnp.sum(es[i][j] * hats[i][j], 0, keepdims=True)
                v0[2 * i + 1 : 2 * i + 2, cols(j)] += jnp.sum(es[i][j], 0, keepdims=True)

    steps(rows, 64, norm0)
    pump(37)

    vs, vx = r.vs, r.vx
    heads_here = heads // 2
    for side, dst in ((0, vs.at[0]), (1, vx.at[0])):
        cols = (own_cols, oth_cols)[side]
        dst[...] = jnp.zeros(dst.shape, F32)
        for i in range(2):
            for j in range(2):
                dst[2 * i + j : 2 * i + j + 1, :] = v0[
                    2 * side + i : 2 * side + i + 1, j * half : (j + 1) * half
                ]
        dst[4:6, :] = v1[:, cols]
        dst[6:8, :] = r.vq[:, (left, right)[side]]
        dst[8:11, :] = v2[0:3, cols]
        if side == 0:
            dst[11:12, :] = r.gb2[...]
            for j in range(hidden // half):
                dst[12 + j : 13 + j, :] = r.gb1[:, j * half : (j + 1) * half]
        dst[16 : 16 + heads_here, 0 : r.rel.shape[1]] = r.rel[
            side * heads_here : (side + 1) * heads_here, :
        ]
    link.copy(6, vx.at[0], vx.at[1]).start()
    pump(38)

    outs[0].wait()
    pixel_rows = ones(gather_rows(rows, tokens, windows)[1])
    for b in range(2):
        for a in range(2):
            value = dot(pixel_rows, qkvb[b, :, (left, right)[a]])
            outs[-1].wait()
            r.pix[...] = value.reshape(*r.pix.shape)
            outs.append(load(2 * b + a, r.pix, r.pixels_grad.at[:, a, :, who[b]]))
            outs[-1].start()
    pump(39)
    pump(40)
    r.o_vec[...] = vs[bits]
    outs[-1].wait()
    for u in range(n_units):
        write(u).wait()
        for step in range(bits):
            if step > 0 or u >= first_unit - 2:
                unit(u).copy(step).wait_send()


def back(count, dim, heads, area, windows, entries, small, large):
    bits = count.bit_length() - 1
    rows, tokens = windows * PAD, windows * area
    hidden = large["fc1"].shape[1]
    model = large["fc1"].shape[0]
    half = model // 2
    side = int(area**0.5)
    slots = -(-entries // 128) * 128
    n_blocks = 2 * (hidden // CHUNK) + 6
    n_units = n_blocks + 2
    part = model // count
    orders = orders_of(count)
    big = dict(
        out=shape((2 * tokens, half), BF16),
        pixels_grad=shape((side, 2, side, 2, windows, half)),
        o_fc1=shape((part, hidden)), o_fc2=shape((part, hidden)), o_qkv=shape((3, part, half)),
        o_proj=shape((part, half)), o_merge=shape((part, model)),
        acts=shape((hidden // CHUNK, 2 * rows, CHUNK), BF16),
    )
    outs = dict(big, o_vec=shape((32, half)))
    vm, dma = pltpu.VMEM, pltpu.SemaphoreType.DMA
    scratch = dict(
        sec=vm((2 * rows, model), BF16), gfb=vm((2 * rows, model), BF16),
        facc=vm((2 * rows, model), F32), gacc=vm((2 * rows, model), F32),
        st=vm((rows, model), F32), ex=vm((2, rows, model), BF16),
        w1b=vm((2, model, CHUNK), BF16), w2b=vm((2, CHUNK, model), BF16),
        cotb=vm((5, rows, half), BF16), qkvb=vm((3, rows, model), BF16),
        biasb=vm((PAD * heads, 128), F32), sums=vm((PAD * heads, 128), F32),
        act=vm((2 * rows, CHUNK), BF16), gh=vm((2 * rows, CHUNK), BF16),
        pix=vm((side, side, windows, half), F32),
        src=vm((8, *([2] * bits), part, CHUNK), BF16),
        bufs=[vm((n_blocks, *([2] * k), part, CHUNK), BF16) for k in reversed(range(bits))],
        v0=vm((4, model), F32), v1=vm((2, model), F32), v2=vm((3, model), F32),
        vq=vm((2, model), F32), rel=vm((heads, slots), F32), gb1=vm((1, hidden), F32),
        vs=vm((bits + 1, 32, half), F32), vx=vm((2, 32, half), F32), vbuf=vm((bits, 32, half), F32),
        lsem=dma((23,)), wsem=dma((2, 2)), xsend=dma((9,)), xrecv=dma((9,)), osem=dma((n_units,)),
        rsend=dma((n_units, bits)), rrecv=dma((n_units, bits)),
        vsend=dma((bits,)), vrecv=dma((bits,)),
    )

    def body(r):
        back_body(bits, orders, dim, heads, area, r)

    return kernel_call(body, small, large, outs, scratch, big, collective=1)


def hand_on(large, vec, hidden, heads, entries):
    names, n = list(large), len(large)
    half = vec.shape[1]
    model = 2 * half
    free = pl.BlockSpec(memory_space=pl.ANY)
    small = dict(
        mg=(0, model), ms=(2, model), n1g=(4, half), n1s=(5, half), n2g=(8, half),
        n2s=(9, half), pb=(10, half), b2=(11, half), b1=(12, hidden),
    )
    tiny_shapes = [shape((1, width)) for _, width in small.values()]
    tiny_shapes += [shape((2, half)), shape((heads // 2, entries))]
    m = len(tiny_shapes)

    def run(*refs):
        given, taken = refs[: n + 1], refs[n + 1 : 2 * n + 1 + m]
        held, v, sem = refs[2 * n + 1 + m : -2], refs[-2], refs[-1]
        ins = [pltpu.make_async_copy(given[n], v, sem.at[0, n])]
        ins += [pltpu.make_async_copy(given[k], held[k], sem.at[0, k]) for k in range(n)]
        outs = [pltpu.make_async_copy(held[k], taken[k], sem.at[1, k]) for k in range(n + m)]
        for one in ins:
            one.start()
        ins[0].wait()
        for ref, (row, width) in zip(held[n:], small.values()):
            for j in range(width // half):
                ref[:, j * half : (j + 1) * half] = v[row + j : row + j + 1, :]
        held[-2][...] = v[6:8, :]
        held[-1][...] = v[16 : 16 + heads // 2, 0:entries]
        for one in outs[n:]:
            one.start()
        for one, other in zip(ins[1:], outs):
            one.wait()
            other.start()
        for one in outs:
            one.wait()

    shapes = [*[shape(a.shape, a.dtype) for a in large.values()], *tiny_shapes]
    results = pl.pallas_call(
        run,
        out_shape=tuple(shapes),
        in_specs=[free] * (n + 1),
        out_specs=(free,) * (n + m),
        scratch_shapes=[pltpu.VMEM(a.shape, a.dtype) for a in shapes]
        + [pltpu.VMEM(vec.shape, F32), pltpu.SemaphoreType.DMA((2, n + m))],
    )(*large.values(), vec)
    return SimpleNamespace(**dict(zip([*names, *small, "qb", "rel"], results)))


def solution(mesh):
    count = mesh.shape["win"]

    def shards(
        pixels, merge_gain, merge_shift, merge_weight, norm1_gain, norm1_shift, qkv_weight,
        qkv_bias, rel_table, proj_weight, proj_bias, norm2_gain, norm2_shift, fc1_weight,
        fc1_bias, fc2_weight, fc2_bias, rel_index, keep, cotangent,
    ):
        wins, height, _, channels = pixels.shape
        side = height // 2
        area = side * side
        rows = wins * PAD
        model = merge_weight.shape[1]
        half = model // 2
        heads = 2 * rel_table.shape[1]
        dim = half // rel_table.shape[1]
        hidden = fc1_weight.shape[1]

        def row(v):
            return v.reshape(1, -1)

        wqkv = qkv_weight.transpose(1, 0, 2)
        a = front(
            dim, heads, area, wins,
            dict(
                mg=row(merge_gain), ms=row(merge_shift), n1g=row(norm1_gain),
                n1s=row(norm1_shift), pb=row(proj_bias), n2g=row(norm2_gain),
                n2s=row(norm2_shift), qb=qkv_bias, table=rel_table.T, rel_index=rel_index, keep=keep,
            ),
            dict(
                pixels=pixels.transpose(1, 2, 0, 3).reshape(side, 2, side, 2, wins, channels),
                wm=merge_weight, wqkv=wqkv, wp=proj_weight, cot=cotangent,
            ),
        )
        b = back(
            count, dim, heads, area, wins, rel_table.shape[0],
            dict(
                keep=a.kept_rows, b1=row(fc1_bias), b2=row(fc2_bias), nat=a.nat, mgo=a.mgo,
                lse=a.lse, index=a.index, gb2=a.gb2,
            ),
            dict(
                second=a.second, second_sib=a.second_sib, gf=a.gf, stream1=a.stream1, stream0=a.stream0,
                fc1=fc1_weight, fc2=fc2_weight, wp_own=proj_weight, wp_oth=a.wp_oth,
                wqkv_own=wqkv, wqkv_oth=a.wqkv_oth, wm_own=merge_weight, wm_oth=a.wm_oth,
                att_own=a.att_own, att_sib=a.att_sib, qkv=a.qkv, bias=a.bias,
                first_own=a.first_own, first_sib=a.first_sib, mn_own=a.mn_own, mn_sib=a.mn_sib,
                x=a.x,
            ),
        )
        large = vars(b)
        vec = large.pop("o_vec")
        large.pop("acts")
        f = hand_on(large, vec, hidden, heads, rel_table.shape[0])

        def flat(v):
            return v.reshape(-1)

        pixels_grad = f.pixels_grad.reshape(height, height, wins, channels)
        return (
            f.out, pixels_grad.transpose(2, 0, 1, 3), flat(f.mg), flat(f.ms), f.o_merge.T,
            flat(f.n1g), flat(f.n1s), f.o_qkv.transpose(1, 0, 2), f.qb, f.rel.T,
            f.o_proj.T, flat(f.pb), flat(f.n2g), flat(f.n2s), f.o_fc1, flat(f.b1),
            f.o_fc2.T, flat(f.b2),
        )

    in_specs = (
        P(("win", "tp"), None, None, None), P("tp"), P("tp"), P("tp", None), P("tp"), P("tp"),
        P(None, None, "tp"), P(None, "tp"), P(None, "tp"), P("tp", None), P("tp"), P("tp"),
        P("tp"), P(None, "tp"), P("tp"), P("tp", None), P("tp"), P(), P("win"), P("win", "tp"),
    )
    out_specs = (
        P("win", "tp"), P(("win", "tp"), None, None, None), P("tp"), P("tp"), P("tp", "win"),
        P("tp"), P("tp"), P("win", None, "tp"), P(None, "tp"), P(None, "tp"), P("tp", "win"),
        P("tp"), P("tp"), P("tp"), P("win", "tp"), P("tp"), P("tp", "win"), P("tp"),
    )
    return jax.shard_map(shards, mesh=mesh, in_specs=in_specs, out_specs=out_specs, check_vma=False)
```
